256 devices in a mesh: conf: 8 (over y_hi, x), orient: 32 (over z, y_lo, core).
Axes of the slice: x: 4, y: 4 (y_hi: 2, y_lo: 2; y = y_hi * 2 + y_lo), z: 8, core: 2. Of those that a mesh axis runs over, the one named last changes fastest.
Arguments:
- particles: bfloat16 [2048, 4096], P(('conf', 'orient')), may hold values from -68 to 68
- defocus_class: int32 [2048], P(('conf', 'orient')), may hold values from 0 to 15
- densities: bfloat16 [64, 4096], P('conf'), may hold values from -6 to 6
- contrast: float32 [16, 4096], replicated, may hold values from -1 to 1
- grid_shift: int32 [3072], P('orient'), may hold values from 0 to 4095
- log_prior: float32 [3072], P('orient'), may hold values from -3 to 0
Outputs:
- loglik: float32 [3, 8, 2048], P(None, None, ('conf', 'orient'))
The draws below stay inside these ranges and needn't reach their ends.
All inputs are finite; a program needn't handle non-finite values.
Results may differ from the reference program's by a relative error of at most 0.00094.
Values may be sent and summed in bfloat16 or wider, within the bound.
A program may use at most 128 MiB of HBM per device.

```python
import jax
import jax.numpy as jnp
from jax import lax

SIDE = 64
PIX = 4096
PB = 256
C_DEV = 8
NCLS = 16
VISITS = 3
SHIFTS = 3072
PARTICLES = 2048
CONFS = 64
N_CONF = 8


def draw_particles(key, part):
    key = jax.random.fold_in(key, 11)
    first_key = jax.random.fold_in(key, 0)
    return jnp.clip(jax.random.normal(first_key, (PARTICLES, PIX), jnp.float32), -6.0, 6.0).astype(jnp.bfloat16)


def set_ends(array, own_key, least, top_value):
    shape = array.shape
    place = [jax.random.randint(jax.random.fold_in(own_key, axis), (), 0, shape[axis]) for axis in range(len(shape))]
    array = array.at[tuple(place)].set(least)
    longest = shape.index(max(shape))
    place[longest] = (place[longest] + 1) % shape[longest]
    return array.at[tuple(place)].set(top_value)


def shard_levels(key, shape, pieces, smallest, largest):
    factor_of = 1.0
    for position, blocks in pieces:
        heights = jax.random.uniform(jax.random.fold_in(jax.random.fold_in(key, 6), position), (blocks,), jnp.float32, smallest / len(pieces), largest / len(pieces))
        factor_of = factor_of * jnp.repeat(jnp.exp(heights), shape[position] // blocks).reshape((-1,) + (1,) * (len(shape) - 1 - position))
    return factor_of


def gaussian(key, extent, deviation, most, cuts=(), kind=jnp.bfloat16):
    values = deviation * jax.random.normal(key, extent, jnp.float32)
    if cuts:
        values = values * shard_levels(key, extent, cuts, -0.22, 0.18)
    return jnp.clip(values, -most, most).astype(kind)


def setup_inputs(seed: int = 0) -> dict:
    key_of = jax.random.split(jax.random.key(seed), 7)
    particles = draw_particles(jax.random.fold_in(key_of[6], 71), 0)
    defocus_class = set_ends(jax.random.randint(key_of[1], (PARTICLES,), 0, NCLS), jax.random.fold_in(key_of[1], 1), 0, NCLS - 1).astype(jnp.int32)
    densities = gaussian(key_of[2], (CONFS, PIX), 1.0, 6.0, ((0, 8),))
    contrast = jnp.clip(jax.random.uniform(key_of[3], (NCLS, PIX), jnp.float32, -1.0, 1.0), -1.0, 1.0)
    grid_shift = set_ends(jax.random.randint(key_of[4], (SHIFTS,), 0, PIX), jax.random.fold_in(key_of[4], 1), 0, PIX - 1).astype(jnp.int32)
    log_prior = jnp.clip(-3.0 + 3.0 * jax.random.uniform(key_of[5], (SHIFTS,), jnp.float32) ** shard_levels(key_of[5], (SHIFTS,), ((0, 32),), -0.2, 0.2), -3.0, 0.0)
    return {"particles": particles, "defocus_class": defocus_class, "densities": densities, "contrast": contrast, "grid_shift": grid_shift, "log_prior": log_prior}


INV_SIXTEEN = 1.0 / 16.0
INV_THIRTY_TWO = 1.0 / 32.0


def projections(local_maps, shift_amount, image_side):
    conf_count = local_maps.shape[0]
    images = local_maps.reshape(conf_count, image_side, image_side)

    def rolled_at(offset):
        return jnp.roll(images, (offset // image_side, offset % image_side), axis=(1, 2))

    panels = jax.vmap(rolled_at, out_axes=1)(shift_amount)
    return panels.reshape(conf_count * shift_amount.shape[0], image_side * image_side)


def excess_power(contrast_sq, panels):
    wide = panels.astype(jnp.float32)
    excess = (wide * wide - 1.0).astype(jnp.bfloat16)
    return lax.dot_general(contrast_sq, excess, (((1,), (1,)), ((), ())), preferred_element_type=jnp.float32)


def reference(particles, defocus_class, densities, contrast, grid_shift, log_prior):
    filtered = (particles.astype(jnp.float32) * contrast[defocus_class]).astype(jnp.bfloat16)
    contrast_sq = (contrast * contrast).astype(jnp.bfloat16)

    def score_group(group_idx):
        local_maps = lax.dynamic_slice_in_dim(densities, group_idx * C_DEV, C_DEV, 0)
        panels = projections(local_maps, grid_shift, SIDE)
        power_table = excess_power(contrast_sq, panels)
        results = []
        for visit_idx in range(VISITS):
            block_idx = ((group_idx - visit_idx) % N_CONF).astype(jnp.int32)
            block_rows = lax.dynamic_slice_in_dim(filtered, block_idx * PB, PB, 0)
            block_class = lax.dynamic_slice_in_dim(defocus_class, block_idx * PB, PB, 0)
            correlate = lax.dot_general(block_rows, panels, (((1,), (1,)), ((), ())), preferred_element_type=jnp.float32)
            chosen = jnp.take(power_table, block_class, axis=0)
            score = (correlate * INV_SIXTEEN - chosen * INV_THIRTY_TWO).reshape(PB, C_DEV, SHIFTS) + log_prior[None, None, :]
            highest = jnp.max(score, axis=2)
            total = jnp.sum(jnp.exp(score - highest[:, :, None]), axis=2)
            results.append(jnp.transpose(highest + jnp.log(total)))
        return jnp.stack(results)

    per_group = lax.map(score_group, jnp.arange(N_CONF, dtype=jnp.int32))
    return jnp.transpose(per_group, (1, 2, 0, 3)).reshape(VISITS, C_DEV, N_CONF * PB)
```

```python
import functools
import math

import jax
import jax.numpy as jnp
import numpy as np
from jax import lax
from jax.experimental import pallas as pl
from jax.experimental.pallas import tpu as pltpu
from jax.sharding import PartitionSpec as P

SIDE = 64
ROWS = 8
LANES = 128
TILES = 32
HALF = TILES // 2 + 1
MESH = pl.DeviceIdType.MESH
F32 = jnp.float32
BF16 = jnp.bfloat16
FAR = -1e30


def lane_matrix():
    yl, x = np.divmod(np.arange(LANES), SIDE)
    phase = 2.0 * np.pi * (np.outer(x, x) % SIDE) / SIDE + np.pi * (np.outer(yl, yl) % 2)
    c, s = np.cos(phase), np.sin(phase)
    full = np.block([[c, s], [-s, c]]).astype(np.float32)
    high = full.astype(jnp.bfloat16)
    low = (full - high.astype(np.float32)).astype(jnp.bfloat16)
    return np.concatenate([high, low], axis=0)


def turned(z, num, den):
    re, im = z
    eighth = (8 * num / den) % 8
    if eighth == 0:
        return z
    if eighth == 2:
        return (-im, re)
    angle = 2.0 * math.pi * num / den
    c, s = math.cos(angle), math.sin(angle)
    if eighth == 1:
        return ((re - im) * c, (re + im) * c)
    if eighth == 3:
        return ((re + im) * c, (im - re) * c)
    return (re * c - im * s, re * s + im * c)


def complex_dft(z):
    n = len(z)
    if n == 1:
        return z
    even, odd = complex_dft(z[0::2]), complex_dft(z[1::2])
    out = [None] * n
    for k in range(n // 2):
        (er, ei), (re, im) = even[k], odd[k]
        if 4 * k == n:
            out[k], out[k + n // 2] = (er - im, ei + re), (er + im, ei - re)
        else:
            tr, ti = turned((re, im), k, n)
            out[k], out[k + n // 2] = (er + tr, ei + ti), (er - tr, ei - ti)
    return out


def real_dft(x):
    n = len(x)
    if n == 2:
        return [(x[0] + x[1], None, False), (x[0] - x[1], None, False)]
    h, q = n // 2, n // 4
    a = [x[j] + x[j + h] for j in range(h)]
    b = [x[j] - x[j + h] for j in range(h)]
    out = [None] * (h + 1)
    out[0::2] = real_dft(a)
    z = complex_dft([turned((b[j], b[j + q]), j, n) for j in range(q)])
    for m in range(q):
        k = 4 * m + 1
        if k <= h:
            out[k] = (*z[m], False)
        else:
            out[n - k] = (*z[m], True)
    return out


def inverse_real_dft(spec):
    h = len(spec) - 1
    n = 2 * h
    if n == 2:
        return [spec[0][0] + spec[1][0], spec[0][0] - spec[1][0]]
    q = n // 4
    even = inverse_real_dft(spec[0::2])
    z = complex_dft([spec[k] if k <= h else spec[n - k] for k in range(1, n, 4)])
    out = [None] * n
    for j in range(q):
        tr, ti = turned(z[j], j, n)
        out[j], out[j + h] = even[j] + tr, even[j] - tr
        out[j + q], out[j + q + h] = even[j + q] - ti, even[j + q] + ti
    return out


def needs_conjugate(k):
    while k % 2 == 0:
        k //= 2
    return k % 4 == 3


def lane_turn(k, scale):
    lane = lax.broadcasted_iota(jnp.int32, (ROWS, LANES), 1)
    angle = 2.0 * math.pi * k / SIDE
    c = jnp.where(lane >= SIDE, F32(scale * math.cos(angle)), F32(scale))
    s = jnp.where(lane >= SIDE, F32(scale * math.sin(angle)), F32(0.0))
    return c, s


def forward_rows(tiles, scale, dst, row):
    spec = real_dft(tiles)
    lane = lax.broadcasted_iota(jnp.int32, (ROWS, LANES), 1)
    rows = pl.ds(row, ROWS)
    zero = jnp.zeros((ROWS, LANES), F32)
    for k, (re, im, conj) in enumerate(spec):
        if k == 0:
            nr, ni = re, zero
        elif k == HALF - 1:
            nr, ni = jnp.where(lane < SIDE, re, 0.0), jnp.where(lane < SIDE, 0.0, re)
        else:
            c, s = lane_turn(k, scale)
            if conj:
                nr, ni = re * c + im * s, re * s - im * c
            else:
                nr, ni = re * c - im * s, re * s + im * c
        dst[k, rows, 0:LANES] = nr
        dst[k, rows, LANES : 2 * LANES] = ni


def split_in_two(x):
    high = x.astype(BF16)
    return high, (x - high.astype(F32)).astype(BF16)


def times_lane_matrix(high, low, w_ref):
    w_high, w_low = w_ref[0 : 2 * LANES, :], w_ref[2 * LANES :, :]
    return jnp.dot(
        jnp.concatenate([high, low, high], axis=1),
        jnp.concatenate([w_high, w_high, w_low], axis=0),
        preferred_element_type=F32,
    )


def forward_lanes(src, w_ref, dst):
    x = src[...].reshape(HALF * 2 * ROWS, 2 * LANES)
    high, low = split_in_two(x)
    dst[...] = times_lane_matrix(high, low, w_ref).reshape(HALF, 2 * ROWS, 2 * LANES)


def log_weights(gath, count):
    shift = gath[:, 0, :].astype(jnp.int32)
    weight = gath[:, 1, :]
    tile, lane = shift // LANES, shift % LANES
    tile_row = lax.broadcasted_iota(jnp.int32, (TILES, LANES), 0)
    lane_row = lax.broadcasted_iota(jnp.int32, (LANES, LANES), 0)
    lefts, rights = [], []
    for r in range(count):
        left = jnp.where(tile_row == tile[r : r + 1, :], weight[r : r + 1, :], 0.0)
        lefts.append(jnp.concatenate(split_in_two(left), axis=0))
        rights.append(jnp.where(lane_row == lane[r : r + 1, :], 1.0, 0.0).astype(BF16))
    both = lax.dot_general(
        jnp.concatenate(lefts, axis=1),
        jnp.concatenate(rights, axis=1),
        (((1,), (1,)), ((), ())),
        preferred_element_type=F32,
    )
    total = both[0:TILES] + both[TILES:]
    return jnp.where(total > 0.0, jnp.log(jnp.where(total > 0.0, total, 1.0)), FAR)


def spectra_product(fr, fi, qr, qi, dr, di, er, ei):
    return (
        fr * dr + fi * di + (qr * er + qi * ei),
        fr * di - fi * dr + (qr * ei - qi * er),
    )


def pair_products(sets, de, lhs, count):
    def one_tile(k, _):
        fq = []
        for ref in sets:
            f, q = ref[k, 0:ROWS, :], ref[k, ROWS : 2 * ROWS, :]
            fq.append((f[:, :LANES], f[:, LANES:], q[:, :LANES], q[:, LANES:]))
        parts = []
        for c in range(count):
            d, e = de[k, c : c + 1, :], de[k, ROWS + c : ROWS + c + 1, :]
            other = (d[:, :LANES], d[:, LANES:], e[:, :LANES], e[:, LANES:])
            for own in fq:
                parts.append(jnp.concatenate(spectra_product(*own, *other), axis=1))
        for i in range(0, len(parts), 2):
            high, low = split_in_two(jnp.concatenate(parts[i : i + 2], axis=0))
            rows = pl.ds(i * ROWS, 2 * ROWS)
            lhs[k, rows, 0 : 2 * LANES] = high
            lhs[k, rows, 2 * LANES :] = low
        return 0

    lax.fori_loop(0, HALF, one_tile, 0)


def inverse_lanes(lhs, w_ref, dst, rows):
    x = lhs[:, 0:rows, :].reshape(HALF * rows, 4 * LANES)
    out = times_lane_matrix(x[:, : 2 * LANES], x[:, 2 * LANES :], w_ref)
    dst[:, 0:rows, :] = out.reshape(HALF, rows, 2 * LANES)


def log_sums(g_ref, lw_ref, ms_ref, groups):
    lane = lax.broadcasted_iota(jnp.int32, (ROWS, LANES), 1)

    def one_group(i, _):
        rows = pl.ds(pl.multiple_of(i * ROWS, ROWS), ROWS)
        spec = []
        for k in range(HALF):
            re, im = g_ref[k, rows, 0:LANES], g_ref[k, rows, LANES : 2 * LANES]
            if k == 0:
                spec.append((re, None))
            elif k == HALF - 1:
                spec.append((jnp.where(lane < SIDE, re, -im), None))
            else:
                c, s = lane_turn(k, 1.0)
                nr = re * c - im * s
                ni = -(re * s) - im * c if needs_conjugate(k) else re * s + im * c
                spec.append((nr, ni))
        score = inverse_real_dft(spec)
        score = [score[j] + lw_ref[j : j + 1, :] for j in range(TILES)]
        top = functools.reduce(jnp.maximum, score)
        total = functools.reduce(jnp.add, [jnp.exp(v - top) for v in score])
        ms_ref[i, 0:ROWS, :] = top
        ms_ref[i, ROWS : 2 * ROWS, :] = total
        return 0

    lax.fori_loop(0, groups, one_group, 0)


def gathered_result(ms_ref, first, step, count):
    lane = lax.broadcasted_iota(jnp.int32, (ROWS, LANES), 1)
    out = jnp.zeros((ROWS, LANES), F32)
    for c in range(count):
        top = ms_ref[first + step * c, 0:ROWS, :]
        total = ms_ref[first + step * c, ROWS : 2 * ROWS, :]
        highest = jnp.max(top, axis=1, keepdims=True)
        summed = jnp.sum(total * jnp.exp(top - highest), axis=1, keepdims=True)
        out = jnp.where(lane == c, highest + jnp.log(summed), out)
    return out.T[0:count, :]


def kernel(
    n_conf,
    n_orient,
    cls_ref,
    part_ref,
    dens_ref,
    con_ref,
    shift_ref,
    prior_ref,
    w_ref,
    out_ref,
    fq_own,
    fq_sib,
    d_send,
    d_recv,
    msg,
    gath,
    stage_a,
    stage_b,
    spec_own,
    spec_sib,
    spec_de,
    lhs,
    g_ref,
    lw_ref,
    ms_ref,
    res_send,
    res_recv,
    gath_send_sem,
    gath_recv_sem,
    big_send_sem,
    big_recv_sem,
    res_send_sem,
    res_recv_sem,
):
    b = lax.axis_index("conf")
    o = lax.axis_index("orient")
    core = lax.rem(o, 2)
    sibling = o + 1 - 2 * core
    reach = 1 + core

    def conf_at(offset):
        return lax.rem(b + offset + 2 * n_conf, n_conf)

    def signal(conf, orient):
        pl.semaphore_signal(
            barrier, inc=1, device_id=(conf, orient), device_id_type=MESH
        )

    barrier = pltpu.get_barrier_semaphore()

    def greet(t, _):
        signal(b, lax.rem(o + t, n_orient))
        return 0

    lax.fori_loop(1, n_orient, greet, 0)
    signal(conf_at(reach), o)
    signal(conf_at(-1), o - core)
    signal(conf_at(-2), o - core + 1)

    row = lax.broadcasted_iota(jnp.int32, (ROWS, LANES), 0)
    cls = jnp.zeros((ROWS, LANES), jnp.int32)
    for i in range(ROWS):
        cls = jnp.where(row == i, cls_ref[i], cls)
    own = [cls == k for k in range(con_ref.shape[0])]
    dens = dens_ref[...].astype(F32)
    d_send[...] = jnp.concatenate(
        [dens[:, : TILES // 2 * LANES], dens[:, TILES // 2 * LANES :]], axis=0
    ).astype(BF16)
    for j in range(TILES):
        cols = slice(j * LANES, (j + 1) * LANES)
        envelope = jnp.zeros((ROWS, LANES), F32)
        for k in range(con_ref.shape[0]):
            envelope = jnp.where(own[k], con_ref[k : k + 1, cols], envelope)
        f = part_ref[:, cols].astype(F32) * envelope
        fq_own[:, cols] = jnp.concatenate([f, envelope * envelope], axis=0).astype(BF16)

    count = shift_ref.shape[0]
    msg[...] = jnp.zeros_like(msg)
    msg[0:1, 0:count] = shift_ref[...].astype(F32).reshape(1, count)
    msg[1:2, 0:count] = jnp.exp(prior_ref[...]).reshape(1, count)
    gath[o] = msg[...]

    pl.semaphore_wait(barrier, n_orient + 2)

    def grid_copy(t):
        return pltpu.make_async_remote_copy(
            src_ref=msg,
            dst_ref=gath.at[o],
            send_sem=gath_send_sem,
            recv_sem=gath_recv_sem,
            device_id=(b, lax.rem(o + t, n_orient)),
            device_id_type=MESH,
        )

    d_copy = pltpu.make_async_remote_copy(
        src_ref=d_send,
        dst_ref=d_recv,
        send_sem=big_send_sem.at[0],
        recv_sem=big_recv_sem.at[0],
        device_id=(conf_at(-reach), o),
        device_id_type=MESH,
    )
    fq_copy = pltpu.make_async_remote_copy(
        src_ref=fq_own,
        dst_ref=fq_sib,
        send_sem=big_send_sem.at[1],
        recv_sem=big_recv_sem.at[1],
        device_id=(b, sibling),
        device_id_type=MESH,
    )
    d_copy.start()
    fq_copy.start()

    def send_grid(t, _):
        grid_copy(t).start()
        return 0

    lax.fori_loop(1, n_orient, send_grid, 0)

    def forward_fq(src, dst):
        for half, scale in ((0, 2.0**-16), (1, -(2.0**-17))):
            tiles = []
            for j in range(TILES):
                both = src[:, j * LANES : (j + 1) * LANES].astype(F32)
                tiles.append(both[half * ROWS : (half + 1) * ROWS] * scale)
            forward_rows(tiles, 2.0, stage_a, half * ROWS)
        forward_lanes(stage_a, w_ref, dst)

    def forward_de(src, dst):
        tiles = []
        for j in range(TILES // 2):
            both = src[:, j * LANES : (j + 1) * LANES].astype(F32)
            tiles.append((both[:ROWS], both[ROWS:]))
        tiles = [t[0] for t in tiles] + [t[1] for t in tiles]
        forward_rows(tiles, 1.0, stage_b, 0)
        excess = [(t * t - 1.0).astype(BF16).astype(F32) for t in tiles]
        forward_rows(excess, 1.0, stage_b, ROWS)
        forward_lanes(stage_b, w_ref, dst)

    forward_fq(fq_own, spec_own)
    forward_de(d_send, spec_de)
    pair_products([spec_own], spec_de, lhs, ROWS)
    inverse_lanes(lhs, w_ref, g_ref, ROWS * ROWS)

    others = pl.ds(0, n_orient - 1)
    everyone = pltpu.make_async_remote_copy(
        src_ref=gath.at[others],
        dst_ref=gath.at[others],
        send_sem=gath_send_sem,
        recv_sem=gath_recv_sem,
        device_id=(b, sibling),
        device_id_type=MESH,
    )
    everyone.wait_recv()
    lw_ref[...] = log_weights(gath, n_orient)
    log_sums(g_ref, lw_ref, ms_ref, ROWS)
    out_ref[0] = gathered_result(ms_ref, 0, 1, ROWS)

    fq_copy.wait_recv()
    forward_fq(fq_sib, spec_sib)
    d_copy.wait_recv()
    forward_de(d_recv, spec_de)
    pair_products([spec_own, spec_sib], spec_de, lhs, ROWS)
    inverse_lanes(lhs, w_ref, g_ref, 2 * ROWS * ROWS)
    log_sums(g_ref, lw_ref, ms_ref, 2 * ROWS)

    res_copies = []
    for p, target in enumerate((o, sibling)):
        res_send[p, :, 0:ROWS] = gathered_result(ms_ref, p, 2, ROWS)
        copy = pltpu.make_async_remote_copy(
            src_ref=res_send.at[p],
            dst_ref=res_recv.at[core],
            send_sem=res_send_sem.at[p],
            recv_sem=res_recv_sem.at[core],
            device_id=(conf_at(reach), target),
            device_id_type=MESH,
        )
        copy.start()
        res_copies.append(copy)

    for v in range(2):
        pltpu.make_async_remote_copy(
            src_ref=res_send.at[v],
            dst_ref=res_recv.at[v],
            send_sem=res_send_sem.at[v],
            recv_sem=res_recv_sem.at[v],
            device_id=(b, sibling),
            device_id_type=MESH,
        ).wait_recv()
        out_ref[1 + v] = res_recv[v, :, 0:ROWS]

    everyone.wait_send()
    d_copy.wait_send()
    fq_copy.wait_send()
    for copy in res_copies:
        copy.wait_send()


def solution(mesh):
    n_conf, n_orient = mesh.shape["conf"], mesh.shape["orient"]
    w = lane_matrix()

    def per_device(particles, defocus_class, densities, contrast, grid_shift, log_prior):
        pix = particles.shape[1]
        vmem = pl.BlockSpec(memory_space=pltpu.VMEM)
        return pl.pallas_call(
            functools.partial(kernel, n_conf, n_orient),
            out_shape=jax.ShapeDtypeStruct((3, ROWS, ROWS), F32),
            in_specs=[pl.BlockSpec(memory_space=pltpu.SMEM)] + [vmem] * 6,
            out_specs=vmem,
            scratch_shapes=[
                pltpu.VMEM((2 * ROWS, pix), BF16),
                pltpu.VMEM((2 * ROWS, pix), BF16),
                pltpu.VMEM((2 * ROWS, pix // 2), BF16),
                pltpu.VMEM((2 * ROWS, pix // 2), BF16),
                pltpu.VMEM((2, LANES), F32),
                pltpu.VMEM((n_orient, 2, LANES), F32),
                pltpu.VMEM((HALF, 2 * ROWS, 2 * LANES), F32),
                pltpu.VMEM((HALF, 2 * ROWS, 2 * LANES), F32),
                pltpu.VMEM((HALF, 2 * ROWS, 2 * LANES), F32),
                pltpu.VMEM((HALF, 2 * ROWS, 2 * LANES), F32),
                pltpu.VMEM((HALF, 2 * ROWS, 2 * LANES), F32),
                pltpu.VMEM((HALF, 2 * ROWS * ROWS, 4 * LANES), BF16),
                pltpu.VMEM((HALF, 2 * ROWS * ROWS, 2 * LANES), F32),
                pltpu.VMEM((TILES, LANES), F32),
                pltpu.VMEM((2 * ROWS, 2 * ROWS, LANES), F32),
                pltpu.VMEM((2, ROWS, LANES), F32),
                pltpu.VMEM((2, ROWS, LANES), F32),
                pltpu.SemaphoreType.DMA,
                pltpu.SemaphoreType.DMA,
                pltpu.SemaphoreType.DMA((2,)),
                pltpu.SemaphoreType.DMA((2,)),
                pltpu.SemaphoreType.DMA((2,)),
                pltpu.SemaphoreType.DMA((2,)),
            ],
            compiler_params=pltpu.CompilerParams(
                collective_id=0, has_side_effects=True, vmem_limit_bytes=48 * 2**20
            ),
        )(defocus_class, particles, densities, contrast, grid_shift, log_prior, jnp.asarray(w))

    placed = (
        P(("conf", "orient"), None),
        P(("conf", "orient")),
        P("conf", None),
        P(),
        P("orient"),
        P("orient"),
    )
    return jax.shard_map(
        per_device,
        mesh=mesh,
        in_specs=placed,
        out_specs=P(None, None, ("conf", "orient")),
        check_vma=False,
    )
```

```python
import functools
import math

import jax
import jax.numpy as jnp
import numpy as np
from jax import lax
from jax.experimental import pallas as pl
from jax.experimental.pallas import tpu as pltpu
from jax.sharding import PartitionSpec as P

SIDE = 64
ROWS = 8
LANES = 128
TILES = 32
HALF = TILES // 2 + 1
MESH = pl.DeviceIdType.MESH
F32 = jnp.float32
BF16 = jnp.bfloat16
FAR = -1e30
LAYER = 4


def lane_matrix():
    yl, x = np.divmod(np.arange(LANES), SIDE)
    phase = 2.0 * np.pi * (np.outer(x, x) % SIDE) / SIDE + np.pi * (np.outer(yl, yl) % 2)
    c, s = np.cos(phase), np.sin(phase)
    full = np.block([[c, s], [-s, c]]).astype(np.float32)
    high = full.astype(jnp.bfloat16)
    low = (full - high.astype(np.float32)).astype(jnp.bfloat16)
    return np.concatenate([high, low], axis=0)


def turned(z, num, den):
    re, im = z
    eighth = (8 * num / den) % 8
    if eighth == 0:
        return z
    if eighth == 2:
        return (-im, re)
    angle = 2.0 * math.pi * num / den
    c, s = math.cos(angle), math.sin(angle)
    if eighth == 1:
        return ((re - im) * c, (re + im) * c)
    if eighth == 3:
        return ((re + im) * c, (im - re) * c)
    return (re * c - im * s, re * s + im * c)


def complex_dft(z):
    n = len(z)
    if n == 1:
        return z
    even, odd = complex_dft(z[0::2]), complex_dft(z[1::2])
    out = [None] * n
    for k in range(n // 2):
        (er, ei), (re, im) = even[k], odd[k]
        if 4 * k == n:
            out[k], out[k + n // 2] = (er - im, ei + re), (er + im, ei - re)
        else:
            tr, ti = turned((re, im), k, n)
            out[k], out[k + n // 2] = (er + tr, ei + ti), (er - tr, ei - ti)
    return out


def real_dft(x):
    n = len(x)
    if n == 2:
        return [(x[0] + x[1], None, False), (x[0] - x[1], None, False)]
    h, q = n // 2, n // 4
    a = [x[j] + x[j + h] for j in range(h)]
    b = [x[j] - x[j + h] for j in range(h)]
    out = [None] * (h + 1)
    out[0::2] = real_dft(a)
    z = complex_dft([turned((b[j], b[j + q]), j, n) for j in range(q)])
    for m in range(q):
        k = 4 * m + 1
        if k <= h:
            out[k] = (*z[m], False)
        else:
            out[n - k] = (*z[m], True)
    return out


def inverse_real_dft(spec):
    h = len(spec) - 1
    n = 2 * h
    if n == 2:
        return [spec[0][0] + spec[1][0], spec[0][0] - spec[1][0]]
    q = n // 4
    even = inverse_real_dft(spec[0::2])
    z = complex_dft([spec[k] if k <= h else spec[n - k] for k in range(1, n, 4)])
    out = [None] * n
    for j in range(q):
        tr, ti = turned(z[j], j, n)
        out[j], out[j + h] = even[j] + tr, even[j] - tr
        out[j + q], out[j + q + h] = even[j + q] - ti, even[j + q] + ti
    return out


def needs_conjugate(k):
    while k % 2 == 0:
        k //= 2
    return k % 4 == 3


def lane_turn(k, scale):
    lane = lax.broadcasted_iota(jnp.int32, (ROWS, LANES), 1)
    angle = 2.0 * math.pi * k / SIDE
    c = jnp.where(lane >= SIDE, F32(scale * math.cos(angle)), F32(scale))
    s = jnp.where(lane >= SIDE, F32(scale * math.sin(angle)), F32(0.0))
    return c, s


def forward_rows(tiles, scale, dst, row):
    spec = real_dft(tiles)
    lane = lax.broadcasted_iota(jnp.int32, (ROWS, LANES), 1)
    rows = pl.ds(row, ROWS)
    zero = jnp.zeros((ROWS, LANES), F32)
    for k, (re, im, conj) in enumerate(spec):
        if k == 0:
            nr, ni = re, zero
        elif k == HALF - 1:
            nr, ni = jnp.where(lane < SIDE, re, 0.0), jnp.where(lane < SIDE, 0.0, re)
        else:
            c, s = lane_turn(k, scale)
            if conj:
                nr, ni = re * c + im * s, re * s - im * c
            else:
                nr, ni = re * c - im * s, re * s + im * c
        dst[k, rows, 0:LANES] = nr
        dst[k, rows, LANES : 2 * LANES] = ni


def split_in_two(x):
    high = x.astype(BF16)
    return high, (x - high.astype(F32)).astype(BF16)


def times_lane_matrix(high, low, w_ref):
    w_high, w_low = w_ref[0 : 2 * LANES, :], w_ref[2 * LANES :, :]
    return jnp.dot(
        jnp.concatenate([high, low, high], axis=1),
        jnp.concatenate([w_high, w_high, w_low], axis=0),
        preferred_element_type=F32,
    )


def forward_lanes(src, w_ref, dst):
    x = src[...].reshape(HALF * 2 * ROWS, 2 * LANES)
    high, low = split_in_two(x)
    dst[...] = times_lane_matrix(high, low, w_ref).reshape(HALF, 2 * ROWS, 2 * LANES)


def log_weights(gath, count):
    shift = gath[:, 0, :].astype(jnp.int32)
    weight = gath[:, 1, :]
    tile, lane = shift // LANES, shift % LANES
    tile_row = lax.broadcasted_iota(jnp.int32, (TILES, LANES), 0)
    lane_row = lax.broadcasted_iota(jnp.int32, (LANES, LANES), 0)
    lefts, rights = [], []
    for r in range(count):
        left = jnp.where(tile_row == tile[r : r + 1, :], weight[r : r + 1, :], 0.0)
        lefts.append(jnp.concatenate(split_in_two(left), axis=0))
        rights.append(jnp.where(lane_row == lane[r : r + 1, :], 1.0, 0.0).astype(BF16))
    both = lax.dot_general(
        jnp.concatenate(lefts, axis=1),
        jnp.concatenate(rights, axis=1),
        (((1,), (1,)), ((), ())),
        preferred_element_type=F32,
    )
    total = both[0:TILES] + both[TILES:]
    return jnp.where(total > 0.0, jnp.log(jnp.where(total > 0.0, total, 1.0)), FAR)


def spectra_product(fr, fi, qr, qi, dr, di, er, ei):
    return (
        fr * dr + fi * di + (qr * er + qi * ei),
        fr * di - fi * dr + (qr * ei - qi * er),
    )


def pair_products(fq, de, lhs):
    def one_tile(k, _):
        f, q = fq[k, 0:ROWS, :], fq[k, ROWS : 2 * ROWS, :]
        own = (f[:, :LANES], f[:, LANES:], q[:, :LANES], q[:, LANES:])
        parts = []
        for c in range(ROWS):
            d, e = de[k, c : c + 1, :], de[k, ROWS + c : ROWS + c + 1, :]
            other = (d[:, :LANES], d[:, LANES:], e[:, :LANES], e[:, LANES:])
            parts.append(jnp.concatenate(spectra_product(*own, *other), axis=1))
        for i in range(0, len(parts), 2):
            high, low = split_in_two(jnp.concatenate(parts[i : i + 2], axis=0))
            rows = pl.ds(i * ROWS, 2 * ROWS)
            lhs[k, rows, 0 : 2 * LANES] = high
            lhs[k, rows, 2 * LANES :] = low
        return 0

    lax.fori_loop(0, HALF, one_tile, 0)


def inverse_lanes(lhs, w_ref, dst):
    rows = lhs.shape[1]
    x = lhs[...].reshape(HALF * rows, 4 * LANES)
    out = times_lane_matrix(x[:, : 2 * LANES], x[:, 2 * LANES :], w_ref)
    dst[...] = out.reshape(HALF, rows, 2 * LANES)


def scores(g_ref, score_ref, first):
    lane = lax.broadcasted_iota(jnp.int32, (ROWS, LANES), 1)

    def one_group(i, _):
        rows = pl.ds(pl.multiple_of(i * ROWS, ROWS), ROWS)
        spec = []
        for k in range(HALF):
            re, im = g_ref[k, rows, 0:LANES], g_ref[k, rows, LANES : 2 * LANES]
            if k == 0:
                spec.append((re, None))
            elif k == HALF - 1:
                spec.append((jnp.where(lane < SIDE, re, -im), None))
            else:
                c, s = lane_turn(k, 1.0)
                nr = re * c - im * s
                ni = -(re * s) - im * c if needs_conjugate(k) else re * s + im * c
                spec.append((nr, ni))
        for j, value in enumerate(inverse_real_dft(spec)):
            score_ref[first + i, j] = value
        return 0

    lax.fori_loop(0, ROWS, one_group, 0)


def log_sums(score_ref, lw_ref, ms_ref, per_step):
    def some_groups(step, _):
        for p in range(per_step):
            i = step * per_step + p
            value = [score_ref[i, j] + lw_ref[j : j + 1, :] for j in range(TILES)]
            top = functools.reduce(jnp.maximum, value)
            total = functools.reduce(jnp.add, [jnp.exp(v - top) for v in value])
            ms_ref[i, 0:ROWS, :] = top
            ms_ref[i, ROWS : 2 * ROWS, :] = total
        return 0

    lax.fori_loop(0, score_ref.shape[0] // per_step, some_groups, 0)


def results(ms_ref):
    lane = lax.broadcasted_iota(jnp.int32, (ROWS, LANES), 1)
    out = jnp.zeros((ROWS, LANES), F32)
    for i in range(ms_ref.shape[0]):
        top, total = ms_ref[i, 0:ROWS, :], ms_ref[i, ROWS : 2 * ROWS, :]
        highest = jnp.max(top, axis=1, keepdims=True)
        summed = jnp.sum(total * jnp.exp(top - highest), axis=1, keepdims=True)
        out = jnp.where(lane == i, highest + jnp.log(summed), out)
    return out.T


def kernel(
    n_conf,
    n_orient,
    cls_hbm,
    part_hbm,
    dens_hbm,
    con_hbm,
    shift_hbm,
    prior_hbm,
    w_hbm,
    out_ref,
    cls_ref,
    part_ref,
    dens_ref,
    con_ref,
    shift_ref,
    prior_ref,
    w_ref,
    blocks,
    msg,
    gath,
    stage,
    spec_fq,
    spec_de,
    lhs,
    g_ref,
    score_ref,
    lw_ref,
    ms_ref,
    in_sem,
    block_send_sem,
    block_recv_sem,
    grid_send_sem,
    grid_recv_sem,
    lw_send_sem,
    lw_recv_sem,
):
    loads = []
    for i, (src, dst) in enumerate(
        (
            (shift_hbm, shift_ref),
            (prior_hbm, prior_ref),
            (cls_hbm, cls_ref),
            (part_hbm, part_ref),
            (con_hbm, con_ref),
            (dens_hbm, dens_ref),
            (w_hbm, w_ref),
        )
    ):
        loads.append(pltpu.make_async_copy(src, dst, in_sem.at[i]))
        loads[-1].start()

    b = lax.axis_index("conf")
    o = lax.axis_index("orient")
    n_layers = n_orient // LAYER
    n_hubs = n_layers // 2
    z = o // LAYER
    place = lax.rem(o, LAYER)
    is_hub = z < n_hubs

    def conf_at(offset):
        return lax.rem(b + offset + n_conf, n_conf)

    barrier = pltpu.get_barrier_semaphore()

    def greet(conf, orient):
        pl.semaphore_signal(
            barrier, inc=1, device_id=(conf, orient), device_id_type=MESH
        )

    greet(conf_at(-1), o)
    greet(conf_at(-2), o)

    @pl.when(is_hub)
    def _():
        def beside(t, _):
            greet(b, z * LAYER + lax.rem(place + t, LAYER))
            return 0

        def above(t, _):
            greet(b, t)
            return 0

        lax.fori_loop(1, LAYER, beside, 0)
        lax.fori_loop((z + 1) * LAYER, n_orient, above, 0)

    count = shift_ref.shape[0]
    loads[0].wait()
    loads[1].wait()
    msg[...] = jnp.zeros_like(msg)
    msg[0:1, 0:count] = shift_ref[...].astype(F32).reshape(1, count)
    msg[1:2, 0:count] = jnp.exp(prior_ref[...]).reshape(1, count)
    gath[o] = msg[...]

    for load in loads[2:5]:
        load.wait()
    row = lax.broadcasted_iota(jnp.int32, (ROWS, LANES), 0)
    cls = jnp.zeros((ROWS, LANES), jnp.int32)
    for i in range(ROWS):
        cls = jnp.where(row == i, cls_ref[i], cls)

    def envelope_of(classes):
        picked = [classes == k for k in range(con_ref.shape[0])]

        def tile(j):
            out = jnp.zeros((ROWS, LANES), F32)
            for k, mask in enumerate(picked):
                out = jnp.where(mask, con_ref[k : k + 1, j * LANES : (j + 1) * LANES], out)
            return out

        return tile

    envelope = envelope_of(cls)
    half = TILES // 2
    for j in range(half):
        pair = [
            part_ref[:, t * LANES : (t + 1) * LANES].astype(F32) * envelope(t)
            for t in (j, j + half)
        ]
        blocks[0, :, j * LANES : (j + 1) * LANES] = jnp.concatenate(pair, axis=0).astype(BF16)
    blocks[0, :, half * LANES :] = jnp.concatenate([cls, cls], axis=0).astype(F32).astype(BF16)

    pl.semaphore_wait(barrier, 2 + LAYER * jnp.minimum(z, n_hubs) + jnp.where(is_hub, LAYER - 1, 0))

    def send_grid(to):
        pltpu.make_async_remote_copy(
            src_ref=msg,
            dst_ref=gath.at[o],
            send_sem=grid_send_sem,
            recv_sem=grid_recv_sem.at[z],
            device_id=(b, to),
            device_id_type=MESH,
        ).start()

    def send_below(t, _):
        send_grid(t)
        return 0

    def send_beside(t, _):
        send_grid(z * LAYER + lax.rem(place + t, LAYER))
        return 0

    lax.fori_loop(0, LAYER * jnp.minimum(z, n_hubs), send_below, 0)
    lax.fori_loop(1, jnp.where(is_hub, LAYER, 1), send_beside, 0)

    block_copies = []
    for v in (1, 2):
        block_copies.append(
            pltpu.make_async_remote_copy(
                src_ref=blocks.at[0],
                dst_ref=blocks.at[v],
                send_sem=block_send_sem.at[v],
                recv_sem=block_recv_sem.at[v],
                device_id=(conf_at(v), o),
                device_id_type=MESH,
            )
        )
        block_copies[-1].start()

    def grid_wait(layer, number):
        slots = gath.at[pl.ds(layer * LAYER, number)]
        return pltpu.make_async_remote_copy(
            src_ref=slots,
            dst_ref=slots,
            send_sem=grid_send_sem,
            recv_sem=grid_recv_sem.at[layer],
            device_id=(conf_at(1), o),
            device_id_type=MESH,
        )

    def answer(layer):
        @pl.when(z < layer)
        def _():
            grid_wait(layer, LAYER).wait_recv()
            for t in range(LAYER):
                send_grid(layer * LAYER + t)

    def forward(real_tiles, scale, other_tiles, dst):
        forward_rows(real_tiles, scale[0], stage, 0)
        forward_rows(other_tiles, scale[1], stage, ROWS)
        forward_lanes(stage, w_ref, dst)

    loads[5].wait()
    loads[6].wait()
    dens = [dens_ref[:, j * LANES : (j + 1) * LANES].astype(F32) for j in range(TILES)]
    excess = [(t * t - 1.0).astype(BF16).astype(F32) for t in dens]
    forward(dens, (1.0, 1.0), excess, spec_de)

    def visit(v, _):
        @pl.when(v > 0)
        def _():
            pltpu.make_async_remote_copy(
                src_ref=blocks.at[0],
                dst_ref=blocks.at[v],
                send_sem=block_send_sem.at[v],
                recv_sem=block_recv_sem.at[v],
                device_id=(conf_at(1), o),
                device_id_type=MESH,
            ).wait_recv()

        classes = blocks[v, :, half * LANES :].astype(F32)[0:ROWS].astype(jnp.int32)
        tile_of = envelope_of(classes)
        pairs = [blocks[v, :, j * LANES : (j + 1) * LANES].astype(F32) for j in range(half)]
        rows = [p[0:ROWS] for p in pairs] + [p[ROWS:] for p in pairs]
        square = []
        for j in range(TILES):
            e = tile_of(j)
            square.append((e * e).astype(BF16).astype(F32) * -(2.0**-17))
        rows = [r * 2.0**-16 for r in rows]
        forward(rows, (2.0, 2.0), square, spec_fq)
        pair_products(spec_fq, spec_de, lhs)
        inverse_lanes(lhs, w_ref, g_ref)
        scores(g_ref, score_ref, v * ROWS)
        return 0

    lax.fori_loop(0, 2, visit, 0)
    for layer in range(1, n_hubs):
        answer(layer)
    lax.fori_loop(2, 3, visit, 0)

    @pl.when(is_hub)
    def _():
        for layer in range(n_layers):

            @pl.when(z == layer)
            def _():
                grid_wait(layer, LAYER - 1).wait_recv()

            @pl.when((z > layer) | ((z != layer) & (layer >= n_hubs)))
            def _():
                grid_wait(layer, LAYER).wait_recv()

        lw_ref[...] = log_weights(gath, n_orient)

    def lw_copy(layer):
        return pltpu.make_async_remote_copy(
            src_ref=lw_ref,
            dst_ref=lw_ref,
            send_sem=lw_send_sem.at[layer],
            recv_sem=lw_recv_sem,
            device_id=(b, layer * LAYER + place),
            device_id_type=MESH,
        )

    def hub_of(layer):
        return n_hubs - 1 if layer < n_hubs + (n_layers - n_hubs) // 2 else 0

    for layer in range(n_hubs, n_layers):

        @pl.when(z == hub_of(layer))
        def _():
            lw_copy(layer).start()

    @pl.when(jnp.logical_not(is_hub))
    def _():
        pltpu.make_async_remote_copy(
            src_ref=lw_ref,
            dst_ref=lw_ref,
            send_sem=lw_send_sem.at[0],
            recv_sem=lw_recv_sem,
            device_id=(b, place),
            device_id_type=MESH,
        ).wait_recv()

    log_sums(score_ref, lw_ref, ms_ref, 2)
    final = results(ms_ref)
    for v in range(3):
        out_ref[v] = final[v * ROWS : (v + 1) * ROWS, :]

    for layer in range(n_hubs, n_layers):

        @pl.when(z == hub_of(layer))
        def _():
            lw_copy(layer).wait_send()

    @pl.when(is_hub)
    def _():
        grid_wait(0, LAYER * n_hubs - 1).wait_send()

    @pl.when(jnp.logical_not(is_hub))
    def _():
        grid_wait(0, LAYER * n_hubs).wait_send()

    for copy in block_copies:
        copy.wait_send()


def solution(mesh):
    n_conf, n_orient = mesh.shape["conf"], mesh.shape["orient"]
    w = lane_matrix()

    def per_device(*given):
        particles, defocus_class, densities, contrast, grid_shift, log_prior = given
        operands = [
            pltpu.with_memory_space_constraint(x, pltpu.HBM)
            for x in (
                defocus_class,
                particles,
                densities,
                contrast,
                grid_shift,
                log_prior,
                jnp.asarray(w),
            )
        ]
        spectrum = pltpu.VMEM((HALF, 2 * ROWS, 2 * LANES), F32)
        return pl.pallas_call(
            functools.partial(kernel, n_conf, n_orient),
            out_shape=pltpu.VMEM((3, ROWS, ROWS), F32),
            in_specs=[pl.BlockSpec(memory_space=pltpu.HBM)] * 7,
            out_specs=pl.BlockSpec(memory_space=pltpu.VMEM),
            scratch_shapes=[
                pltpu.SMEM(defocus_class.shape, jnp.int32),
                pltpu.VMEM(particles.shape, BF16),
                pltpu.VMEM(densities.shape, BF16),
                pltpu.VMEM(contrast.shape, F32),
                pltpu.VMEM(grid_shift.shape, jnp.int32),
                pltpu.VMEM(log_prior.shape, F32),
                pltpu.VMEM(w.shape, BF16),
                pltpu.VMEM((3, 2 * ROWS, (TILES // 2 + 1) * LANES), BF16),
                pltpu.VMEM((2, LANES), F32),
                pltpu.VMEM((n_orient, 2, LANES), F32),
                spectrum,
                spectrum,
                spectrum,
                pltpu.VMEM((HALF, ROWS * ROWS, 4 * LANES), BF16),
                pltpu.VMEM((HALF, ROWS * ROWS, 2 * LANES), F32),
                pltpu.VMEM((3 * ROWS, TILES, ROWS, LANES), F32),
                pltpu.VMEM((TILES, LANES), F32),
                pltpu.VMEM((3 * ROWS, 2 * ROWS, LANES), F32),
                pltpu.SemaphoreType.DMA((7,)),
                pltpu.SemaphoreType.DMA((3,)),
                pltpu.SemaphoreType.DMA((3,)),
                pltpu.SemaphoreType.DMA,
                pltpu.SemaphoreType.DMA((n_orient // LAYER,)),
                pltpu.SemaphoreType.DMA((n_orient // LAYER,)),
                pltpu.SemaphoreType.DMA,
            ],
            compiler_params=pltpu.CompilerParams(
                collective_id=0, has_side_effects=True, vmem_limit_bytes=56 * 2**20
            ),
        )(*operands)

    placed = (
        P(("conf", "orient"), None),
        P(("conf", "orient")),
        P("conf", None),
        P(),
        P("orient"),
        P("orient"),
    )
    return jax.shard_map(
        per_device,
        mesh=mesh,
        in_specs=placed,
        out_specs=P(None, None, ("conf", "orient")),
        check_vma=False,
    )
```

```python
import functools
import math

import jax
import jax.numpy as jnp
import numpy as np
from jax import lax
from jax.experimental import pallas as pl
from jax.experimental.pallas import tpu as pltpu
from jax.sharding import PartitionSpec as P

SIDE = 64
ROWS = 8
LANES = 128
TILES = 32
HALF = TILES // 2 + 1
MESH = pl.DeviceIdType.MESH
F32 = jnp.float32
BF16 = jnp.bfloat16
FAR = -1e30
LAYER = 4


def lane_matrix():
    yl, x = np.divmod(np.arange(LANES), SIDE)
    phase = 2.0 * np.pi * (np.outer(x, x) % SIDE) / SIDE + np.pi * (np.outer(yl, yl) % 2)
    c, s = np.cos(phase), np.sin(phase)
    full = np.block([[c, s], [-s, c]]).astype(np.float32)
    high = full.astype(jnp.bfloat16)
    low = (full - high.astype(np.float32)).astype(jnp.bfloat16)
    return np.concatenate([high, low], axis=0)


def turned(z, num, den):
    re, im = z
    eighth = (8 * num / den) % 8
    if eighth == 0:
        return z
    if eighth == 2:
        return (-im, re)
    angle = 2.0 * math.pi * num / den
    c, s = math.cos(angle), math.sin(angle)
    if eighth == 1:
        return ((re - im) * c, (re + im) * c)
    if eighth == 3:
        return ((re + im) * c, (im - re) * c)
    return (re * c - im * s, re * s + im * c)


def complex_dft(z):
    n = len(z)
    if n == 1:
        return z
    even, odd = complex_dft(z[0::2]), complex_dft(z[1::2])
    out = [None] * n
    for k in range(n // 2):
        (er, ei), (re, im) = even[k], odd[k]
        if 4 * k == n:
            out[k], out[k + n // 2] = (er - im, ei + re), (er + im, ei - re)
        else:
            tr, ti = turned((re, im), k, n)
            out[k], out[k + n // 2] = (er + tr, ei + ti), (er - tr, ei - ti)
    return out


def real_dft(x):
    n = len(x)
    if n == 2:
        return [(x[0] + x[1], None, False), (x[0] - x[1], None, False)]
    h, q = n // 2, n // 4
    a = [x[j] + x[j + h] for j in range(h)]
    b = [x[j] - x[j + h] for j in range(h)]
    out = [None] * (h + 1)
    out[0::2] = real_dft(a)
    z = complex_dft([turned((b[j], b[j + q]), j, n) for j in range(q)])
    for m in range(q):
        k = 4 * m + 1
        if k <= h:
            out[k] = (*z[m], False)
        else:
            out[n - k] = (*z[m], True)
    return out


def inverse_real_dft(spec):
    h = len(spec) - 1
    n = 2 * h
    if n == 2:
        return [spec[0][0] + spec[1][0], spec[0][0] - spec[1][0]]
    q = n // 4
    even = inverse_real_dft(spec[0::2])
    z = complex_dft([spec[k] if k <= h else spec[n - k] for k in range(1, n, 4)])
    out = [None] * n
    for j in range(q):
        tr, ti = turned(z[j], j, n)
        out[j], out[j + h] = even[j] + tr, even[j] - tr
        out[j + q], out[j + q + h] = even[j + q] - ti, even[j + q] + ti
    return out


def needs_conjugate(k):
    while k % 2 == 0:
        k //= 2
    return k % 4 == 3


def lane_turn(k, scale):
    lane = lax.broadcasted_iota(jnp.int32, (ROWS, LANES), 1)
    angle = 2.0 * math.pi * k / SIDE
    c = jnp.where(lane >= SIDE, F32(scale * math.cos(angle)), F32(scale))
    s = jnp.where(lane >= SIDE, F32(scale * math.sin(angle)), F32(0.0))
    return c, s


def forward_rows(tiles, scale, dst, row):
    spec = real_dft(tiles)
    lane = lax.broadcasted_iota(jnp.int32, (ROWS, LANES), 1)
    rows = pl.ds(row, ROWS)
    zero = jnp.zeros((ROWS, LANES), F32)
    for k, (re, im, conj) in enumerate(spec):
        if k == 0:
            nr, ni = re, zero
        elif k == HALF - 1:
            nr, ni = jnp.where(lane < SIDE, re, 0.0), jnp.where(lane < SIDE, 0.0, re)
        else:
            c, s = lane_turn(k, scale)
            if conj:
                nr, ni = re * c + im * s, re * s - im * c
            else:
                nr, ni = re * c - im * s, re * s + im * c
        dst[k, rows, 0:LANES] = nr
        dst[k, rows, LANES : 2 * LANES] = ni


def split_in_two(x):
    high = x.astype(BF16)
    return high, (x - high.astype(F32)).astype(BF16)


def times_lane_matrix(high, low, w_ref):
    w_high, w_low = w_ref[0 : 2 * LANES, :], w_ref[2 * LANES :, :]
    return jnp.dot(
        jnp.concatenate([high, low, high], axis=1),
        jnp.concatenate([w_high, w_high, w_low], axis=0),
        preferred_element_type=F32,
    )


def forward_lanes(src, w_ref, dst):
    x = src[...].reshape(HALF * 2 * ROWS, 2 * LANES)
    high, low = split_in_two(x)
    dst[...] = times_lane_matrix(high, low, w_ref).reshape(HALF, 2 * ROWS, 2 * LANES)


def grid_weights(gath, first, count):
    shift = gath[first : first + count, 0, :].astype(jnp.int32)
    weight = gath[first : first + count, 1, :]
    high = weight.astype(BF16).astype(F32)
    low = weight - high
    dy, dx = shift // SIDE, shift % SIDE
    place = dy % 2 * TILES + dy // 2
    row = lax.broadcasted_iota(jnp.int32, (SIDE, LANES), 0)
    lefts, rights = [], []
    for r in range(count):
        mine = row == place[r : r + 1, :]
        parts = [jnp.where(mine, x[r : r + 1, :], 0.0) for x in (high, low)]
        lefts.append(jnp.concatenate(parts, axis=0).astype(BF16))
        right = jnp.where(row == dx[r : r + 1, :], 1.0, 0.0).astype(BF16)
        rights.append(jnp.concatenate([right, right], axis=0))
    both = lax.dot_general(
        jnp.concatenate(lefts, axis=1),
        jnp.concatenate(rights, axis=1),
        (((1,), (1,)), ((), ())),
        preferred_element_type=F32,
    )
    total = both[0:SIDE] + both[SIDE:]
    lane = lax.broadcasted_iota(jnp.int32, (TILES, LANES), 1)
    return jnp.where(lane < SIDE, total[0:TILES], total[TILES:])


def log_or_far(total):
    return jnp.where(total > 0.0, jnp.log(jnp.where(total > 0.0, total, 1.0)), FAR)


def spectra_product(fr, fi, qr, qi, dr, di, er, ei):
    return (
        fr * dr + fi * di + (qr * er + qi * ei),
        fr * di - fi * dr + (qr * ei - qi * er),
    )


def pair_products(fq, de, first, count, lhs):
    for k in range(HALF):
        f, q = fq[k, 0:ROWS, :], fq[k, ROWS : 2 * ROWS, :]
        own = (f[:, :LANES], f[:, LANES:], q[:, :LANES], q[:, LANES:])
        parts = []
        for c in range(first, first + count):
            d, e = de[k, c : c + 1, :], de[k, ROWS + c : ROWS + c + 1, :]
            other = (d[:, :LANES], d[:, LANES:], e[:, :LANES], e[:, LANES:])
            parts.append(jnp.concatenate(spectra_product(*own, *other), axis=1))
        for i in range(0, count, 2):
            high, low = split_in_two(jnp.concatenate(parts[i : i + 2], axis=0))
            rows = pl.ds(i * ROWS, 2 * ROWS)
            lhs[k, rows, 0 : 2 * LANES] = high
            lhs[k, rows, 2 * LANES :] = low


def inverse_lanes(lhs, w_ref, dst):
    rows = lhs.shape[1]
    x = lhs[...].reshape(HALF * rows, 4 * LANES)
    out = times_lane_matrix(x[:, : 2 * LANES], x[:, 2 * LANES :], w_ref)
    dst[...] = out.reshape(HALF, rows, 2 * LANES)


def scores(g_ref, score_ref, first, count):
    lane = lax.broadcasted_iota(jnp.int32, (ROWS, LANES), 1)
    for i in range(count):
        rows = pl.ds(i * ROWS, ROWS)
        spec = []
        for k in range(HALF):
            re, im = g_ref[k, rows, 0:LANES], g_ref[k, rows, LANES : 2 * LANES]
            if k == 0:
                spec.append((re, None))
            elif k == HALF - 1:
                spec.append((jnp.where(lane < SIDE, re, -im), None))
            else:
                c, s = lane_turn(k, 1.0)
                nr = re * c - im * s
                ni = -(re * s) - im * c if needs_conjugate(k) else re * s + im * c
                spec.append((nr, ni))
        for j, value in enumerate(inverse_real_dft(spec)):
            score_ref[first + i, j] = value


def log_sums(score_ref, lw_ref, ms_ref, per_step):
    def some_groups(step, _):
        for p in range(per_step):
            i = step * per_step + p
            value = [score_ref[i, j] + lw_ref[j : j + 1, :] for j in range(TILES)]
            top = functools.reduce(jnp.maximum, value)
            total = functools.reduce(jnp.add, [jnp.exp(v - top) for v in value])
            ms_ref[i, 0:ROWS, :] = top
            ms_ref[i, ROWS : 2 * ROWS, :] = total
        return 0

    lax.fori_loop(0, score_ref.shape[0] // per_step, some_groups, 0)


def results(ms_ref):
    lane = lax.broadcasted_iota(jnp.int32, (ROWS, LANES), 1)
    out = jnp.zeros((ROWS, LANES), F32)
    for i in range(ms_ref.shape[0]):
        top, total = ms_ref[i, 0:ROWS, :], ms_ref[i, ROWS : 2 * ROWS, :]
        highest = jnp.max(top, axis=1, keepdims=True)
        summed = jnp.sum(total * jnp.exp(top - highest), axis=1, keepdims=True)
        out = jnp.where(lane == i, highest + jnp.log(summed), out)
    return out.T


def kernel(
    n_conf,
    n_orient,
    cls_hbm,
    part_hbm,
    dens_hbm,
    con_hbm,
    shift_hbm,
    prior_hbm,
    w_hbm,
    out_ref,
    cls_ref,
    part_ref,
    dens_ref,
    con_ref,
    shift_ref,
    prior_ref,
    w_ref,
    blocks,
    msg,
    gath,
    stage,
    spec_fq,
    spec_de,
    lhs_a,
    lhs_b,
    g_a,
    g_b,
    score_ref,
    early_ref,
    lw_ref,
    ms_ref,
    in_sem,
    block_send_sem,
    block_recv_sem,
    grid_send_sem,
    grid_recv_sem,
    lw_send_sem,
    lw_recv_sem,
    pair_sem,
):
    loads = []
    for i, (src, dst) in enumerate(
        (
            (shift_hbm, shift_ref),
            (prior_hbm, prior_ref),
            (cls_hbm, cls_ref),
            (part_hbm, part_ref),
            (con_hbm, con_ref),
            (dens_hbm, dens_ref),
            (w_hbm, w_ref),
        )
    ):
        loads.append(pltpu.make_async_copy(src, dst, in_sem.at[i]))
        loads[-1].start()

    b = lax.axis_index("conf")
    o = lax.axis_index("orient")
    n_layers = n_orient // LAYER
    n_hubs = max(n_layers // 4, 1)
    z = o // LAYER
    place = lax.rem(o, LAYER)
    core = lax.rem(o, 2)
    first_core = core == 0
    is_hub = z < n_hubs

    def conf_at(offset):
        return lax.rem(b + offset + n_conf, n_conf)

    barrier = pltpu.get_barrier_semaphore()

    def greet(conf, orient):
        pl.semaphore_signal(
            barrier, inc=1, device_id=(conf, orient), device_id_type=MESH
        )

    def tell_sibling():
        pl.semaphore_signal(
            pair_sem, inc=1, device_id=(b, o + 1 - 2 * core), device_id_type=MESH
        )

    @pl.when(core == 1)
    def _():
        greet(b, o - 1)

    @pl.when(is_hub)
    def _():
        for t in range(2, LAYER, 2):
            greet(b, z * LAYER + lax.rem(place - core + t, LAYER))

        def above(t, _):
            greet(b, 2 * t)
            return 0

        lax.fori_loop((z + 1) * (LAYER // 2), n_orient // 2, above, 0)

    greet(conf_at(-1), o - core + 1)
    greet(conf_at(-2), o - core + 1)

    count = shift_ref.shape[0]
    loads[0].wait()
    loads[1].wait()
    msg[...] = jnp.zeros_like(msg)
    msg[0:1, 0:count] = shift_ref[...].astype(F32).reshape(1, count)
    msg[1:2, 0:count] = jnp.exp(prior_ref[...]).reshape(1, count)
    gath[o] = msg[...]

    hubs_below = LAYER * jnp.minimum(z, n_hubs)

    @pl.when(first_core)
    def _():
        pl.semaphore_wait(barrier, 1 + hubs_below + jnp.where(is_hub, LAYER - 2, 0))
        tell_sibling()

    @pl.when(core == 1)
    def _():
        pl.semaphore_wait(pair_sem, 1)

    def send_grid(to):
        pltpu.make_async_remote_copy(
            src_ref=msg,
            dst_ref=gath.at[o],
            send_sem=grid_send_sem,
            recv_sem=grid_recv_sem.at[z],
            device_id=(b, to),
            device_id_type=MESH,
        ).start()

    def send_below(t, _):
        send_grid(t)
        return 0

    def send_beside(t, _):
        send_grid(z * LAYER + lax.rem(place + t, LAYER))
        return 0

    lax.fori_loop(0, hubs_below, send_below, 0)
    lax.fori_loop(1, jnp.where(is_hub, LAYER, 1), send_beside, 0)

    for load in loads[2:5]:
        load.wait()
    row = lax.broadcasted_iota(jnp.int32, (ROWS, LANES), 0)
    cls = jnp.zeros((ROWS, LANES), jnp.int32)
    for i in range(ROWS):
        cls = jnp.where(row == i, cls_ref[i], cls)

    def envelope_of(classes):
        picked = [classes == k for k in range(con_ref.shape[0])]

        def tile(j):
            out = jnp.zeros((ROWS, LANES), F32)
            for k, mask in enumerate(picked):
                out = jnp.where(mask, con_ref[k : k + 1, j * LANES : (j + 1) * LANES], out)
            return out

        return tile

    envelope = envelope_of(cls)
    half = TILES // 2
    for j in range(half):
        pair = [
            part_ref[:, t * LANES : (t + 1) * LANES].astype(F32) * envelope(t)
            for t in (j, j + half)
        ]
        blocks[0, :, j * LANES : (j + 1) * LANES] = jnp.concatenate(pair, axis=0).astype(BF16)
    blocks[0, :, half * LANES :] = jnp.concatenate([cls, cls], axis=0).astype(F32).astype(BF16)

    @pl.when(core == 1)
    def _():
        pl.semaphore_wait(barrier, 4)
        tell_sibling()

    @pl.when(first_core)
    def _():
        pl.semaphore_wait(pair_sem, 1)

    block_copies = []
    for v in (1, 2):
        block_copies.append(
            pltpu.make_async_remote_copy(
                src_ref=blocks.at[0],
                dst_ref=blocks.at[v],
                send_sem=block_send_sem.at[v],
                recv_sem=block_recv_sem.at[v],
                device_id=(conf_at(v), o),
                device_id_type=MESH,
            )
        )
        block_copies[-1].start()

    def grid_wait(layer, number):
        slots = gath.at[pl.ds(layer * LAYER, number)]
        return pltpu.make_async_remote_copy(
            src_ref=slots,
            dst_ref=slots,
            send_sem=grid_send_sem,
            recv_sem=grid_recv_sem.at[layer],
            device_id=(conf_at(1), o),
            device_id_type=MESH,
        )

    def answer(layer):
        @pl.when(z < layer)
        def _():
            grid_wait(layer, LAYER).wait_recv()
            for t in range(LAYER):
                send_grid(layer * LAYER + t)

    def forward(real_tiles, scale, other_tiles, dst):
        forward_rows(real_tiles, scale[0], stage, 0)
        forward_rows(other_tiles, scale[1], stage, ROWS)
        forward_lanes(stage, w_ref, dst)

    loads[5].wait()
    loads[6].wait()
    dens = [dens_ref[:, j * LANES : (j + 1) * LANES].astype(F32) for j in range(TILES)]
    excess = [(t * t - 1.0).astype(BF16).astype(F32) for t in dens]
    forward(dens, (1.0, 1.0), excess, spec_de)

    def visit(v, _):
        @pl.when(v > 0)
        def _():
            pltpu.make_async_remote_copy(
                src_ref=blocks.at[0],
                dst_ref=blocks.at[v],
                send_sem=block_send_sem.at[v],
                recv_sem=block_recv_sem.at[v],
                device_id=(conf_at(1), o),
                device_id_type=MESH,
            ).wait_recv()

        classes = blocks[v, :, half * LANES :].astype(F32)[0:ROWS].astype(jnp.int32)
        tile_of = envelope_of(classes)
        pairs = [blocks[v, :, j * LANES : (j + 1) * LANES].astype(F32) for j in range(half)]
        rows = [p[0:ROWS] for p in pairs] + [p[ROWS:] for p in pairs]
        square = []
        for j in range(TILES):
            e = tile_of(j)
            square.append((e * e).astype(BF16).astype(F32) * -(2.0**-17))
        rows = [r * 2.0**-16 for r in rows]
        forward(rows, (2.0, 2.0), square, spec_fq)
        part = ROWS // 2
        pair_products(spec_fq, spec_de, 0, part, lhs_a)
        inverse_lanes(lhs_a, w_ref, g_a)
        pair_products(spec_fq, spec_de, part, part, lhs_b)
        inverse_lanes(lhs_b, w_ref, g_b)
        scores(g_a, score_ref, v * ROWS, part)
        scores(g_b, score_ref, v * ROWS + part, part)
        return 0

    lax.fori_loop(0, 1, visit, 0)
    for layer in range(1, n_hubs):
        answer(layer)
    lax.fori_loop(1, 3, visit, 0)

    @pl.when(is_hub)
    def _():
        def hear(layers):
            for layer in layers:

                @pl.when(z == layer)
                def _():
                    grid_wait(layer, LAYER - 1).wait_recv()

                @pl.when((z > layer) | ((z != layer) & (layer >= n_hubs)))
                def _():
                    grid_wait(layer, LAYER).wait_recv()

        middle = n_layers // 2
        hear(range(middle))
        early_ref[...] = grid_weights(gath, 0, middle * LAYER)
        hear(range(middle, n_layers))
        late = grid_weights(gath, middle * LAYER, n_orient - middle * LAYER)
        lw_ref[...] = log_or_far(early_ref[...] + late)

    def lw_copy(layer):
        return pltpu.make_async_remote_copy(
            src_ref=lw_ref,
            dst_ref=lw_ref,
            send_sem=lw_send_sem.at[layer],
            recv_sem=lw_recv_sem,
            device_id=(b, layer * LAYER + place),
            device_id_type=MESH,
        )

    def hub_of(layer):
        return n_hubs - 1 if layer <= n_layers // 2 else 0

    for layer in range(n_hubs, n_layers):

        @pl.when(z == hub_of(layer))
        def _():
            lw_copy(layer).start()

    @pl.when(jnp.logical_not(is_hub))
    def _():
        pltpu.make_async_remote_copy(
            src_ref=lw_ref,
            dst_ref=lw_ref,
            send_sem=lw_send_sem.at[0],
            recv_sem=lw_recv_sem,
            device_id=(b, place),
            device_id_type=MESH,
        ).wait_recv()

    log_sums(score_ref, lw_ref, ms_ref, 4)
    final = results(ms_ref)
    for v in range(3):
        out_ref[v] = final[v * ROWS : (v + 1) * ROWS, :]

    for layer in range(n_hubs, n_layers):

        @pl.when(z == hub_of(layer))
        def _():
            lw_copy(layer).wait_send()

    @pl.when(is_hub)
    def _():
        grid_wait(0, LAYER * n_hubs - 1).wait_send()

    @pl.when(jnp.logical_not(is_hub))
    def _():
        grid_wait(0, LAYER * n_hubs).wait_send()

    for copy in block_copies:
        copy.wait_send()


def solution(mesh):
    n_conf, n_orient = mesh.shape["conf"], mesh.shape["orient"]
    w = lane_matrix()

    def per_device(*given):
        particles, defocus_class, densities, contrast, grid_shift, log_prior = given
        operands = [
            pltpu.with_memory_space_constraint(x, pltpu.HBM)
            for x in (
                defocus_class,
                particles,
                densities,
                contrast,
                grid_shift,
                log_prior,
                jnp.asarray(w),
            )
        ]
        spectrum = pltpu.VMEM((HALF, 2 * ROWS, 2 * LANES), F32)
        return pl.pallas_call(
            functools.partial(kernel, n_conf, n_orient),
            out_shape=pltpu.VMEM((3, ROWS, ROWS), F32),
            in_specs=[pl.BlockSpec(memory_space=pltpu.HBM)] * 7,
            out_specs=pl.BlockSpec(memory_space=pltpu.VMEM),
            scratch_shapes=[
                pltpu.SMEM(defocus_class.shape, jnp.int32),
                pltpu.VMEM(particles.shape, BF16),
                pltpu.VMEM(densities.shape, BF16),
                pltpu.VMEM(contrast.shape, F32),
                pltpu.VMEM(grid_shift.shape, jnp.int32),
                pltpu.VMEM(log_prior.shape, F32),
                pltpu.VMEM(w.shape, BF16),
                pltpu.VMEM((3, 2 * ROWS, (TILES // 2 + 1) * LANES), BF16),
                pltpu.VMEM((2, LANES), F32),
                pltpu.VMEM((n_orient, 2, LANES), F32),
                spectrum,
                spectrum,
                spectrum,
                pltpu.VMEM((HALF, ROWS * ROWS // 2, 4 * LANES), BF16),
                pltpu.VMEM((HALF, ROWS * ROWS // 2, 4 * LANES), BF16),
                pltpu.VMEM((HALF, ROWS * ROWS // 2, 2 * LANES), F32),
                pltpu.VMEM((HALF, ROWS * ROWS // 2, 2 * LANES), F32),
                pltpu.VMEM((3 * ROWS, TILES, ROWS, LANES), F32),
                pltpu.VMEM((TILES, LANES), F32),
                pltpu.VMEM((TILES, LANES), F32),
                pltpu.VMEM((3 * ROWS, 2 * ROWS, LANES), F32),
                pltpu.SemaphoreType.DMA((7,)),
                pltpu.SemaphoreType.DMA((3,)),
                pltpu.SemaphoreType.DMA((3,)),
                pltpu.SemaphoreType.DMA,
                pltpu.SemaphoreType.DMA((n_orient // LAYER,)),
                pltpu.SemaphoreType.DMA((n_orient // LAYER,)),
                pltpu.SemaphoreType.DMA,
                pltpu.SemaphoreType.REGULAR,
            ],
            compiler_params=pltpu.CompilerParams(
                collective_id=0, has_side_effects=True, vmem_limit_bytes=56 * 2**20
            ),
        )(*operands)

    placed = (
        P(("conf", "orient"), None),
        P(("conf", "orient")),
        P("conf", None),
        P(),
        P("orient"),
        P("orient"),
    )
    return jax.shard_map(
        per_device,
        mesh=mesh,
        in_specs=placed,
        out_specs=P(None, None, ("conf", "orient")),
        check_vma=False,
    )
```

```python
import functools
import math

import jax
import jax.numpy as jnp
import numpy as np
from jax import lax
from jax.experimental import pallas as pl
from jax.experimental.pallas import tpu as pltpu
from jax.sharding import PartitionSpec as P

SIDE = 64
ROWS = 8
LANES = 128
TILES = 32
HALF = TILES // 2 + 1
MESH = pl.DeviceIdType.MESH
F32 = jnp.float32
BF16 = jnp.bfloat16
FAR = -1e30
LOG2E = 1.0 / math.log(2.0)
LAYER = 4


def lane_matrix():
    yl, x = np.divmod(np.arange(LANES), SIDE)
    phase = 2.0 * np.pi * (np.outer(x, x) % SIDE) / SIDE + np.pi * (np.outer(yl, yl) % 2)
    c, s = np.cos(phase), np.sin(phase)
    full = np.block([[c, s], [-s, c]]).astype(np.float32)
    high = full.astype(jnp.bfloat16)
    low = (full - high.astype(np.float32)).astype(jnp.bfloat16)
    return np.concatenate([high, low], axis=0)


def turned(z, num, den):
    re, im = z
    eighth = (8 * num / den) % 8
    if eighth == 0:
        return z
    if eighth == 2:
        return (-im, re)
    angle = 2.0 * math.pi * num / den
    c, s = math.cos(angle), math.sin(angle)
    if eighth == 1:
        return ((re - im) * c, (re + im) * c)
    if eighth == 3:
        return ((re + im) * c, (im - re) * c)
    return (re * c - im * s, re * s + im * c)


def complex_dft(z):
    n = len(z)
    if n == 1:
        return z
    even, odd = complex_dft(z[0::2]), complex_dft(z[1::2])
    out = [None] * n
    for k in range(n // 2):
        (er, ei), (re, im) = even[k], odd[k]
        if 4 * k == n:
            out[k], out[k + n // 2] = (er - im, ei + re), (er + im, ei - re)
        else:
            tr, ti = turned((re, im), k, n)
            out[k], out[k + n // 2] = (er + tr, ei + ti), (er - tr, ei - ti)
    return out


def real_dft(x):
    n = len(x)
    if n == 2:
        return [(x[0] + x[1], None, False), (x[0] - x[1], None, False)]
    h, q = n // 2, n // 4
    a = [x[j] + x[j + h] for j in range(h)]
    b = [x[j] - x[j + h] for j in range(h)]
    out = [None] * (h + 1)
    out[0::2] = real_dft(a)
    z = complex_dft([turned((b[j], b[j + q]), j, n) for j in range(q)])
    for m in range(q):
        k = 4 * m + 1
        if k <= h:
            out[k] = (*z[m], False)
        else:
            out[n - k] = (*z[m], True)
    return out


def inverse_real_dft(spec):
    h = len(spec) - 1
    n = 2 * h
    if n == 2:
        return [spec[0][0] + spec[1][0], spec[0][0] - spec[1][0]]
    q = n // 4
    even = inverse_real_dft(spec[0::2])
    z = complex_dft([spec[k] if k <= h else spec[n - k] for k in range(1, n, 4)])
    out = [None] * n
    for j in range(q):
        tr, ti = turned(z[j], j, n)
        out[j], out[j + h] = even[j] + tr, even[j] - tr
        out[j + q], out[j + q + h] = even[j + q] - ti, even[j + q] + ti
    return out


def needs_conjugate(k):
    while k % 2 == 0:
        k //= 2
    return k % 4 == 3


def lane_turn(k, scale):
    lane = lax.broadcasted_iota(jnp.int32, (ROWS, LANES), 1)
    angle = 2.0 * math.pi * k / SIDE
    c = jnp.where(lane >= SIDE, F32(scale * math.cos(angle)), F32(scale))
    s = jnp.where(lane >= SIDE, F32(scale * math.sin(angle)), F32(0.0))
    return c, s


def forward_rows(tiles, scale, dst, row):
    spec = real_dft(tiles)
    lane = lax.broadcasted_iota(jnp.int32, (ROWS, LANES), 1)
    rows = pl.ds(row, ROWS)
    zero = jnp.zeros((ROWS, LANES), F32)
    for k, (re, im, conj) in enumerate(spec):
        if k == 0:
            nr, ni = re, zero
        elif k == HALF - 1:
            nr, ni = jnp.where(lane < SIDE, re, 0.0), jnp.where(lane < SIDE, 0.0, re)
        else:
            c, s = lane_turn(k, scale)
            if conj:
                nr, ni = re * c + im * s, re * s - im * c
            else:
                nr, ni = re * c - im * s, re * s + im * c
        dst[k, rows, 0:LANES] = nr
        dst[k, rows, LANES : 2 * LANES] = ni


def split_in_two(x):
    high = x.astype(BF16)
    return high, (x - high.astype(F32)).astype(BF16)


def times_lane_matrix(high, low, w_ref):
    w_high, w_low = w_ref[0 : 2 * LANES, :], w_ref[2 * LANES :, :]
    return jnp.dot(
        jnp.concatenate([high, low, high], axis=1),
        jnp.concatenate([w_high, w_high, w_low], axis=0),
        preferred_element_type=F32,
    )


def forward_lanes(src, w_ref):
    x = src[...].reshape(HALF * 2 * ROWS, 2 * LANES)
    high, low = split_in_two(x)
    return times_lane_matrix(high, low, w_ref).reshape(HALF, 2 * ROWS, 2 * LANES)


def grid_weights(gath, first, count):
    shift = gath[first : first + count, 0, :].astype(jnp.int32)
    weight = gath[first : first + count, 1, :]
    high = weight.astype(BF16).astype(F32)
    low = weight - high
    dy, dx = shift // SIDE, shift % SIDE
    place = dy % 2 * TILES + dy // 2
    row = lax.broadcasted_iota(jnp.int32, (SIDE, LANES), 0)
    lefts, rights = [], []
    for r in range(count):
        mine = row == place[r : r + 1, :]
        parts = [jnp.where(mine, x[r : r + 1, :], 0.0) for x in (high, low)]
        lefts.append(jnp.concatenate(parts, axis=0).astype(BF16))
        right = jnp.where(row == dx[r : r + 1, :], 1.0, 0.0).astype(BF16)
        rights.append(jnp.concatenate([right, right], axis=0))
    both = lax.dot_general(
        jnp.concatenate(lefts, axis=1),
        jnp.concatenate(rights, axis=1),
        (((1,), (1,)), ((), ())),
        preferred_element_type=F32,
    )
    total = both[0:SIDE] + both[SIDE:]
    lane = lax.broadcasted_iota(jnp.int32, (TILES, LANES), 1)
    return jnp.where(lane < SIDE, total[0:TILES], total[TILES:])


def log2_or_far(total):
    some = total > 0.0
    return jnp.where(some, jnp.log(jnp.where(some, total, 1.0)) / math.log(2.0), FAR)


def pair_products(fq, de, first, count, lhs):
    for k in range(HALF):
        f, q = fq[k, 0:ROWS, :], fq[k, ROWS : 2 * ROWS, :]
        fr, fi, qr, qi = f[:, :LANES], f[:, LANES:], q[:, :LANES], q[:, LANES:]
        fd, qd = fr - fi, qr - qi
        parts = []
        for c in range(first, first + count):
            d, e = de[k, c : c + 1, :], de[k, ROWS + c : ROWS + c + 1, :]
            dr, ds, dm = (d[:, i * LANES : (i + 1) * LANES] for i in range(3))
            er, es, em = (e[:, i * LANES : (i + 1) * LANES] for i in range(3))
            shared = dr * fd + er * qd
            re = shared + (fi * ds + qi * es)
            im = shared + (fr * dm + qr * em)
            parts.append(jnp.concatenate([re, im], axis=1))
        for i in range(0, count, 2):
            high, low = split_in_two(jnp.concatenate(parts[i : i + 2], axis=0))
            rows = pl.ds(i * ROWS, 2 * ROWS)
            lhs[k, rows, 0 : 2 * LANES] = high
            lhs[k, rows, 2 * LANES :] = low


def inverse_lanes(lhs, w_ref, dst):
    rows = lhs.shape[1]
    x = lhs[...].reshape(HALF * rows, 4 * LANES)
    out = times_lane_matrix(x[:, : 2 * LANES], x[:, 2 * LANES :], w_ref)
    dst[...] = out.reshape(HALF, rows, 2 * LANES)


def scores(g_ref, score_ref, first, count):
    lane = lax.broadcasted_iota(jnp.int32, (ROWS, LANES), 1)
    for i in range(count):
        rows = pl.ds(i * ROWS, ROWS)
        spec = []
        for k in range(HALF):
            re, im = g_ref[k, rows, 0:LANES], g_ref[k, rows, LANES : 2 * LANES]
            if k == 0:
                spec.append((re, None))
            elif k == HALF - 1:
                spec.append((jnp.where(lane < SIDE, re, -im), None))
            else:
                c, s = lane_turn(k, 1.0)
                nr = re * c - im * s
                ni = -(re * s) - im * c if needs_conjugate(k) else re * s + im * c
                spec.append((nr, ni))
        for j, value in enumerate(inverse_real_dft(spec)):
            score_ref[first + i, j] = value


def tree(join, values):
    while len(values) > 1:
        values = [join(*values[i : i + 2]) for i in range(0, len(values) - 1, 2)] + (
            [values[-1]] if len(values) % 2 else []
        )
    return values[0]


def log_sums(score_ref, lw_ref, ms_ref, per_step):
    def some_groups(step, _):
        for p in range(per_step):
            i = step * per_step + p
            value = [score_ref[i, j] + lw_ref[j : j + 1, :] for j in range(TILES)]
            top = tree(jnp.maximum, value)
            total = tree(jnp.add, [jnp.exp2(v - top) for v in value])
            ms_ref[i, 0:ROWS, :] = top
            ms_ref[i, ROWS : 2 * ROWS, :] = total
        return 0

    lax.fori_loop(0, score_ref.shape[0] // per_step, some_groups, 0)


def results(ms_ref):
    lane = lax.broadcasted_iota(jnp.int32, (ROWS, LANES), 1)
    tops = jnp.zeros((ROWS, LANES), F32)
    sums = jnp.ones((ROWS, LANES), F32)
    for i in range(ms_ref.shape[0]):
        top, total = ms_ref[i, 0:ROWS, :], ms_ref[i, ROWS : 2 * ROWS, :]
        highest = jnp.max(top, axis=1, keepdims=True)
        summed = jnp.sum(total * jnp.exp2(top - highest), axis=1, keepdims=True)
        tops = jnp.where(lane == i, highest, tops)
        sums = jnp.where(lane == i, summed, sums)
    return (tops * math.log(2.0) + jnp.log(sums)).T


def kernel(
    n_conf,
    n_orient,
    cls_hbm,
    part_hbm,
    dens_hbm,
    con_hbm,
    shift_hbm,
    prior_hbm,
    w_hbm,
    out_ref,
    cls_ref,
    part_ref,
    dens_ref,
    con_ref,
    shift_ref,
    prior_ref,
    w_ref,
    blocks,
    msg,
    gath,
    stage,
    spec_fq,
    spec_de,
    lhs_a,
    lhs_b,
    g_a,
    g_b,
    score_ref,
    csq_ref,
    early_ref,
    lw_ref,
    ms_ref,
    in_sem,
    block_send_sem,
    block_recv_sem,
    grid_send_sem,
    grid_recv_sem,
    lw_send_sem,
    lw_recv_sem,
    pair_sem,
):
    b = lax.axis_index("conf")
    o = lax.axis_index("orient")
    n_layers = n_orient // LAYER
    n_hubs = max(n_layers // 4, 1)
    z = o // LAYER
    place = lax.rem(o, LAYER)
    core = lax.rem(o, 2)
    first_core = core == 0
    is_hub = z < n_hubs

    def conf_at(offset):
        return lax.rem(b + offset + n_conf, n_conf)

    barrier = pltpu.get_barrier_semaphore()

    def greet(conf, orient):
        pl.semaphore_signal(
            barrier, inc=1, device_id=(conf, orient), device_id_type=MESH
        )

    def tell_sibling():
        pl.semaphore_signal(
            pair_sem, inc=1, device_id=(b, o + 1 - 2 * core), device_id_type=MESH
        )

    x = lax.rem(b, n_conf // 2)
    last_x = x == n_conf // 2 - 1

    @pl.when(x != 1)
    def _():
        greet(conf_at(-2), o - core + 1)

    greet(conf_at(-1), o - core + 1)

    loads = []
    for i, (src, dst) in enumerate(
        (
            (shift_hbm, shift_ref),
            (prior_hbm, prior_ref),
            (cls_hbm, cls_ref),
            (part_hbm, part_ref),
            (con_hbm, con_ref),
            (dens_hbm, dens_ref),
            (w_hbm, w_ref),
        )
    ):
        loads.append(pltpu.make_async_copy(src, dst, in_sem.at[i]))
        loads[-1].start()

    @pl.when(core == 1)
    def _():
        greet(b, o - 1)

    @pl.when(is_hub)
    def _():
        for t in range(2, LAYER, 2):
            greet(b, z * LAYER + lax.rem(place - core + t, LAYER))

        def above(t, _):
            greet(b, 2 * t)
            return 0

        lax.fori_loop((z + 1) * (LAYER // 2), n_orient // 2, above, 0)

    count = shift_ref.shape[0]
    loads[0].wait()
    loads[1].wait()
    msg[...] = jnp.zeros_like(msg)
    msg[0:1, 0:count] = shift_ref[...].astype(F32).reshape(1, count)
    msg[1:2, 0:count] = jnp.exp(prior_ref[...]).reshape(1, count)
    gath[o] = msg[...]

    hubs_below = LAYER * jnp.minimum(z, n_hubs)

    @pl.when(first_core)
    def _():
        pl.semaphore_wait(barrier, 1 + hubs_below + jnp.where(is_hub, LAYER - 2, 0))
        tell_sibling()

    @pl.when(core == 1)
    def _():
        pl.semaphore_wait(pair_sem, 1)

    def send_grid(to):
        pltpu.make_async_remote_copy(
            src_ref=msg,
            dst_ref=gath.at[o],
            send_sem=grid_send_sem,
            recv_sem=grid_recv_sem.at[z],
            device_id=(b, to),
            device_id_type=MESH,
        ).start()

    def send_below(t, _):
        send_grid(t)
        return 0

    def send_beside(t, _):
        send_grid(z * LAYER + lax.rem(place + t, LAYER))
        return 0

    lax.fori_loop(0, hubs_below, send_below, 0)
    lax.fori_loop(1, jnp.where(is_hub, LAYER, 1), send_beside, 0)

    for load in loads[2:5]:
        load.wait()
    row = lax.broadcasted_iota(jnp.int32, (ROWS, LANES), 0)
    cls = jnp.zeros((ROWS, LANES), jnp.int32)
    for i in range(ROWS):
        cls = jnp.where(row == i, cls_ref[i], cls)

    picked = [cls == k for k in range(con_ref.shape[0])]

    def envelope(j):
        out = jnp.zeros((ROWS, LANES), F32)
        for k, mask in enumerate(picked):
            out = jnp.where(mask, con_ref[k : k + 1, j * LANES : (j + 1) * LANES], out)
        return out

    half = TILES // 2
    for j in range(half):
        pair = [
            part_ref[:, t * LANES : (t + 1) * LANES].astype(F32) * envelope(t)
            for t in (j, j + half)
        ]
        blocks[0, :, j * LANES : (j + 1) * LANES] = jnp.concatenate(pair, axis=0).astype(BF16)
    blocks[0, :, half * LANES :] = jnp.concatenate([cls, cls], axis=0).astype(F32).astype(BF16)

    def block_copy(src, dst, to):
        return pltpu.make_async_remote_copy(
            src_ref=blocks.at[src],
            dst_ref=blocks.at[dst],
            send_sem=block_send_sem.at[2 * src + to - 1],
            recv_sem=block_recv_sem.at[dst],
            device_id=(conf_at(to), o),
            device_id_type=MESH,
        )

    first_copy, second_copy, passed_copy = (
        block_copy(0, 1, 1),
        block_copy(0, 2, 2),
        block_copy(1, 2, 1),
    )

    def send_blocks():
        @pl.when(core == 1)
        def _():
            pl.semaphore_wait(barrier, jnp.where(last_x, 2, 4))
            tell_sibling()

        @pl.when(first_core)
        def _():
            pl.semaphore_wait(pair_sem, 1)

        first_copy.start()
        pl.when(jnp.logical_not(last_x))(second_copy.start)

    send_early = b >= n_conf - 2
    pl.when(send_early)(send_blocks)

    def grid_wait(layer, number):
        slots = gath.at[pl.ds(layer * LAYER, number)]
        return pltpu.make_async_remote_copy(
            src_ref=slots,
            dst_ref=slots,
            send_sem=grid_send_sem,
            recv_sem=grid_recv_sem.at[layer],
            device_id=(conf_at(1), o),
            device_id_type=MESH,
        )

    def answer(layer):
        @pl.when(z < layer)
        def _():
            grid_wait(layer, LAYER).wait_recv()
            for t in range(LAYER):
                send_grid(layer * LAYER + t)

    def forward(tiles, other_tiles, scale):
        forward_rows(tiles, scale, stage, 0)
        forward_rows(other_tiles, scale, stage, ROWS)
        return forward_lanes(stage, w_ref)

    loads[5].wait()
    loads[6].wait()
    dens = [dens_ref[:, j * LANES : (j + 1) * LANES].astype(F32) for j in range(TILES)]
    excess = [(t * t - 1.0).astype(BF16).astype(F32) for t in dens]
    de = forward(dens, excess, 1.0)
    dr, di = de[:, :, :LANES], de[:, :, LANES:]
    spec_de[...] = jnp.concatenate([dr, dr + di, di - dr], axis=2)
    con = con_ref[...]
    csq_ref[...] = (con * con).astype(BF16)

    def visit(v):
        n_cls = csq_ref.shape[0]
        classes = blocks[v, :, half * LANES :].astype(F32)[0:ROWS, 0:n_cls]
        column = lax.broadcasted_iota(jnp.int32, (ROWS, n_cls), 1).astype(F32)
        picks = jnp.where(classes == column, 1.0, 0.0).astype(BF16)
        squares = jnp.dot(picks, csq_ref[...], preferred_element_type=F32)
        pairs = [blocks[v, :, j * LANES : (j + 1) * LANES].astype(F32) for j in range(half)]
        rows = [p[0:ROWS] for p in pairs] + [p[ROWS:] for p in pairs]
        rows = [r * (LOG2E * 2.0**-16) for r in rows]
        others = [
            squares[:, j * LANES : (j + 1) * LANES] * (-LOG2E * 2.0**-17) for j in range(TILES)
        ]
        spec_fq[...] = forward(rows, others, 2.0)
        part = ROWS // 2
        pair_products(spec_fq, spec_de, 0, part, lhs_a)
        inverse_lanes(lhs_a, w_ref, g_a)
        pair_products(spec_fq, spec_de, part, part, lhs_b)
        inverse_lanes(lhs_b, w_ref, g_b)
        scores(g_a, score_ref, v * ROWS, part)
        scores(g_b, score_ref, v * ROWS + part, part)

    def lw_copy(layer):
        return pltpu.make_async_remote_copy(
            src_ref=lw_ref,
            dst_ref=lw_ref,
            send_sem=lw_send_sem.at[layer],
            recv_sem=lw_recv_sem,
            device_id=(b, layer * LAYER + place),
            device_id_type=MESH,
        )

    def hub_of(layer):
        return n_hubs - 1 if layer <= n_layers // 2 else 0

    def hear(layers):
        for layer in layers:

            @pl.when(z == layer)
            def _():
                grid_wait(layer, LAYER - 1).wait_recv()

            @pl.when((z > layer) | ((z != layer) & (layer >= n_hubs)))
            def _():
                grid_wait(layer, LAYER).wait_recv()

    early = max(n_layers // 2 - 1, 1)

    def make_weights():
        last = (early + n_layers + 1) // 2
        total = early_ref[...]
        for first, end in ((last, n_layers), (early, last)):
            hear(range(first, end))
            total = total + grid_weights(gath, first * LAYER, (end - first) * LAYER)
        lw_ref[...] = log2_or_far(total)
        for layer in range(n_hubs, n_layers):

            @pl.when(z == hub_of(layer))
            def _():
                lw_copy(layer).start()

    visit(0)
    pl.when(jnp.logical_not(send_early))(send_blocks)
    for layer in range(1, n_hubs):
        answer(layer)

    @pl.when(is_hub)
    def _():
        hear(range(early))
        early_ref[...] = grid_weights(gath, 0, early * LAYER)

    weights_at = jnp.where((x == 1) | ((x == 0) & (z > 0)), 2, 3)

    def step(v, _):
        @pl.when(is_hub & (weights_at == v))
        def _():
            make_weights()

        @pl.when(v < 3)
        def _():
            pltpu.make_async_remote_copy(
                src_ref=blocks.at[0],
                dst_ref=blocks.at[v],
                send_sem=block_send_sem.at[v],
                recv_sem=block_recv_sem.at[v],
                device_id=(conf_at(1), o),
                device_id_type=MESH,
            ).wait_recv()
            pl.when((v == 1) & (x == 0))(passed_copy.start)
            visit(v)

        return 0

    lax.fori_loop(1, 4, step, 0)

    @pl.when(jnp.logical_not(is_hub))
    def _():
        pltpu.make_async_remote_copy(
            src_ref=lw_ref,
            dst_ref=lw_ref,
            send_sem=lw_send_sem.at[0],
            recv_sem=lw_recv_sem,
            device_id=(b, place),
            device_id_type=MESH,
        ).wait_recv()

    log_sums(score_ref, lw_ref, ms_ref, 4)
    final = results(ms_ref)
    for v in range(3):
        out_ref[v] = final[v * ROWS : (v + 1) * ROWS, :]

    for layer in range(n_hubs, n_layers):

        @pl.when(z == hub_of(layer))
        def _():
            lw_copy(layer).wait_send()

    @pl.when(is_hub)
    def _():
        grid_wait(0, LAYER * n_hubs - 1).wait_send()

    @pl.when(jnp.logical_not(is_hub))
    def _():
        grid_wait(0, LAYER * n_hubs).wait_send()

    first_copy.wait_send()
    pl.when(jnp.logical_not(last_x))(second_copy.wait_send)
    pl.when(x == 0)(passed_copy.wait_send)


def solution(mesh):
    n_conf, n_orient = mesh.shape["conf"], mesh.shape["orient"]
    w = lane_matrix()

    def per_device(*given):
        particles, defocus_class, densities, contrast, grid_shift, log_prior = given
        operands = [
            pltpu.with_memory_space_constraint(x, pltpu.HBM)
            for x in (
                defocus_class,
                particles,
                densities,
                contrast,
                grid_shift,
                log_prior,
                jnp.asarray(w),
            )
        ]
        spectrum = pltpu.VMEM((HALF, 2 * ROWS, 2 * LANES), F32)
        return pl.pallas_call(
            functools.partial(kernel, n_conf, n_orient),
            out_shape=pltpu.VMEM((3, ROWS, ROWS), F32),
            in_specs=[pl.BlockSpec(memory_space=pltpu.HBM)] * 7,
            out_specs=pl.BlockSpec(memory_space=pltpu.VMEM),
            scratch_shapes=[
                pltpu.SMEM(defocus_class.shape, jnp.int32),
                pltpu.VMEM(particles.shape, BF16),
                pltpu.VMEM(densities.shape, BF16),
                pltpu.VMEM(contrast.shape, F32),
                pltpu.VMEM(grid_shift.shape, jnp.int32),
                pltpu.VMEM(log_prior.shape, F32),
                pltpu.VMEM(w.shape, BF16),
                pltpu.VMEM((3, 2 * ROWS, (TILES // 2 + 1) * LANES), BF16),
                pltpu.VMEM((2, LANES), F32),
                pltpu.VMEM((n_orient, 2, LANES), F32),
                spectrum,
                spectrum,
                pltpu.VMEM((HALF, 2 * ROWS, 3 * LANES), F32),
                pltpu.VMEM((HALF, ROWS * ROWS // 2, 4 * LANES), BF16),
                pltpu.VMEM((HALF, ROWS * ROWS // 2, 4 * LANES), BF16),
                pltpu.VMEM((HALF, ROWS * ROWS // 2, 2 * LANES), F32),
                pltpu.VMEM((HALF, ROWS * ROWS // 2, 2 * LANES), F32),
                pltpu.VMEM((3 * ROWS, TILES, ROWS, LANES), F32),
                pltpu.VMEM(contrast.shape, BF16),
                pltpu.VMEM((TILES, LANES), F32),
                pltpu.VMEM((TILES, LANES), F32),
                pltpu.VMEM((3 * ROWS, 2 * ROWS, LANES), F32),
                pltpu.SemaphoreType.DMA((7,)),
                pltpu.SemaphoreType.DMA((4,)),
                pltpu.SemaphoreType.DMA((3,)),
                pltpu.SemaphoreType.DMA,
                pltpu.SemaphoreType.DMA((n_orient // LAYER,)),
                pltpu.SemaphoreType.DMA((n_orient // LAYER,)),
                pltpu.SemaphoreType.DMA,
                pltpu.SemaphoreType.REGULAR,
            ],
            compiler_params=pltpu.CompilerParams(
                collective_id=0, has_side_effects=True, vmem_limit_bytes=56 * 2**20
            ),
        )(*operands)

    placed = (
        P(("conf", "orient"), None),
        P(("conf", "orient")),
        P("conf", None),
        P(),
        P("orient"),
        P("orient"),
    )
    return jax.shard_map(
        per_device,
        mesh=mesh,
        in_specs=placed,
        out_specs=P(None, None, ("conf", "orient")),
        check_vma=False,
    )
```

```python
import functools
import math

import jax
import jax.numpy as jnp
import numpy as np
from jax import lax
from jax.experimental import pallas as pl
from jax.experimental.pallas import tpu as pltpu
from jax.sharding import PartitionSpec as P

SIDE = 64
ROWS = 8
LANES = 128
TILES = 32
HALF = TILES // 2 + 1
MESH = pl.DeviceIdType.MESH
F32 = jnp.float32
BF16 = jnp.bfloat16
FAR = -1e30
LOG2E = 1.0 / math.log(2.0)
LAYER = 4


def lane_matrix():
    yl, x = np.divmod(np.arange(LANES), SIDE)
    phase = 2.0 * np.pi * (np.outer(x, x) % SIDE) / SIDE + np.pi * (np.outer(yl, yl) % 2)
    c, s = np.cos(phase), np.sin(phase)
    full = np.block([[c, s], [-s, c]]).astype(np.float32)
    high = full.astype(jnp.bfloat16)
    low = (full - high.astype(np.float32)).astype(jnp.bfloat16)
    return np.concatenate([high, low], axis=0)


def turned(z, num, den):
    re, im = z
    eighth = (8 * num / den) % 8
    if eighth == 0:
        return z
    if eighth == 2:
        return (-im, re)
    angle = 2.0 * math.pi * num / den
    c, s = math.cos(angle), math.sin(angle)
    if eighth == 1:
        return ((re - im) * c, (re + im) * c)
    if eighth == 3:
        return ((re + im) * c, (im - re) * c)
    return (re * c - im * s, re * s + im * c)


def complex_dft(z):
    n = len(z)
    if n == 1:
        return z
    even, odd = complex_dft(z[0::2]), complex_dft(z[1::2])
    out = [None] * n
    for k in range(n // 2):
        (er, ei), (re, im) = even[k], odd[k]
        if 4 * k == n:
            out[k], out[k + n // 2] = (er - im, ei + re), (er + im, ei - re)
        else:
            tr, ti = turned((re, im), k, n)
            out[k], out[k + n // 2] = (er + tr, ei + ti), (er - tr, ei - ti)
    return out


def real_dft(x):
    n = len(x)
    if n == 2:
        return [(x[0] + x[1], None, False), (x[0] - x[1], None, False)]
    h, q = n // 2, n // 4
    a = [x[j] + x[j + h] for j in range(h)]
    b = [x[j] - x[j + h] for j in range(h)]
    out = [None] * (h + 1)
    out[0::2] = real_dft(a)
    z = complex_dft([turned((b[j], b[j + q]), j, n) for j in range(q)])
    for m in range(q):
        k = 4 * m + 1
        if k <= h:
            out[k] = (*z[m], False)
        else:
            out[n - k] = (*z[m], True)
    return out


def inverse_real_dft(spec):
    h = len(spec) - 1
    n = 2 * h
    if n == 2:
        return [spec[0][0] + spec[1][0], spec[0][0] - spec[1][0]]
    q = n // 4
    even = inverse_real_dft(spec[0::2])
    z = complex_dft([spec[k] if k <= h else spec[n - k] for k in range(1, n, 4)])
    out = [None] * n
    for j in range(q):
        tr, ti = turned(z[j], j, n)
        out[j], out[j + h] = even[j] + tr, even[j] - tr
        out[j + q], out[j + q + h] = even[j + q] - ti, even[j + q] + ti
    return out


def needs_conjugate(k):
    while k % 2 == 0:
        k //= 2
    return k % 4 == 3


def by_half(first, second):
    lane = lax.broadcasted_iota(jnp.int32, (ROWS, LANES), 1)
    return jnp.where(lane >= SIDE, F32(second), F32(first))


def forward_rows(tiles, dst, row, scale=1.0, for_products=False):
    spec = real_dft(tiles)
    rows = pl.ds(row, ROWS)
    zero = jnp.zeros((ROWS, LANES), F32)
    lane = lax.broadcasted_iota(jnp.int32, (ROWS, LANES), 1)
    for k, (re, im, conj) in enumerate(spec):
        if im is None:
            re = re if scale == 1.0 else re * scale
        if k == 0:
            nr, ni = re, zero
        elif k == HALF - 1:
            nr, ni = jnp.where(lane < SIDE, re, 0.0), jnp.where(lane < SIDE, 0.0, re)
        else:
            angle = 2.0 * math.pi * k / SIDE
            if for_products:
                h = math.cos(angle / 2.0) * 2.0 * scale
                c, v = F32(h * math.cos(angle / 2.0)), h * math.sin(angle / 2.0)
                s = by_half(-v, v)
            else:
                c, s = by_half(1.0, math.cos(angle)), by_half(0.0, math.sin(angle))
            if conj:
                nr, ni = re * c + im * s, re * s - im * c
            else:
                nr, ni = re * c - im * s, re * s + im * c
        dst[k, rows, 0:LANES] = nr
        dst[k, rows, LANES : 2 * LANES] = ni


def inverse_turn(k, re, im):
    if k == 0:
        return re, None
    if k == HALF - 1:
        lane = lax.broadcasted_iota(jnp.int32, (ROWS, LANES), 1)
        return jnp.where(lane < SIDE, re, -im), None
    t = math.tan(math.pi * k / SIDE)
    if needs_conjugate(k):
        return re - im * by_half(-t, t), re * by_half(t, -t) - im
    return re - im * by_half(-t, t), im + re * by_half(-t, t)


def split_in_two(x):
    high = x.astype(BF16)
    return high, (x - high.astype(F32)).astype(BF16)


def times_lane_matrix(high, low, w_ref):
    w_high, w_low = w_ref[0 : 2 * LANES, :], w_ref[2 * LANES :, :]
    return jnp.dot(
        jnp.concatenate([high, low, high], axis=1),
        jnp.concatenate([w_high, w_high, w_low], axis=0),
        preferred_element_type=F32,
    )


def forward_lanes(src, w_ref):
    tiles, rows, lanes = src.shape
    high, low = split_in_two(src[...].reshape(tiles * rows, lanes))
    return times_lane_matrix(high, low, w_ref).reshape(tiles, rows, lanes)


def grid_weights(gath, first, count):
    shift = gath[first : first + count, 0, :].astype(jnp.int32)
    weight = gath[first : first + count, 1, :]
    high = weight.astype(BF16).astype(F32)
    low = weight - high
    dy, dx = shift // SIDE, shift % SIDE
    place = dy % 2 * TILES + dy // 2
    row = lax.broadcasted_iota(jnp.int32, (SIDE, LANES), 0)
    lefts, rights = [], []
    for r in range(count):
        mine = row == place[r : r + 1, :]
        parts = [jnp.where(mine, x[r : r + 1, :], 0.0) for x in (high, low)]
        lefts.append(jnp.concatenate(parts, axis=0).astype(BF16))
        right = jnp.where(row == dx[r : r + 1, :], 1.0, 0.0).astype(BF16)
        rights.append(jnp.concatenate([right, right], axis=0))
    both = lax.dot_general(
        jnp.concatenate(lefts, axis=1),
        jnp.concatenate(rights, axis=1),
        (((1,), (1,)), ((), ())),
        preferred_element_type=F32,
    )
    total = both[0:SIDE] + both[SIDE:]
    lane = lax.broadcasted_iota(jnp.int32, (TILES, LANES), 1)
    return jnp.where(lane < SIDE, total[0:TILES], total[TILES:])


def log2_or_far(total):
    some = total > 0.0
    return jnp.where(some, jnp.log(jnp.where(some, total, 1.0)) / math.log(2.0), FAR)


def pair_products(f_ref, q_ref, de, first, count, lhs):
    for k in range(HALF):
        f, q = f_ref[k], q_ref[:, k * 2 * LANES : (k + 1) * 2 * LANES]
        fr, fi, qr, qi = f[:, :LANES], f[:, LANES:], q[:, :LANES], q[:, LANES:]
        fd, qd = fr - fi, qr - qi
        parts = []
        for c in range(first, first + count):
            d, e = de[k, c : c + 1, :], de[k, ROWS + c : ROWS + c + 1, :]
            dr, ds, dm = (d[:, i * LANES : (i + 1) * LANES] for i in range(3))
            er, es, em = (e[:, i * LANES : (i + 1) * LANES] for i in range(3))
            shared = dr * fd + er * qd
            re = shared + (fi * ds + qi * es)
            im = shared + (fr * dm + qr * em)
            parts.append(jnp.concatenate([re, im], axis=1))
        for i in range(0, count, 2):
            high, low = split_in_two(jnp.concatenate(parts[i : i + 2], axis=0))
            rows = pl.ds(i * ROWS, 2 * ROWS)
            lhs[k, rows, 0 : 2 * LANES] = high
            lhs[k, rows, 2 * LANES :] = low


def inverse_lanes(lhs, w_ref, dst):
    rows = lhs.shape[1]
    x = lhs[...].reshape(HALF * rows, 4 * LANES)
    out = times_lane_matrix(x[:, : 2 * LANES], x[:, 2 * LANES :], w_ref)
    dst[...] = out.reshape(HALF, rows, 2 * LANES)


def scores(g_ref, score_ref, first, count):
    for i in range(count):
        rows = pl.ds(i * ROWS, ROWS)
        spec = [
            inverse_turn(k, g_ref[k, rows, 0:LANES], g_ref[k, rows, LANES : 2 * LANES])
            for k in range(HALF)
        ]
        for j, value in enumerate(inverse_real_dft(spec)):
            score_ref[first + i, j] = value


def tree(join, values):
    while len(values) > 1:
        values = [join(*values[i : i + 2]) for i in range(0, len(values) - 1, 2)] + (
            [values[-1]] if len(values) % 2 else []
        )
    return values[0]


def log_sums(score_ref, lw_ref, ms_ref, first, end):
    def one_visit(v, _):
        for p in range(ROWS):
            i = v * ROWS + p
            value = [score_ref[i, j] + lw_ref[j : j + 1, :] for j in range(TILES)]
            top = tree(jnp.maximum, value)
            total = tree(jnp.add, [jnp.exp2(v - top) for v in value])
            ms_ref[i, 0:ROWS, :] = top
            ms_ref[i, ROWS : 2 * ROWS, :] = total
        return 0

    lax.fori_loop(first, end, one_visit, 0)


def results(ms_ref):
    lane = lax.broadcasted_iota(jnp.int32, (ROWS, LANES), 1)
    tops = jnp.zeros((ROWS, LANES), F32)
    sums = jnp.ones((ROWS, LANES), F32)
    for i in range(ms_ref.shape[0]):
        top, total = ms_ref[i, 0:ROWS, :], ms_ref[i, ROWS : 2 * ROWS, :]
        highest = jnp.max(top, axis=1, keepdims=True)
        summed = jnp.sum(total * jnp.exp2(top - highest), axis=1, keepdims=True)
        tops = jnp.where(lane == i, highest, tops)
        sums = jnp.where(lane == i, summed, sums)
    return (tops * math.log(2.0) + jnp.log(sums)).T


def kernel(
    n_conf,
    n_orient,
    cls_hbm,
    part_hbm,
    dens_hbm,
    con_hbm,
    shift_hbm,
    prior_hbm,
    w_hbm,
    out_ref,
    cls_ref,
    part_ref,
    dens_ref,
    con_ref,
    shift_ref,
    prior_ref,
    w_ref,
    blocks,
    msg,
    gath,
    stage,
    stage_f,
    spec_f,
    spec_q,
    spec_de,
    lhs_a,
    lhs_b,
    g_a,
    g_b,
    score_ref,
    class_spec,
    early_ref,
    lw_ref,
    ms_ref,
    in_sem,
    block_send_sem,
    block_recv_sem,
    grid_send_sem,
    grid_recv_sem,
    lw_send_sem,
    lw_recv_sem,
    pair_sem,
):
    b = lax.axis_index("conf")
    o = lax.axis_index("orient")
    n_layers = n_orient // LAYER
    n_hubs = max(n_layers // 4, 1)
    z = o // LAYER
    place = lax.rem(o, LAYER)
    core = lax.rem(o, 2)
    first_core = core == 0
    is_hub = z < n_hubs

    def conf_at(offset):
        return lax.rem(b + offset + n_conf, n_conf)

    barrier = pltpu.get_barrier_semaphore()

    def greet(conf, orient):
        pl.semaphore_signal(
            barrier, inc=1, device_id=(conf, orient), device_id_type=MESH
        )

    def tell_sibling():
        pl.semaphore_signal(
            pair_sem, inc=1, device_id=(b, o + 1 - 2 * core), device_id_type=MESH
        )

    x = lax.rem(b, n_conf // 2)
    last_x = x == n_conf // 2 - 1

    @pl.when(x != 1)
    def _():
        greet(conf_at(-2), o - core + 1)

    greet(conf_at(-1), o - core + 1)

    loads = []
    for i, (src, dst) in enumerate(
        (
            (shift_hbm, shift_ref),
            (prior_hbm, prior_ref),
            (cls_hbm, cls_ref),
            (part_hbm, part_ref),
            (con_hbm, con_ref),
            (dens_hbm, dens_ref),
            (w_hbm, w_ref),
        )
    ):
        loads.append(pltpu.make_async_copy(src, dst, in_sem.at[i]))
        loads[-1].start()

    @pl.when(core == 1)
    def _():
        greet(b, o - 1)

    @pl.when(is_hub)
    def _():
        for t in range(2, LAYER, 2):
            greet(b, z * LAYER + lax.rem(place - core + t, LAYER))

        def above(t, _):
            greet(b, 2 * t)
            return 0

        lax.fori_loop((z + 1) * (LAYER // 2), n_orient // 2, above, 0)

    count = shift_ref.shape[0]
    loads[0].wait()
    loads[1].wait()
    msg[...] = jnp.zeros_like(msg)
    msg[0:1, 0:count] = shift_ref[...].astype(F32).reshape(1, count)
    msg[1:2, 0:count] = jnp.exp(prior_ref[...]).reshape(1, count)
    gath[o] = msg[...]

    hubs_below = LAYER * jnp.minimum(z, n_hubs)

    @pl.when(first_core)
    def _():
        pl.semaphore_wait(barrier, 1 + hubs_below + jnp.where(is_hub, LAYER - 2, 0))
        tell_sibling()

    @pl.when(core == 1)
    def _():
        pl.semaphore_wait(pair_sem, 1)

    def send_grid(to):
        pltpu.make_async_remote_copy(
            src_ref=msg,
            dst_ref=gath.at[o],
            send_sem=grid_send_sem,
            recv_sem=grid_recv_sem.at[z],
            device_id=(b, to),
            device_id_type=MESH,
        ).start()

    def send_below(t, _):
        send_grid(t)
        return 0

    def send_beside(t, _):
        send_grid(z * LAYER + lax.rem(place + t, LAYER))
        return 0

    lax.fori_loop(0, hubs_below, send_below, 0)
    lax.fori_loop(1, jnp.where(is_hub, LAYER, 1), send_beside, 0)

    for load in loads[2:5]:
        load.wait()
    row = lax.broadcasted_iota(jnp.int32, (ROWS, LANES), 0)
    cls = jnp.zeros((ROWS, LANES), jnp.int32)
    for i in range(ROWS):
        cls = jnp.where(row == i, cls_ref[i], cls)

    picked = [cls == k for k in range(con_ref.shape[0])]

    def envelope(j):
        out = jnp.zeros((ROWS, LANES), F32)
        for k, mask in enumerate(picked):
            out = jnp.where(mask, con_ref[k : k + 1, j * LANES : (j + 1) * LANES], out)
        return out

    half = TILES // 2
    for j in range(half):
        pair = [
            part_ref[:, t * LANES : (t + 1) * LANES].astype(F32) * envelope(t)
            for t in (j, j + half)
        ]
        blocks[0, :, j * LANES : (j + 1) * LANES] = jnp.concatenate(pair, axis=0).astype(BF16)
    blocks[0, :, half * LANES :] = jnp.concatenate([cls, cls], axis=0).astype(F32).astype(BF16)

    middle = half // 2 * LANES
    pieces = (pl.ds(0, middle), pl.ds(middle, blocks.shape[2] - middle))

    def block_copies(src, dst, to):
        return [
            pltpu.make_async_remote_copy(
                src_ref=blocks.at[src, :, piece],
                dst_ref=blocks.at[dst, :, piece],
                send_sem=block_send_sem.at[2 * src + to - 1, i],
                recv_sem=block_recv_sem.at[dst, i],
                device_id=(conf_at(to), o),
                device_id_type=MESH,
            )
            for i, piece in enumerate(pieces)
        ]

    first_copies, second_copies, passed_copies = (
        block_copies(0, 1, 1),
        block_copies(0, 2, 2),
        block_copies(1, 2, 1),
    )

    def send_blocks():
        @pl.when(core == 1)
        def _():
            pl.semaphore_wait(barrier, jnp.where(last_x, 2, 4))
            tell_sibling()

        @pl.when(first_core)
        def _():
            pl.semaphore_wait(pair_sem, 1)

        for copy in first_copies:
            copy.start()

        @pl.when(jnp.logical_not(last_x))
        def _():
            for copy in second_copies:
                copy.start()

    send_early = b >= n_conf - 2
    pl.when(send_early)(send_blocks)

    def grid_wait(layer, number):
        slots = gath.at[pl.ds(layer * LAYER, number)]
        return pltpu.make_async_remote_copy(
            src_ref=slots,
            dst_ref=slots,
            send_sem=grid_send_sem,
            recv_sem=grid_recv_sem.at[layer],
            device_id=(conf_at(1), o),
            device_id_type=MESH,
        )

    def answer(layer):
        @pl.when(z < layer)
        def _():
            grid_wait(layer, LAYER).wait_recv()
            for t in range(LAYER):
                send_grid(layer * LAYER + t)

    loads[5].wait()
    loads[6].wait()
    dens = [dens_ref[:, j * LANES : (j + 1) * LANES].astype(F32) for j in range(TILES)]
    forward_rows(dens, stage, 0)
    excess = [(t * t - 1.0).astype(BF16).astype(F32) for t in dens]
    forward_rows(excess, stage, ROWS)
    de = forward_lanes(stage, w_ref)
    dr, di = de[:, :, :LANES], de[:, :, LANES:]
    spec_de[...] = jnp.concatenate([dr, dr + di, di - dr], axis=2)

    n_cls = con_ref.shape[0]
    for row in range(0, n_cls, ROWS):
        squares = []
        for j in range(TILES):
            tile = con_ref[row : row + ROWS, j * LANES : (j + 1) * LANES]
            squares.append((tile * tile).astype(BF16).astype(F32))
        forward_rows(squares, stage, row, -LOG2E * 2.0**-17, True)
    of_classes = forward_lanes(stage, w_ref)
    for k in range(HALF):
        high, low = split_in_two(of_classes[k])
        cols = slice(k * 2 * LANES, (k + 1) * 2 * LANES)
        class_spec[0:n_cls, cols] = high
        class_spec[n_cls:, cols] = low

    def visit(v):
        classes = blocks[v, :, half * LANES :].astype(F32)[0:ROWS, 0 : 2 * n_cls]
        column = lax.broadcasted_iota(jnp.int32, (ROWS, 2 * n_cls), 1) % n_cls
        picks = jnp.where(classes == column.astype(F32), 1.0, 0.0).astype(BF16)
        spec_q[...] = jnp.dot(picks, class_spec[...], preferred_element_type=F32)
        pairs = [blocks[v, :, j * LANES : (j + 1) * LANES].astype(F32) for j in range(half)]
        rows = [p[0:ROWS] for p in pairs] + [p[ROWS:] for p in pairs]
        forward_rows(rows, stage_f, 0, LOG2E * 2.0**-16, True)
        spec_f[...] = forward_lanes(stage_f, w_ref)
        part = ROWS // 2
        pair_products(spec_f, spec_q, spec_de, 0, part, lhs_a)
        inverse_lanes(lhs_a, w_ref, g_a)
        pair_products(spec_f, spec_q, spec_de, part, part, lhs_b)
        inverse_lanes(lhs_b, w_ref, g_b)
        scores(g_a, score_ref, v * ROWS, part)
        scores(g_b, score_ref, v * ROWS + part, part)

    def lw_copy(layer):
        return pltpu.make_async_remote_copy(
            src_ref=lw_ref,
            dst_ref=lw_ref,
            send_sem=lw_send_sem.at[layer],
            recv_sem=lw_recv_sem,
            device_id=(b, layer * LAYER + place),
            device_id_type=MESH,
        )

    def hub_of(layer):
        return n_hubs - 1 if layer <= n_layers // 2 else 0

    def hear(layers):
        for layer in layers:

            @pl.when(z == layer)
            def _():
                grid_wait(layer, LAYER - 1).wait_recv()

            @pl.when((z > layer) | ((z != layer) & (layer >= n_hubs)))
            def _():
                grid_wait(layer, LAYER).wait_recv()

    early = n_layers // 2

    def make_weights():
        last = (early + n_layers) // 2
        total = early_ref[...]
        for first, end in ((last, n_layers), (early, last)):
            hear(range(first, end))
            total = total + grid_weights(gath, first * LAYER, (end - first) * LAYER)
        lw_ref[...] = log2_or_far(total)
        for layer in range(n_hubs, n_layers):

            @pl.when(z == hub_of(layer))
            def _():
                lw_copy(layer).start()

    visit(0)
    pl.when(jnp.logical_not(send_early))(send_blocks)
    for layer in range(1, n_hubs):
        answer(layer)

    @pl.when(is_hub)
    def _():
        hear(range(early))
        early_ref[...] = grid_weights(gath, 0, early * LAYER)

    weights_at = jnp.where((x == 1) | (z > 0), 2, 3)
    sums_early = is_hub & (x == 1)

    def step(v, _):
        pl.when(is_hub & (weights_at == v))(make_weights)

        @pl.when(sums_early & (v == 2))
        def _():
            log_sums(score_ref, lw_ref, ms_ref, 0, 2)

        @pl.when(v < 3)
        def _():
            for i, piece in enumerate(pieces):
                pltpu.make_async_remote_copy(
                    src_ref=blocks.at[0, :, piece],
                    dst_ref=blocks.at[v, :, piece],
                    send_sem=block_send_sem.at[0, i],
                    recv_sem=block_recv_sem.at[v, i],
                    device_id=(conf_at(1), o),
                    device_id_type=MESH,
                ).wait_recv()
                pl.when((v == 1) & (x == 0))(passed_copies[i].start)
            visit(v)

        return 0

    lax.fori_loop(1, 4, step, 0)

    @pl.when(jnp.logical_not(is_hub))
    def _():
        pltpu.make_async_remote_copy(
            src_ref=lw_ref,
            dst_ref=lw_ref,
            send_sem=lw_send_sem.at[0],
            recv_sem=lw_recv_sem,
            device_id=(b, place),
            device_id_type=MESH,
        ).wait_recv()

    log_sums(score_ref, lw_ref, ms_ref, jnp.where(sums_early, 2, 0), 3)
    final = results(ms_ref)
    for v in range(3):
        out_ref[v] = final[v * ROWS : (v + 1) * ROWS, :]

    for layer in range(n_hubs, n_layers):

        @pl.when(z == hub_of(layer))
        def _():
            lw_copy(layer).wait_send()

    @pl.when(is_hub)
    def _():
        grid_wait(0, LAYER * n_hubs - 1).wait_send()

    @pl.when(jnp.logical_not(is_hub))
    def _():
        grid_wait(0, LAYER * n_hubs).wait_send()

    for copies, sent in (
        (first_copies, x >= 0),
        (second_copies, jnp.logical_not(last_x)),
        (passed_copies, x == 0),
    ):
        for copy in copies:
            pl.when(sent)(copy.wait_send)


def solution(mesh):
    n_conf, n_orient = mesh.shape["conf"], mesh.shape["orient"]
    w = lane_matrix()

    def per_device(*given):
        particles, defocus_class, densities, contrast, grid_shift, log_prior = given
        operands = [
            pltpu.with_memory_space_constraint(x, pltpu.HBM)
            for x in (
                defocus_class,
                particles,
                densities,
                contrast,
                grid_shift,
                log_prior,
                jnp.asarray(w),
            )
        ]
        return pl.pallas_call(
            functools.partial(kernel, n_conf, n_orient),
            out_shape=pltpu.VMEM((3, ROWS, ROWS), F32),
            in_specs=[pl.BlockSpec(memory_space=pltpu.HBM)] * 7,
            out_specs=pl.BlockSpec(memory_space=pltpu.VMEM),
            scratch_shapes=[
                pltpu.SMEM(defocus_class.shape, jnp.int32),
                pltpu.VMEM(particles.shape, BF16),
                pltpu.VMEM(densities.shape, BF16),
                pltpu.VMEM(contrast.shape, F32),
                pltpu.VMEM(grid_shift.shape, jnp.int32),
                pltpu.VMEM(log_prior.shape, F32),
                pltpu.VMEM(w.shape, BF16),
                pltpu.VMEM((3, 2 * ROWS, (TILES // 2 + 1) * LANES), BF16),
                pltpu.VMEM((2, LANES), F32),
                pltpu.VMEM((n_orient, 2, LANES), F32),
                pltpu.VMEM((HALF, 2 * ROWS, 2 * LANES), F32),
                pltpu.VMEM((HALF, ROWS, 2 * LANES), F32),
                pltpu.VMEM((HALF, ROWS, 2 * LANES), F32),
                pltpu.VMEM((ROWS, HALF * 2 * LANES), F32),
                pltpu.VMEM((HALF, 2 * ROWS, 3 * LANES), F32),
                pltpu.VMEM((HALF, ROWS * ROWS // 2, 4 * LANES), BF16),
                pltpu.VMEM((HALF, ROWS * ROWS // 2, 4 * LANES), BF16),
                pltpu.VMEM((HALF, ROWS * ROWS // 2, 2 * LANES), F32),
                pltpu.VMEM((HALF, ROWS * ROWS // 2, 2 * LANES), F32),
                pltpu.VMEM((3 * ROWS, TILES, ROWS, LANES), F32),
                pltpu.VMEM((2 * contrast.shape[0], HALF * 2 * LANES), BF16),
                pltpu.VMEM((TILES, LANES), F32),
                pltpu.VMEM((TILES, LANES), F32),
                pltpu.VMEM((3 * ROWS, 2 * ROWS, LANES), F32),
                pltpu.SemaphoreType.DMA((7,)),
                pltpu.SemaphoreType.DMA((4, 2)),
                pltpu.SemaphoreType.DMA((3, 2)),
                pltpu.SemaphoreType.DMA,
                pltpu.SemaphoreType.DMA((n_orient // LAYER,)),
                pltpu.SemaphoreType.DMA((n_orient // LAYER,)),
                pltpu.SemaphoreType.DMA,
                pltpu.SemaphoreType.REGULAR,
            ],
            compiler_params=pltpu.CompilerParams(
                collective_id=0, has_side_effects=True, vmem_limit_bytes=56 * 2**20
            ),
        )(*operands)

    placed = (
        P(("conf", "orient"), None),
        P(("conf", "orient")),
        P("conf", None),
        P(),
        P("orient"),
        P("orient"),
    )
    return jax.shard_map(
        per_device,
        mesh=mesh,
        in_specs=placed,
        out_specs=P(None, None, ("conf", "orient")),
        check_vma=False,
    )
```

```python
import functools
import math

import jax
import jax.numpy as jnp
import numpy as np
from jax import lax
from jax.experimental import pallas as pl
from jax.experimental.pallas import tpu as pltpu
from jax.sharding import PartitionSpec as P

SIDE = 64
ROWS = 8
LANES = 128
TILES = 32
HALF = TILES // 2 + 1
MESH = pl.DeviceIdType.MESH
F32 = jnp.float32
BF16 = jnp.bfloat16
FAR = -1e30
LOG2E = 1.0 / math.log(2.0)
LAYER = 4


def lane_matrix():
    yl, x = np.divmod(np.arange(LANES), SIDE)
    phase = 2.0 * np.pi * (np.outer(x, x) % SIDE) / SIDE + np.pi * (np.outer(yl, yl) % 2)
    c, s = np.cos(phase), np.sin(phase)
    full = np.block([[c, s], [-s, c]]).astype(np.float32)
    high = full.astype(jnp.bfloat16)
    low = (full - high.astype(np.float32)).astype(jnp.bfloat16)
    return np.concatenate([high, low], axis=0)


def turned(z, num, den):
    re, im = z
    eighth = (8 * num / den) % 8
    if eighth == 0:
        return z
    if eighth == 2:
        return (-im, re)
    angle = 2.0 * math.pi * num / den
    c, s = math.cos(angle), math.sin(angle)
    if eighth == 1:
        return ((re - im) * c, (re + im) * c)
    if eighth == 3:
        return ((re + im) * c, (im - re) * c)
    return (re * c - im * s, re * s + im * c)


def complex_dft(z):
    n = len(z)
    if n == 1:
        return z
    even, odd = complex_dft(z[0::2]), complex_dft(z[1::2])
    out = [None] * n
    for k in range(n // 2):
        (er, ei), (re, im) = even[k], odd[k]
        if 4 * k == n:
            out[k], out[k + n // 2] = (er - im, ei + re), (er + im, ei - re)
        else:
            tr, ti = turned((re, im), k, n)
            out[k], out[k + n // 2] = (er + tr, ei + ti), (er - tr, ei - ti)
    return out


def real_dft(x):
    n = len(x)
    if n == 2:
        return [(x[0] + x[1], None, False), (x[0] - x[1], None, False)]
    h, q = n // 2, n // 4
    a = [x[j] + x[j + h] for j in range(h)]
    b = [x[j] - x[j + h] for j in range(h)]
    out = [None] * (h + 1)
    out[0::2] = real_dft(a)
    z = complex_dft([turned((b[j], b[j + q]), j, n) for j in range(q)])
    for m in range(q):
        k = 4 * m + 1
        if k <= h:
            out[k] = (*z[m], False)
        else:
            out[n - k] = (*z[m], True)
    return out


def inverse_real_dft(spec):
    h = len(spec) - 1
    n = 2 * h
    if n == 2:
        return [spec[0][0] + spec[1][0], spec[0][0] - spec[1][0]]
    q = n // 4
    even = inverse_real_dft(spec[0::2])
    z = complex_dft([spec[k] if k <= h else spec[n - k] for k in range(1, n, 4)])
    out = [None] * n
    for j in range(q):
        tr, ti = turned(z[j], j, n)
        out[j], out[j + h] = even[j] + tr, even[j] - tr
        out[j + q], out[j + q + h] = even[j + q] - ti, even[j + q] + ti
    return out


def needs_conjugate(k):
    while k % 2 == 0:
        k //= 2
    return k % 4 == 3


def by_half(first, second):
    lane = lax.broadcasted_iota(jnp.int32, (ROWS, LANES), 1)
    return jnp.where(lane >= SIDE, F32(second), F32(first))


def forward_rows(tiles, dst, row, scale=1.0, for_products=False):
    spec = real_dft(tiles)
    rows = pl.ds(row, ROWS)
    zero = jnp.zeros((ROWS, LANES), F32)
    lane = lax.broadcasted_iota(jnp.int32, (ROWS, LANES), 1)
    for k, (re, im, conj) in enumerate(spec):
        if im is None:
            re = re if scale == 1.0 else re * scale
        if k == 0:
            nr, ni = re, zero
        elif k == HALF - 1:
            nr, ni = jnp.where(lane < SIDE, re, 0.0), jnp.where(lane < SIDE, 0.0, re)
        else:
            angle = 2.0 * math.pi * k / SIDE
            if for_products:
                h = math.cos(angle / 2.0) * 2.0 * scale
                c, v = F32(h * math.cos(angle / 2.0)), h * math.sin(angle / 2.0)
                s = by_half(-v, v)
            else:
                c, s = by_half(1.0, math.cos(angle)), by_half(0.0, math.sin(angle))
            if conj:
                nr, ni = re * c + im * s, re * s - im * c
            else:
                nr, ni = re * c - im * s, re * s + im * c
        dst[k, rows, 0:LANES] = nr
        dst[k, rows, LANES : 2 * LANES] = ni


def inverse_turn(k, re, im):
    if k == 0:
        return re, None
    if k == HALF - 1:
        lane = lax.broadcasted_iota(jnp.int32, (ROWS, LANES), 1)
        return jnp.where(lane < SIDE, re, -im), None
    t = math.tan(math.pi * k / SIDE)
    if needs_conjugate(k):
        return re - im * by_half(-t, t), re * by_half(t, -t) - im
    return re - im * by_half(-t, t), im + re * by_half(-t, t)


def split_in_two(x):
    high = x.astype(BF16)
    return high, (x - high.astype(F32)).astype(BF16)


def times_lane_matrix(high, low, w_ref):
    w_high, w_low = w_ref[0 : 2 * LANES, :], w_ref[2 * LANES :, :]
    return jnp.dot(
        jnp.concatenate([high, low, high], axis=1),
        jnp.concatenate([w_high, w_high, w_low], axis=0),
        preferred_element_type=F32,
    )


def forward_lanes(src, w_ref):
    tiles, rows, lanes = src.shape
    high, low = split_in_two(src[...].reshape(tiles * rows, lanes))
    return times_lane_matrix(high, low, w_ref).reshape(tiles, rows, lanes)


def grid_weights(gath, first, count):
    shift = gath[first : first + count, 0, :].astype(jnp.int32)
    weight = gath[first : first + count, 1, :]
    high = weight.astype(BF16).astype(F32)
    low = weight - high
    dy, dx = shift // SIDE, shift % SIDE
    place = dy % 2 * TILES + dy // 2
    row = lax.broadcasted_iota(jnp.int32, (SIDE, LANES), 0)
    lefts, rights = [], []
    for r in range(count):
        mine = row == place[r : r + 1, :]
        parts = [jnp.where(mine, x[r : r + 1, :], 0.0) for x in (high, low)]
        lefts.append(jnp.concatenate(parts, axis=0).astype(BF16))
        right = jnp.where(row == dx[r : r + 1, :], 1.0, 0.0).astype(BF16)
        rights.append(jnp.concatenate([right, right], axis=0))
    both = lax.dot_general(
        jnp.concatenate(lefts, axis=1),
        jnp.concatenate(rights, axis=1),
        (((1,), (1,)), ((), ())),
        preferred_element_type=F32,
    )
    total = both[0:SIDE] + both[SIDE:]
    lane = lax.broadcasted_iota(jnp.int32, (TILES, LANES), 1)
    return jnp.where(lane < SIDE, total[0:TILES], total[TILES:])


def log2_or_far(total):
    some = total > 0.0
    return jnp.where(some, jnp.log(jnp.where(some, total, 1.0)) / math.log(2.0), FAR)


def pair_products(f_ref, q_ref, de, first, count, lhs):
    for k in range(HALF):
        f, q = f_ref[k], q_ref[:, k * 2 * LANES : (k + 1) * 2 * LANES]
        fr, fi, qr, qi = f[:, :LANES], f[:, LANES:], q[:, :LANES], q[:, LANES:]
        fd, qd = fr - fi, qr - qi
        parts = []
        for c in range(first, first + count):
            d, e = de[k, c : c + 1, :], de[k, ROWS + c : ROWS + c + 1, :]
            dr, ds, dm = (d[:, i * LANES : (i + 1) * LANES] for i in range(3))
            er, es, em = (e[:, i * LANES : (i + 1) * LANES] for i in range(3))
            shared = dr * fd + er * qd
            re = shared + (fi * ds + qi * es)
            im = shared + (fr * dm + qr * em)
            parts.append(jnp.concatenate([re, im], axis=1))
        for i in range(0, count, 2):
            high, low = split_in_two(jnp.concatenate(parts[i : i + 2], axis=0))
            rows = pl.ds(i * ROWS, 2 * ROWS)
            lhs[k, rows, 0 : 2 * LANES] = high
            lhs[k, rows, 2 * LANES :] = low


def inverse_lanes(lhs, w_ref, dst):
    rows = lhs.shape[1]
    x = lhs[...].reshape(HALF * rows, 4 * LANES)
    out = times_lane_matrix(x[:, : 2 * LANES], x[:, 2 * LANES :], w_ref)
    dst[...] = out.reshape(HALF, rows, 2 * LANES)


def scores(g_ref, score_ref, first, count):
    for i in range(count):
        rows = pl.ds(i * ROWS, ROWS)
        spec = [
            inverse_turn(k, g_ref[k, rows, 0:LANES], g_ref[k, rows, LANES : 2 * LANES])
            for k in range(HALF)
        ]
        for j, value in enumerate(inverse_real_dft(spec)):
            score_ref[first + i, j] = value


def tree(join, values):
    while len(values) > 1:
        values = [join(*values[i : i + 2]) for i in range(0, len(values) - 1, 2)] + (
            [values[-1]] if len(values) % 2 else []
        )
    return values[0]


def log_sums(score_ref, lw_ref, ms_ref, first, end):
    def one_visit(v, _):
        for p in range(ROWS):
            i = v * ROWS + p
            value = [score_ref[i, j] + lw_ref[j : j + 1, :] for j in range(TILES)]
            top = tree(jnp.maximum, value)
            total = tree(jnp.add, [jnp.exp2(v - top) for v in value])
            ms_ref[i, 0:ROWS, :] = top
            ms_ref[i, ROWS : 2 * ROWS, :] = total
        return 0

    lax.fori_loop(first, end, one_visit, 0)


def results(ms_ref):
    lane = lax.broadcasted_iota(jnp.int32, (ROWS, LANES), 1)
    tops = jnp.zeros((ROWS, LANES), F32)
    sums = jnp.ones((ROWS, LANES), F32)
    for i in range(ms_ref.shape[0]):
        top, total = ms_ref[i, 0:ROWS, :], ms_ref[i, ROWS : 2 * ROWS, :]
        highest = jnp.max(top, axis=1, keepdims=True)
        summed = jnp.sum(total * jnp.exp2(top - highest), axis=1, keepdims=True)
        tops = jnp.where(lane == i, highest, tops)
        sums = jnp.where(lane == i, summed, sums)
    return (tops * math.log(2.0) + jnp.log(sums)).T


def kernel(
    n_conf,
    n_orient,
    cls_hbm,
    part_hbm,
    dens_hbm,
    con_hbm,
    shift_hbm,
    prior_hbm,
    w_hbm,
    out_ref,
    cls_ref,
    part_ref,
    dens_ref,
    con_ref,
    shift_ref,
    prior_ref,
    w_ref,
    blocks,
    msg,
    gath,
    stage,
    stage_f,
    spec_f,
    spec_q,
    spec_de,
    lhs_a,
    lhs_b,
    g_a,
    g_b,
    score_ref,
    class_spec,
    early_ref,
    lw_ref,
    ms_ref,
    in_sem,
    block_send_sem,
    block_recv_sem,
    grid_send_sem,
    grid_recv_sem,
    lw_send_sem,
    lw_recv_sem,
    pair_sem,
):
    b = lax.axis_index("conf")
    o = lax.axis_index("orient")
    n_layers = n_orient // LAYER
    n_hubs = max(n_layers // 4, 1)
    z = o // LAYER
    place = lax.rem(o, LAYER)
    core = lax.rem(o, 2)
    first_core = core == 0
    is_hub = z < n_hubs

    def conf_at(offset):
        return lax.rem(b + offset + n_conf, n_conf)

    barrier = pltpu.get_barrier_semaphore()

    def greet(conf, orient):
        pl.semaphore_signal(
            barrier, inc=1, device_id=(conf, orient), device_id_type=MESH
        )

    def tell_sibling():
        pl.semaphore_signal(
            pair_sem, inc=1, device_id=(b, o + 1 - 2 * core), device_id_type=MESH
        )

    x = lax.rem(b, n_conf // 2)
    last_x = x == n_conf // 2 - 1

    @pl.when(x != 1)
    def _():
        greet(conf_at(-2), o - core + 1)

    greet(conf_at(-1), o - core + 1)

    loads = []
    for i, (src, dst) in enumerate(
        (
            (shift_hbm, shift_ref),
            (prior_hbm, prior_ref),
            (cls_hbm, cls_ref),
            (part_hbm, part_ref),
            (con_hbm, con_ref),
            (dens_hbm, dens_ref),
            (w_hbm, w_ref),
        )
    ):
        loads.append(pltpu.make_async_copy(src, dst, in_sem.at[i]))
        loads[-1].start()

    @pl.when(core == 1)
    def _():
        greet(b, o - 1)

    @pl.when(is_hub)
    def _():
        for t in range(2, LAYER, 2):
            greet(b, z * LAYER + lax.rem(place - core + t, LAYER))

        def above(t, _):
            greet(b, 2 * t)
            return 0

        lax.fori_loop((z + 1) * (LAYER // 2), n_orient // 2, above, 0)

    count = shift_ref.shape[0]
    loads[0].wait()
    loads[1].wait()
    msg[...] = jnp.zeros_like(msg)
    msg[0:1, 0:count] = shift_ref[...].astype(F32).reshape(1, count)
    msg[1:2, 0:count] = jnp.exp(prior_ref[...]).reshape(1, count)
    gath[o] = msg[...]

    hubs_below = LAYER * jnp.minimum(z, n_hubs)

    @pl.when(first_core)
    def _():
        pl.semaphore_wait(barrier, 1 + hubs_below + jnp.where(is_hub, LAYER - 2, 0))
        tell_sibling()

    @pl.when(core == 1)
    def _():
        pl.semaphore_wait(pair_sem, 1)

    def send_grid(to):
        pltpu.make_async_remote_copy(
            src_ref=msg,
            dst_ref=gath.at[o],
            send_sem=grid_send_sem,
            recv_sem=grid_recv_sem.at[z],
            device_id=(b, to),
            device_id_type=MESH,
        ).start()

    def send_below(t, _):
        send_grid(t)
        return 0

    def send_beside(t, _):
        send_grid(z * LAYER + lax.rem(place + t, LAYER))
        return 0

    lax.fori_loop(0, hubs_below, send_below, 0)
    lax.fori_loop(1, jnp.where(is_hub, LAYER, 1), send_beside, 0)

    for load in loads[2:5]:
        load.wait()
    row = lax.broadcasted_iota(jnp.int32, (ROWS, LANES), 0)
    cls = jnp.zeros((ROWS, LANES), jnp.int32)
    for i in range(ROWS):
        cls = jnp.where(row == i, cls_ref[i], cls)

    picked = [cls == k for k in range(con_ref.shape[0])]

    def envelope(j):
        out = jnp.zeros((ROWS, LANES), F32)
        for k, mask in enumerate(picked):
            out = jnp.where(mask, con_ref[k : k + 1, j * LANES : (j + 1) * LANES], out)
        return out

    half = TILES // 2
    for j in range(half):
        pair = [
            part_ref[:, t * LANES : (t + 1) * LANES].astype(F32) * envelope(t)
            for t in (j, j + half)
        ]
        blocks[0, :, j * LANES : (j + 1) * LANES] = jnp.concatenate(pair, axis=0).astype(BF16)
    blocks[0, :, half * LANES :] = jnp.concatenate([cls, cls], axis=0).astype(F32).astype(BF16)

    middle = half // 2 * LANES
    pieces = (pl.ds(0, middle), pl.ds(middle, blocks.shape[2] - middle))

    def block_copies(src, dst, to):
        return [
            pltpu.make_async_remote_copy(
                src_ref=blocks.at[src, :, piece],
                dst_ref=blocks.at[dst, :, piece],
                send_sem=block_send_sem.at[2 * src + to - 1, i],
                recv_sem=block_recv_sem.at[dst, i],
                device_id=(conf_at(to), o),
                device_id_type=MESH,
            )
            for i, piece in enumerate(pieces)
        ]

    first_copies, second_copies, passed_copies = (
        block_copies(0, 1, 1),
        block_copies(0, 2, 2),
        block_copies(1, 2, 1),
    )

    far = b == n_conf - 2

    def send_blocks():
        @pl.when(core == 1)
        def _():
            pl.semaphore_wait(barrier, jnp.where(last_x, 2, 4))
            tell_sibling()

        @pl.when(first_core)
        def _():
            pl.semaphore_wait(pair_sem, 1)

        for copy in first_copies:
            copy.start()

        @pl.when(jnp.logical_not(last_x | far))
        def _():
            for copy in second_copies:
                copy.start()

    send_early = x >= n_conf // 2 - 2
    pl.when(send_early)(send_blocks)

    def grid_wait(layer, number):
        slots = gath.at[pl.ds(layer * LAYER, number)]
        return pltpu.make_async_remote_copy(
            src_ref=slots,
            dst_ref=slots,
            send_sem=grid_send_sem,
            recv_sem=grid_recv_sem.at[layer],
            device_id=(conf_at(1), o),
            device_id_type=MESH,
        )

    def answer(layer):
        @pl.when(z < layer)
        def _():
            grid_wait(layer, LAYER).wait_recv()
            for t in range(LAYER):
                send_grid(layer * LAYER + t)

    loads[5].wait()
    loads[6].wait()
    dens = [dens_ref[:, j * LANES : (j + 1) * LANES].astype(F32) for j in range(TILES)]
    forward_rows(dens, stage, 0)
    excess = [(t * t - 1.0).astype(BF16).astype(F32) for t in dens]
    forward_rows(excess, stage, ROWS)
    de = forward_lanes(stage, w_ref)
    dr, di = de[:, :, :LANES], de[:, :, LANES:]
    spec_de[...] = jnp.concatenate([dr, dr + di, di - dr], axis=2)

    n_cls = con_ref.shape[0]
    for row in range(0, n_cls, ROWS):
        squares = []
        for j in range(TILES):
            tile = con_ref[row : row + ROWS, j * LANES : (j + 1) * LANES]
            squares.append((tile * tile).astype(BF16).astype(F32))
        forward_rows(squares, stage, row, -LOG2E * 2.0**-17, True)
    of_classes = forward_lanes(stage, w_ref)
    for k in range(HALF):
        high, low = split_in_two(of_classes[k])
        cols = slice(k * 2 * LANES, (k + 1) * 2 * LANES)
        class_spec[0:n_cls, cols] = high
        class_spec[n_cls:, cols] = low

    def visit(v):
        classes = blocks[v, :, half * LANES :].astype(F32)[0:ROWS, 0 : 2 * n_cls]
        column = lax.broadcasted_iota(jnp.int32, (ROWS, 2 * n_cls), 1) % n_cls
        picks = jnp.where(classes == column.astype(F32), 1.0, 0.0).astype(BF16)
        spec_q[...] = jnp.dot(picks, class_spec[...], preferred_element_type=F32)
        pairs = [blocks[v, :, j * LANES : (j + 1) * LANES].astype(F32) for j in range(half)]
        rows = [p[0:ROWS] for p in pairs] + [p[ROWS:] for p in pairs]
        forward_rows(rows, stage_f, 0, LOG2E * 2.0**-16, True)
        spec_f[...] = forward_lanes(stage_f, w_ref)
        part = ROWS // 2
        pair_products(spec_f, spec_q, spec_de, 0, part, lhs_a)
        inverse_lanes(lhs_a, w_ref, g_a)
        pair_products(spec_f, spec_q, spec_de, part, part, lhs_b)
        inverse_lanes(lhs_b, w_ref, g_b)
        scores(g_a, score_ref, v * ROWS, part)
        scores(g_b, score_ref, v * ROWS + part, part)

    def lw_copy(layer):
        return pltpu.make_async_remote_copy(
            src_ref=lw_ref,
            dst_ref=lw_ref,
            send_sem=lw_send_sem.at[layer],
            recv_sem=lw_recv_sem,
            device_id=(b, layer * LAYER + place),
            device_id_type=MESH,
        )

    def hub_of(layer):
        return n_hubs - 1 if layer <= n_layers // 2 else 0

    def hear(layers):
        for layer in layers:

            @pl.when(z == layer)
            def _():
                grid_wait(layer, LAYER - 1).wait_recv()

            @pl.when((z > layer) | ((z != layer) & (layer >= n_hubs)))
            def _():
                grid_wait(layer, LAYER).wait_recv()

    early = n_layers // 2

    def make_weights():
        last = (early + n_layers) // 2
        total = early_ref[...]
        for first, end in ((last, n_layers), (early, last)):
            hear(range(first, end))
            total = total + grid_weights(gath, first * LAYER, (end - first) * LAYER)
        lw_ref[...] = log2_or_far(total)
        for layer in range(n_hubs, n_layers):

            @pl.when(z == hub_of(layer))
            def _():
                lw_copy(layer).start()

    visit(0)
    pl.when(jnp.logical_not(send_early))(send_blocks)

    @pl.when(far)
    def _():
        for copy in second_copies:
            copy.start()

    for layer in range(1, n_hubs):
        answer(layer)

    @pl.when(is_hub)
    def _():
        hear(range(early))
        early_ref[...] = grid_weights(gath, 0, early * LAYER)

    starts_first = (b == 0) & (place < 2)
    weights_at = jnp.where((x == 1) | (z > 0), 2, 3) - jnp.where(starts_first, 1, 0)
    sums_early = is_hub & (x == 1)

    def hear_block(v):
        for i, piece in enumerate(pieces):
            pltpu.make_async_remote_copy(
                src_ref=blocks.at[0, :, piece],
                dst_ref=blocks.at[v, :, piece],
                send_sem=block_send_sem.at[0, i],
                recv_sem=block_recv_sem.at[v, i],
                device_id=(conf_at(1), o),
                device_id_type=MESH,
            ).wait_recv()
            if v == 1:
                pl.when(x == 0)(passed_copies[i].start)

    def step(v, _):
        pl.when(v == 1)(lambda: hear_block(1))
        pl.when(is_hub & (weights_at == v))(make_weights)

        @pl.when(sums_early & (v == 2))
        def _():
            log_sums(score_ref, lw_ref, ms_ref, 0, 2)

        pl.when(v == 2)(lambda: hear_block(2))
        pl.when(v < 3)(lambda: visit(v))
        return 0

    lax.fori_loop(1, 4, step, 0)

    @pl.when(jnp.logical_not(is_hub))
    def _():
        pltpu.make_async_remote_copy(
            src_ref=lw_ref,
            dst_ref=lw_ref,
            send_sem=lw_send_sem.at[0],
            recv_sem=lw_recv_sem,
            device_id=(b, place),
            device_id_type=MESH,
        ).wait_recv()

    log_sums(score_ref, lw_ref, ms_ref, jnp.where(sums_early, 2, 0), 3)
    final = results(ms_ref)
    for v in range(3):
        out_ref[v] = final[v * ROWS : (v + 1) * ROWS, :]

    for layer in range(n_hubs, n_layers):

        @pl.when(z == hub_of(layer))
        def _():
            lw_copy(layer).wait_send()

    @pl.when(is_hub)
    def _():
        grid_wait(0, LAYER * n_hubs - 1).wait_send()

    @pl.when(jnp.logical_not(is_hub))
    def _():
        grid_wait(0, LAYER * n_hubs).wait_send()

    for copies, sent in (
        (first_copies, x >= 0),
        (second_copies, jnp.logical_not(last_x)),
        (passed_copies, x == 0),
    ):
        for copy in copies:
            pl.when(sent)(copy.wait_send)


def solution(mesh):
    n_conf, n_orient = mesh.shape["conf"], mesh.shape["orient"]
    w = lane_matrix()

    def per_device(*given):
        particles, defocus_class, densities, contrast, grid_shift, log_prior = given
        operands = [
            pltpu.with_memory_space_constraint(x, pltpu.HBM)
            for x in (
                defocus_class,
                particles,
                densities,
                contrast,
                grid_shift,
                log_prior,
                jnp.asarray(w),
            )
        ]
        return pl.pallas_call(
            functools.partial(kernel, n_conf, n_orient),
            out_shape=pltpu.VMEM((3, ROWS, ROWS), F32),
            in_specs=[pl.BlockSpec(memory_space=pltpu.HBM)] * 7,
            out_specs=pl.BlockSpec(memory_space=pltpu.VMEM),
            scratch_shapes=[
                pltpu.SMEM(defocus_class.shape, jnp.int32),
                pltpu.VMEM(particles.shape, BF16),
                pltpu.VMEM(densities.shape, BF16),
                pltpu.VMEM(contrast.shape, F32),
                pltpu.VMEM(grid_shift.shape, jnp.int32),
                pltpu.VMEM(log_prior.shape, F32),
                pltpu.VMEM(w.shape, BF16),
                pltpu.VMEM((3, 2 * ROWS, (TILES // 2 + 1) * LANES), BF16),
                pltpu.VMEM((2, LANES), F32),
                pltpu.VMEM((n_orient, 2, LANES), F32),
                pltpu.VMEM((HALF, 2 * ROWS, 2 * LANES), F32),
                pltpu.VMEM((HALF, ROWS, 2 * LANES), F32),
                pltpu.VMEM((HALF, ROWS, 2 * LANES), F32),
                pltpu.VMEM((ROWS, HALF * 2 * LANES), F32),
                pltpu.VMEM((HALF, 2 * ROWS, 3 * LANES), F32),
                pltpu.VMEM((HALF, ROWS * ROWS // 2, 4 * LANES), BF16),
                pltpu.VMEM((HALF, ROWS * ROWS // 2, 4 * LANES), BF16),
                pltpu.VMEM((HALF, ROWS * ROWS // 2, 2 * LANES), F32),
                pltpu.VMEM((HALF, ROWS * ROWS // 2, 2 * LANES), F32),
                pltpu.VMEM((3 * ROWS, TILES, ROWS, LANES), F32),
                pltpu.VMEM((2 * contrast.shape[0], HALF * 2 * LANES), BF16),
                pltpu.VMEM((TILES, LANES), F32),
                pltpu.VMEM((TILES, LANES), F32),
                pltpu.VMEM((3 * ROWS, 2 * ROWS, LANES), F32),
                pltpu.SemaphoreType.DMA((7,)),
                pltpu.SemaphoreType.DMA((4, 2)),
                pltpu.SemaphoreType.DMA((3, 2)),
                pltpu.SemaphoreType.DMA,
                pltpu.SemaphoreType.DMA((n_orient // LAYER,)),
                pltpu.SemaphoreType.DMA((n_orient // LAYER,)),
                pltpu.SemaphoreType.DMA,
                pltpu.SemaphoreType.REGULAR,
            ],
            compiler_params=pltpu.CompilerParams(
                collective_id=0, has_side_effects=True, vmem_limit_bytes=56 * 2**20
            ),
        )(*operands)

    placed = (
        P(("conf", "orient"), None),
        P(("conf", "orient")),
        P("conf", None),
        P(),
        P("orient"),
        P("orient"),
    )
    return jax.shard_map(
        per_device,
        mesh=mesh,
        in_specs=placed,
        out_specs=P(None, None, ("conf", "orient")),
        check_vma=False,
    )
```

```python
import functools
import math

import jax
import jax.numpy as jnp
import numpy as np
from jax import lax
from jax.experimental import pallas as pl
from jax.experimental.pallas import tpu as pltpu
from jax.sharding import PartitionSpec as P

SIDE = 64
ROWS = 8
LANES = 128
TILES = 32
HALF = TILES // 2 + 1
MESH = pl.DeviceIdType.MESH
F32 = jnp.float32
BF16 = jnp.bfloat16
FAR = -1e30
LOG2E = 1.0 / math.log(2.0)
LAYER = 4


def lane_matrix():
    yl, x = np.divmod(np.arange(LANES), SIDE)
    phase = 2.0 * np.pi * (np.outer(x, x) % SIDE) / SIDE + np.pi * (np.outer(yl, yl) % 2)
    c, s = np.cos(phase), np.sin(phase)
    full = np.block([[c, s], [-s, c]]).astype(np.float32)
    high = full.astype(jnp.bfloat16)
    low = (full - high.astype(np.float32)).astype(jnp.bfloat16)
    return np.concatenate([high, low], axis=0)


def turned(z, num, den):
    re, im = z
    eighth = (8 * num / den) % 8
    if eighth == 0:
        return z
    if eighth == 2:
        return (-im, re)
    angle = 2.0 * math.pi * num / den
    c, s = math.cos(angle), math.sin(angle)
    if eighth == 1:
        return ((re - im) * c, (re + im) * c)
    if eighth == 3:
        return ((re + im) * c, (im - re) * c)
    return (re * c - im * s, re * s + im * c)


def complex_dft(z):
    n = len(z)
    if n == 1:
        return z
    even, odd = complex_dft(z[0::2]), complex_dft(z[1::2])
    out = [None] * n
    for k in range(n // 2):
        (er, ei), (re, im) = even[k], odd[k]
        if 4 * k == n:
            out[k], out[k + n // 2] = (er - im, ei + re), (er + im, ei - re)
        else:
            tr, ti = turned((re, im), k, n)
            out[k], out[k + n // 2] = (er + tr, ei + ti), (er - tr, ei - ti)
    return out


def real_dft(x):
    n = len(x)
    if n == 2:
        return [(x[0] + x[1], None, False), (x[0] - x[1], None, False)]
    h, q = n // 2, n // 4
    a = [x[j] + x[j + h] for j in range(h)]
    b = [x[j] - x[j + h] for j in range(h)]
    out = [None] * (h + 1)
    out[0::2] = real_dft(a)
    z = complex_dft([turned((b[j], b[j + q]), j, n) for j in range(q)])
    for m in range(q):
        k = 4 * m + 1
        if k <= h:
            out[k] = (*z[m], False)
        else:
            out[n - k] = (*z[m], True)
    return out


def inverse_real_dft(spec):
    h = len(spec) - 1
    n = 2 * h
    if n == 2:
        return [spec[0][0] + spec[1][0], spec[0][0] - spec[1][0]]
    q = n // 4
    even = inverse_real_dft(spec[0::2])
    z = complex_dft([spec[k] if k <= h else spec[n - k] for k in range(1, n, 4)])
    out = [None] * n
    for j in range(q):
        tr, ti = turned(z[j], j, n)
        out[j], out[j + h] = even[j] + tr, even[j] - tr
        out[j + q], out[j + q + h] = even[j + q] - ti, even[j + q] + ti
    return out


def needs_conjugate(k):
    while k % 2 == 0:
        k //= 2
    return k % 4 == 3


def by_half(first, second):
    lane = lax.broadcasted_iota(jnp.int32, (ROWS, LANES), 1)
    return jnp.where(lane >= SIDE, F32(second), F32(first))


def forward_rows(tiles, dst, row, scale=1.0, for_products=False):
    spec = real_dft(tiles)
    rows = pl.ds(row, ROWS)
    zero = jnp.zeros((ROWS, LANES), F32)
    lane = lax.broadcasted_iota(jnp.int32, (ROWS, LANES), 1)
    for k, (re, im, conj) in enumerate(spec):
        if im is None:
            re = re if scale == 1.0 else re * scale
        if k == 0:
            nr, ni = re, zero
        elif k == HALF - 1:
            nr, ni = jnp.where(lane < SIDE, re, 0.0), jnp.where(lane < SIDE, 0.0, re)
        else:
            angle = 2.0 * math.pi * k / SIDE
            if for_products:
                h = math.cos(angle / 2.0) * 2.0 * scale
                c, v = F32(h * math.cos(angle / 2.0)), h * math.sin(angle / 2.0)
                s = by_half(-v, v)
            else:
                c, s = by_half(1.0, math.cos(angle)), by_half(0.0, math.sin(angle))
            if conj:
                nr, ni = re * c + im * s, re * s - im * c
            else:
                nr, ni = re * c - im * s, re * s + im * c
        dst[k, rows, 0:LANES] = nr
        dst[k, rows, LANES : 2 * LANES] = ni


def inverse_turn(k, re, im):
    if k == 0:
        return re, None
    if k == HALF - 1:
        lane = lax.broadcasted_iota(jnp.int32, (ROWS, LANES), 1)
        return jnp.where(lane < SIDE, re, -im), None
    t = math.tan(math.pi * k / SIDE)
    if needs_conjugate(k):
        return re - im * by_half(-t, t), re * by_half(t, -t) - im
    return re - im * by_half(-t, t), im + re * by_half(-t, t)


def split_in_two(x):
    high = x.astype(BF16)
    return high, (x - high.astype(F32)).astype(BF16)


def times_lane_matrix(high, low, w_ref):
    w_high, w_low = w_ref[0 : 2 * LANES, :], w_ref[2 * LANES :, :]
    return jnp.dot(
        jnp.concatenate([high, low, high], axis=1),
        jnp.concatenate([w_high, w_high, w_low], axis=0),
        preferred_element_type=F32,
    )


def forward_lanes(src, w_ref):
    tiles, rows, lanes = src.shape
    high, low = split_in_two(src[...].reshape(tiles * rows, lanes))
    return times_lane_matrix(high, low, w_ref).reshape(tiles, rows, lanes)


def grid_weights(gath, first, count):
    shift = gath[first : first + count, 0, :].astype(jnp.int32)
    weight = gath[first : first + count, 1, :]
    high = weight.astype(BF16).astype(F32)
    low = weight - high
    dy, dx = shift // SIDE, shift % SIDE
    place = dy % 2 * TILES + dy // 2
    row = lax.broadcasted_iota(jnp.int32, (SIDE, LANES), 0)
    lefts, rights = [], []
    for r in range(count):
        mine = row == place[r : r + 1, :]
        parts = [jnp.where(mine, x[r : r + 1, :], 0.0) for x in (high, low)]
        lefts.append(jnp.concatenate(parts, axis=0).astype(BF16))
        right = jnp.where(row == dx[r : r + 1, :], 1.0, 0.0).astype(BF16)
        rights.append(jnp.concatenate([right, right], axis=0))
    both = lax.dot_general(
        jnp.concatenate(lefts, axis=1),
        jnp.concatenate(rights, axis=1),
        (((1,), (1,)), ((), ())),
        preferred_element_type=F32,
    )
    total = both[0:SIDE] + both[SIDE:]
    lane = lax.broadcasted_iota(jnp.int32, (TILES, LANES), 1)
    return jnp.where(lane < SIDE, total[0:TILES], total[TILES:])


def log2_or_far(total):
    some = total > 0.0
    return jnp.where(some, jnp.log(jnp.where(some, total, 1.0)) / math.log(2.0), FAR)


def pair_products(f_ref, q_ref, de, first, count, lhs):
    for k in range(HALF):
        f, q = f_ref[k], q_ref[:, k * 2 * LANES : (k + 1) * 2 * LANES]
        fr, fi, qr, qi = f[:, :LANES], f[:, LANES:], q[:, :LANES], q[:, LANES:]
        fd, qd = fr - fi, qr - qi
        parts = []
        for c in range(first, first + count):
            d, e = de[k, c : c + 1, :], de[k, ROWS + c : ROWS + c + 1, :]
            dr, ds, dm = (d[:, i * LANES : (i + 1) * LANES] for i in range(3))
            er, es, em = (e[:, i * LANES : (i + 1) * LANES] for i in range(3))
            shared = dr * fd + er * qd
            re = shared + (fi * ds + qi * es)
            im = shared + (fr * dm + qr * em)
            parts.append(jnp.concatenate([re, im], axis=1))
        for i in range(0, count, 2):
            high, low = split_in_two(jnp.concatenate(parts[i : i + 2], axis=0))
            rows = pl.ds(i * ROWS, 2 * ROWS)
            lhs[k, rows, 0 : 2 * LANES] = high
            lhs[k, rows, 2 * LANES :] = low


def inverse_lanes(lhs, w_ref, dst):
    rows = lhs.shape[1]
    x = lhs[...].reshape(HALF * rows, 4 * LANES)
    out = times_lane_matrix(x[:, : 2 * LANES], x[:, 2 * LANES :], w_ref)
    dst[...] = out.reshape(HALF, rows, 2 * LANES)


def scores(g_ref, score_ref, first, count):
    for i in range(count):
        rows = pl.ds(i * ROWS, ROWS)
        spec = [
            inverse_turn(k, g_ref[k, rows, 0:LANES], g_ref[k, rows, LANES : 2 * LANES])
            for k in range(HALF)
        ]
        for j, value in enumerate(inverse_real_dft(spec)):
            score_ref[first + i, j] = value


def tree(join, values):
    while len(values) > 1:
        values = [join(*values[i : i + 2]) for i in range(0, len(values) - 1, 2)] + (
            [values[-1]] if len(values) % 2 else []
        )
    return values[0]


def log_sums(score_ref, lw_ref, ms_ref, first, end):
    def one_visit(v, _):
        for p in range(ROWS):
            i = v * ROWS + p
            value = [score_ref[i, j] + lw_ref[j : j + 1, :] for j in range(TILES)]
            top = tree(jnp.maximum, value)
            total = tree(jnp.add, [jnp.exp2(v - top) for v in value])
            ms_ref[i, 0:ROWS, :] = top
            ms_ref[i, ROWS : 2 * ROWS, :] = total
        return 0

    lax.fori_loop(first, end, one_visit, 0)


def results(ms_ref):
    lane = lax.broadcasted_iota(jnp.int32, (ROWS, LANES), 1)
    tops = jnp.zeros((ROWS, LANES), F32)
    sums = jnp.ones((ROWS, LANES), F32)
    for i in range(ms_ref.shape[0]):
        top, total = ms_ref[i, 0:ROWS, :], ms_ref[i, ROWS : 2 * ROWS, :]
        highest = jnp.max(top, axis=1, keepdims=True)
        summed = jnp.sum(total * jnp.exp2(top - highest), axis=1, keepdims=True)
        tops = jnp.where(lane == i, highest, tops)
        sums = jnp.where(lane == i, summed, sums)
    return (tops * math.log(2.0) + jnp.log(sums)).T


def kernel(
    n_conf,
    n_orient,
    cls_hbm,
    part_hbm,
    dens_hbm,
    con_hbm,
    shift_hbm,
    prior_hbm,
    w_hbm,
    out_ref,
    cls_ref,
    part_ref,
    dens_ref,
    con_ref,
    shift_ref,
    prior_ref,
    w_ref,
    blocks,
    msg,
    gath,
    stage,
    stage_f,
    spec_f,
    spec_q,
    spec_de,
    lhs_a,
    lhs_b,
    g_a,
    g_b,
    score_ref,
    class_spec,
    early_ref,
    lw_ref,
    ms_ref,
    in_sem,
    block_send_sem,
    block_recv_sem,
    grid_send_sem,
    grid_recv_sem,
    lw_send_sem,
    lw_recv_sem,
    pair_sem,
):
    b = lax.axis_index("conf")
    o = lax.axis_index("orient")
    n_layers = n_orient // LAYER
    n_hubs = max(n_layers // 4, 1)
    z = o // LAYER
    place = lax.rem(o, LAYER)
    core = lax.rem(o, 2)
    first_core = core == 0
    is_hub = z < n_hubs

    def conf_at(offset):
        return lax.rem(b + offset + n_conf, n_conf)

    barrier = pltpu.get_barrier_semaphore()

    def greet(conf, orient):
        pl.semaphore_signal(
            barrier, inc=1, device_id=(conf, orient), device_id_type=MESH
        )

    def tell_sibling():
        pl.semaphore_signal(
            pair_sem, inc=1, device_id=(b, o + 1 - 2 * core), device_id_type=MESH
        )

    x = lax.rem(b, n_conf // 2)
    last_x = x == n_conf // 2 - 1

    @pl.when(x != 1)
    def _():
        greet(conf_at(-2), o - core + 1)

    greet(conf_at(-1), o - core + 1)

    loads = []
    for i, (src, dst) in enumerate(
        (
            (shift_hbm, shift_ref),
            (prior_hbm, prior_ref),
            (cls_hbm, cls_ref),
            (part_hbm, part_ref),
            (con_hbm, con_ref),
            (dens_hbm, dens_ref),
            (w_hbm, w_ref),
        )
    ):
        loads.append(pltpu.make_async_copy(src, dst, in_sem.at[i]))
        loads[-1].start()

    greet(b, o + 1 - 2 * core)

    @pl.when(is_hub)
    def _():
        for t in range(2, LAYER, 2):
            greet(b, z * LAYER + lax.rem(place - core + t, LAYER))

        def above(t, _):
            greet(b, 2 * t)
            return 0

        lax.fori_loop((z + 1) * (LAYER // 2), n_orient // 2, above, 0)

    count = shift_ref.shape[0]
    loads[0].wait()
    loads[1].wait()
    msg[...] = jnp.zeros_like(msg)
    msg[0:1, 0:count] = shift_ref[...].astype(F32).reshape(1, count)
    msg[1:2, 0:count] = jnp.exp(prior_ref[...]).reshape(1, count)
    gath[o] = msg[...]

    half = TILES // 2

    def prepare_block():
        for load in loads[2:5]:
            load.wait()
        row = lax.broadcasted_iota(jnp.int32, (ROWS, LANES), 0)
        cls = jnp.zeros((ROWS, LANES), jnp.int32)
        for i in range(ROWS):
            cls = jnp.where(row == i, cls_ref[i], cls)

        picked = [cls == k for k in range(con_ref.shape[0])]

        def envelope(j):
            out = jnp.zeros((ROWS, LANES), F32)
            for k, mask in enumerate(picked):
                out = jnp.where(mask, con_ref[k : k + 1, j * LANES : (j + 1) * LANES], out)
            return out

        for j in range(half):
            pair = [
                part_ref[:, t * LANES : (t + 1) * LANES].astype(F32) * envelope(t)
                for t in (j, j + half)
            ]
            blocks[0, :, j * LANES : (j + 1) * LANES] = jnp.concatenate(pair, axis=0).astype(BF16)
        blocks[0, :, half * LANES :] = jnp.concatenate([cls, cls], axis=0).astype(F32).astype(BF16)

    middle = half // 2 * LANES
    pieces = (pl.ds(0, middle), pl.ds(middle, blocks.shape[2] - middle))

    def block_copies(src, dst, to):
        return [
            pltpu.make_async_remote_copy(
                src_ref=blocks.at[src, :, piece],
                dst_ref=blocks.at[dst, :, piece],
                send_sem=block_send_sem.at[2 * src + to - 1, i],
                recv_sem=block_recv_sem.at[dst, i],
                device_id=(conf_at(to), o),
                device_id_type=MESH,
            )
            for i, piece in enumerate(pieces)
        ]

    first_copies, second_copies, passed_copies = (
        block_copies(0, 1, 1),
        block_copies(0, 2, 2),
        block_copies(1, 2, 1),
    )

    def send_blocks():
        @pl.when(core == 1)
        def _():
            pl.semaphore_wait(barrier, jnp.where(last_x, 3, 5))
            tell_sibling()

        @pl.when(first_core)
        def _():
            pl.semaphore_wait(pair_sem, 1)

        for copy in first_copies:
            copy.start()

        @pl.when(jnp.logical_not(last_x))
        def _():
            for copy in second_copies:
                copy.start()

    send_early = x >= n_conf // 2 - 2
    at_once = b >= n_conf - 2

    @pl.when(at_once)
    def _():
        prepare_block()
        send_blocks()

    hubs_below = LAYER * jnp.minimum(z, n_hubs)

    @pl.when(first_core)
    def _():
        pl.semaphore_wait(barrier, 1 + hubs_below + jnp.where(is_hub, LAYER - 2, 0))
        tell_sibling()

    @pl.when(core == 1)
    def _():
        pl.semaphore_wait(pair_sem, 1)

    def send_grid(to):
        pltpu.make_async_remote_copy(
            src_ref=msg,
            dst_ref=gath.at[o],
            send_sem=grid_send_sem,
            recv_sem=grid_recv_sem.at[z],
            device_id=(b, to),
            device_id_type=MESH,
        ).start()

    def send_below(t, _):
        send_grid(t)
        return 0

    def send_beside(t, _):
        send_grid(z * LAYER + lax.rem(place + t, LAYER))
        return 0

    lax.fori_loop(0, hubs_below, send_below, 0)
    lax.fori_loop(1, jnp.where(is_hub, LAYER, 1), send_beside, 0)

    pl.when(jnp.logical_not(at_once))(prepare_block)
    pl.when(send_early & jnp.logical_not(at_once))(send_blocks)

    def grid_wait(layer, number):
        slots = gath.at[pl.ds(layer * LAYER, number)]
        return pltpu.make_async_remote_copy(
            src_ref=slots,
            dst_ref=slots,
            send_sem=grid_send_sem,
            recv_sem=grid_recv_sem.at[layer],
            device_id=(conf_at(1), o),
            device_id_type=MESH,
        )

    def answer(layer):
        @pl.when(z < layer)
        def _():
            grid_wait(layer, LAYER).wait_recv()
            for t in range(LAYER):
                send_grid(layer * LAYER + t)

    loads[5].wait()
    loads[6].wait()
    dens = [dens_ref[:, j * LANES : (j + 1) * LANES].astype(F32) for j in range(TILES)]
    forward_rows(dens, stage, 0)
    excess = [(t * t - 1.0).astype(BF16).astype(F32) for t in dens]
    forward_rows(excess, stage, ROWS)
    de = forward_lanes(stage, w_ref)
    dr, di = de[:, :, :LANES], de[:, :, LANES:]
    spec_de[...] = jnp.concatenate([dr, dr + di, di - dr], axis=2)

    n_cls = con_ref.shape[0]
    for row in range(0, n_cls, ROWS):
        squares = []
        for j in range(TILES):
            tile = con_ref[row : row + ROWS, j * LANES : (j + 1) * LANES]
            squares.append((tile * tile).astype(BF16).astype(F32))
        forward_rows(squares, stage, row, -LOG2E * 2.0**-17, True)
    of_classes = forward_lanes(stage, w_ref)
    for k in range(HALF):
        high, low = split_in_two(of_classes[k])
        cols = slice(k * 2 * LANES, (k + 1) * 2 * LANES)
        class_spec[0:n_cls, cols] = high
        class_spec[n_cls:, cols] = low

    def visit(v):
        classes = blocks[v, :, half * LANES :].astype(F32)[0:ROWS, 0 : 2 * n_cls]
        column = lax.broadcasted_iota(jnp.int32, (ROWS, 2 * n_cls), 1) % n_cls
        picks = jnp.where(classes == column.astype(F32), 1.0, 0.0).astype(BF16)
        spec_q[...] = jnp.dot(picks, class_spec[...], preferred_element_type=F32)
        pairs = [blocks[v, :, j * LANES : (j + 1) * LANES].astype(F32) for j in range(half)]
        rows = [p[0:ROWS] for p in pairs] + [p[ROWS:] for p in pairs]
        forward_rows(rows, stage_f, 0, LOG2E * 2.0**-16, True)
        spec_f[...] = forward_lanes(stage_f, w_ref)
        part = ROWS // 2
        pair_products(spec_f, spec_q, spec_de, 0, part, lhs_a)
        inverse_lanes(lhs_a, w_ref, g_a)
        pair_products(spec_f, spec_q, spec_de, part, part, lhs_b)
        inverse_lanes(lhs_b, w_ref, g_b)
        scores(g_a, score_ref, v * ROWS, part)
        scores(g_b, score_ref, v * ROWS + part, part)

    def lw_copy(layer):
        return pltpu.make_async_remote_copy(
            src_ref=lw_ref,
            dst_ref=lw_ref,
            send_sem=lw_send_sem.at[layer],
            recv_sem=lw_recv_sem,
            device_id=(b, layer * LAYER + place),
            device_id_type=MESH,
        )

    def hub_of(layer):
        return n_hubs - 1 if layer <= n_layers // 2 else 0

    def hear(layers):
        for layer in layers:

            @pl.when(z == layer)
            def _():
                grid_wait(layer, LAYER - 1).wait_recv()

            @pl.when((z > layer) | ((z != layer) & (layer >= n_hubs)))
            def _():
                grid_wait(layer, LAYER).wait_recv()

    early = n_layers // 2

    def make_weights():
        last = (early + n_layers) // 2
        total = early_ref[...]
        for first, end in ((last, n_layers), (early, last)):
            hear(range(first, end))
            total = total + grid_weights(gath, first * LAYER, (end - first) * LAYER)
        lw_ref[...] = log2_or_far(total)
        for layer in range(n_hubs, n_layers):

            @pl.when(z == hub_of(layer))
            def _():
                lw_copy(layer).start()

    visit(0)
    pl.when(jnp.logical_not(send_early))(send_blocks)

    for layer in range(1, n_hubs):
        answer(layer)

    @pl.when(is_hub)
    def _():
        hear(range(early))
        early_ref[...] = grid_weights(gath, 0, early * LAYER)

    starts_first = (b == 0) & (place < 2)
    weights_at = jnp.where((x == 1) | (z > 0), 2, 3) - jnp.where(starts_first, 1, 0)
    sums_early = is_hub & (x == 1)

    def hear_block(v):
        for i, piece in enumerate(pieces):
            pltpu.make_async_remote_copy(
                src_ref=blocks.at[0, :, piece],
                dst_ref=blocks.at[v, :, piece],
                send_sem=block_send_sem.at[0, i],
                recv_sem=block_recv_sem.at[v, i],
                device_id=(conf_at(1), o),
                device_id_type=MESH,
            ).wait_recv()
            if v == 1:
                pl.when(x == 0)(passed_copies[i].start)

    def step(v, _):
        pl.when(v == 1)(lambda: hear_block(1))
        pl.when(is_hub & (weights_at == v))(make_weights)

        @pl.when(sums_early & (v == 2))
        def _():
            log_sums(score_ref, lw_ref, ms_ref, 0, 2)

        pl.when(v == 2)(lambda: hear_block(2))
        pl.when(v < 3)(lambda: visit(v))
        return 0

    lax.fori_loop(1, 4, step, 0)

    @pl.when(jnp.logical_not(is_hub))
    def _():
        pltpu.make_async_remote_copy(
            src_ref=lw_ref,
            dst_ref=lw_ref,
            send_sem=lw_send_sem.at[0],
            recv_sem=lw_recv_sem,
            device_id=(b, place),
            device_id_type=MESH,
        ).wait_recv()

    log_sums(score_ref, lw_ref, ms_ref, jnp.where(sums_early, 2, 0), 3)
    final = results(ms_ref)
    for v in range(3):
        out_ref[v] = final[v * ROWS : (v + 1) * ROWS, :]

    for layer in range(n_hubs, n_layers):

        @pl.when(z == hub_of(layer))
        def _():
            lw_copy(layer).wait_send()

    @pl.when(is_hub)
    def _():
        grid_wait(0, LAYER * n_hubs - 1).wait_send()

    @pl.when(jnp.logical_not(is_hub))
    def _():
        grid_wait(0, LAYER * n_hubs).wait_send()

    for copies, sent in (
        (first_copies, x >= 0),
        (second_copies, jnp.logical_not(last_x)),
        (passed_copies, x == 0),
    ):
        for copy in copies:
            pl.when(sent)(copy.wait_send)


def solution(mesh):
    n_conf, n_orient = mesh.shape["conf"], mesh.shape["orient"]
    w = lane_matrix()

    def per_device(*given):
        particles, defocus_class, densities, contrast, grid_shift, log_prior = given
        operands = [
            pltpu.with_memory_space_constraint(x, pltpu.HBM)
            for x in (
                defocus_class,
                particles,
                densities,
                contrast,
                grid_shift,
                log_prior,
                jnp.asarray(w),
            )
        ]
        return pl.pallas_call(
            functools.partial(kernel, n_conf, n_orient),
            out_shape=pltpu.VMEM((3, ROWS, ROWS), F32),
            in_specs=[pl.BlockSpec(memory_space=pltpu.HBM)] * 7,
            out_specs=pl.BlockSpec(memory_space=pltpu.VMEM),
            scratch_shapes=[
                pltpu.SMEM(defocus_class.shape, jnp.int32),
                pltpu.VMEM(particles.shape, BF16),
                pltpu.VMEM(densities.shape, BF16),
                pltpu.VMEM(contrast.shape, F32),
                pltpu.VMEM(grid_shift.shape, jnp.int32),
                pltpu.VMEM(log_prior.shape, F32),
                pltpu.VMEM(w.shape, BF16),
                pltpu.VMEM((3, 2 * ROWS, (TILES // 2 + 1) * LANES), BF16),
                pltpu.VMEM((2, LANES), F32),
                pltpu.VMEM((n_orient, 2, LANES), F32),
                pltpu.VMEM((HALF, 2 * ROWS, 2 * LANES), F32),
                pltpu.VMEM((HALF, ROWS, 2 * LANES), F32),
                pltpu.VMEM((HALF, ROWS, 2 * LANES), F32),
                pltpu.VMEM((ROWS, HALF * 2 * LANES), F32),
                pltpu.VMEM((HALF, 2 * ROWS, 3 * LANES), F32),
                pltpu.VMEM((HALF, ROWS * ROWS // 2, 4 * LANES), BF16),
                pltpu.VMEM((HALF, ROWS * ROWS // 2, 4 * LANES), BF16),
                pltpu.VMEM((HALF, ROWS * ROWS // 2, 2 * LANES), F32),
                pltpu.VMEM((HALF, ROWS * ROWS // 2, 2 * LANES), F32),
                pltpu.VMEM((3 * ROWS, TILES, ROWS, LANES), F32),
                pltpu.VMEM((2 * contrast.shape[0], HALF * 2 * LANES), BF16),
                pltpu.VMEM((TILES, LANES), F32),
                pltpu.VMEM((TILES, LANES), F32),
                pltpu.VMEM((3 * ROWS, 2 * ROWS, LANES), F32),
                pltpu.SemaphoreType.DMA((7,)),
                pltpu.SemaphoreType.DMA((4, 2)),
                pltpu.SemaphoreType.DMA((3, 2)),
                pltpu.SemaphoreType.DMA,
                pltpu.SemaphoreType.DMA((n_orient // LAYER,)),
                pltpu.SemaphoreType.DMA((n_orient // LAYER,)),
                pltpu.SemaphoreType.DMA,
                pltpu.SemaphoreType.REGULAR,
            ],
            compiler_params=pltpu.CompilerParams(
                collective_id=0, has_side_effects=True, vmem_limit_bytes=56 * 2**20
            ),
        )(*operands)

    placed = (
        P(("conf", "orient"), None),
        P(("conf", "orient")),
        P("conf", None),
        P(),
        P("orient"),
        P("orient"),
    )
    return jax.shard_map(
        per_device,
        mesh=mesh,
        in_specs=placed,
        out_specs=P(None, None, ("conf", "orient")),
        check_vma=False,
    )
```

```python
import functools
import math

import jax
import jax.numpy as jnp
import numpy as np
from jax import lax
from jax.experimental import pallas as pl
from jax.experimental.pallas import tpu as pltpu
from jax.sharding import PartitionSpec as P

SIDE = 64
ROWS = 8
LANES = 128
TILES = 32
HALF = TILES // 2 + 1
MESH = pl.DeviceIdType.MESH
F32 = jnp.float32
BF16 = jnp.bfloat16
FAR = -1e30
LOG2E = 1.0 / math.log(2.0)
LAYER = 4


def lane_matrix():
    yl, x = np.divmod(np.arange(LANES), SIDE)
    phase = 2.0 * np.pi * (np.outer(x, x) % SIDE) / SIDE + np.pi * (np.outer(yl, yl) % 2)
    c, s = np.cos(phase), np.sin(phase)
    full = np.block([[c, s], [-s, c]]).astype(np.float32)
    high = full.astype(jnp.bfloat16)
    low = (full - high.astype(np.float32)).astype(jnp.bfloat16)
    return np.concatenate([high, low], axis=0)


def turned(z, num, den):
    re, im = z
    eighth = (8 * num / den) % 8
    if eighth == 0:
        return z
    if eighth == 2:
        return (-im, re)
    angle = 2.0 * math.pi * num / den
    c, s = math.cos(angle), math.sin(angle)
    if eighth == 1:
        return ((re - im) * c, (re + im) * c)
    if eighth == 3:
        return ((re + im) * c, (im - re) * c)
    return (re * c - im * s, re * s + im * c)


def complex_dft(z):
    n = len(z)
    if n == 1:
        return z
    even, odd = complex_dft(z[0::2]), complex_dft(z[1::2])
    out = [None] * n
    for k in range(n // 2):
        (er, ei), (re, im) = even[k], odd[k]
        if 4 * k == n:
            out[k], out[k + n // 2] = (er - im, ei + re), (er + im, ei - re)
        else:
            tr, ti = turned((re, im), k, n)
            out[k], out[k + n // 2] = (er + tr, ei + ti), (er - tr, ei - ti)
    return out


def real_dft(x):
    n = len(x)
    if n == 2:
        return [(x[0] + x[1], None, False), (x[0] - x[1], None, False)]
    h, q = n // 2, n // 4
    a = [x[j] + x[j + h] for j in range(h)]
    b = [x[j] - x[j + h] for j in range(h)]
    out = [None] * (h + 1)
    out[0::2] = real_dft(a)
    z = complex_dft([turned((b[j], b[j + q]), j, n) for j in range(q)])
    for m in range(q):
        k = 4 * m + 1
        if k <= h:
            out[k] = (*z[m], False)
        else:
            out[n - k] = (*z[m], True)
    return out


def inverse_real_dft(spec):
    h = len(spec) - 1
    n = 2 * h
    if n == 2:
        return [spec[0][0] + spec[1][0], spec[0][0] - spec[1][0]]
    q = n // 4
    even = inverse_real_dft(spec[0::2])
    z = complex_dft([spec[k] if k <= h else spec[n - k] for k in range(1, n, 4)])
    out = [None] * n
    for j in range(q):
        tr, ti = turned(z[j], j, n)
        out[j], out[j + h] = even[j] + tr, even[j] - tr
        out[j + q], out[j + q + h] = even[j + q] - ti, even[j + q] + ti
    return out


def needs_conjugate(k):
    while k % 2 == 0:
        k //= 2
    return k % 4 == 3


def by_half(first, second):
    lane = lax.broadcasted_iota(jnp.int32, (ROWS, LANES), 1)
    return jnp.where(lane >= SIDE, F32(second), F32(first))


def forward_rows(tiles, dst, row, scale=1.0, for_products=False):
    spec = real_dft(tiles)
    rows = pl.ds(row, ROWS)
    zero = jnp.zeros((ROWS, LANES), F32)
    lane = lax.broadcasted_iota(jnp.int32, (ROWS, LANES), 1)
    for k, (re, im, conj) in enumerate(spec):
        if im is None:
            re = re if scale == 1.0 else re * scale
        if k == 0:
            nr, ni = re, zero
        elif k == HALF - 1:
            nr, ni = jnp.where(lane < SIDE, re, 0.0), jnp.where(lane < SIDE, 0.0, re)
        else:
            angle = 2.0 * math.pi * k / SIDE
            if for_products:
                h = math.cos(angle / 2.0) * 2.0 * scale
                c, v = F32(h * math.cos(angle / 2.0)), h * math.sin(angle / 2.0)
                s = by_half(-v, v)
            else:
                c, s = by_half(1.0, math.cos(angle)), by_half(0.0, math.sin(angle))
            if conj:
                nr, ni = re * c + im * s, re * s - im * c
            else:
                nr, ni = re * c - im * s, re * s + im * c
        dst[k, rows, 0:LANES] = nr
        dst[k, rows, LANES : 2 * LANES] = ni


def inverse_turn(k, re, im):
    if k == 0:
        return re, None
    if k == HALF - 1:
        lane = lax.broadcasted_iota(jnp.int32, (ROWS, LANES), 1)
        return jnp.where(lane < SIDE, re, -im), None
    t = math.tan(math.pi * k / SIDE)
    if needs_conjugate(k):
        return re - im * by_half(-t, t), re * by_half(t, -t) - im
    return re - im * by_half(-t, t), im + re * by_half(-t, t)


def split_in_two(x):
    high = x.astype(BF16)
    return high, (x - high.astype(F32)).astype(BF16)


def times_lane_matrix(high, low, w_ref):
    w_high, w_low = w_ref[0 : 2 * LANES, :], w_ref[2 * LANES :, :]
    return jnp.dot(
        jnp.concatenate([high, low, high], axis=1),
        jnp.concatenate([w_high, w_high, w_low], axis=0),
        preferred_element_type=F32,
    )


def forward_lanes(src, w_ref):
    tiles, rows, lanes = src.shape
    high, low = split_in_two(src[...].reshape(tiles * rows, lanes))
    return times_lane_matrix(high, low, w_ref).reshape(tiles, rows, lanes)


def grid_weights(gath, first, count):
    shift = gath[first : first + count, 0, :].astype(jnp.int32)
    weight = gath[first : first + count, 1, :]
    high = weight.astype(BF16).astype(F32)
    low = weight - high
    dy, dx = shift // SIDE, shift % SIDE
    place = dy % 2 * TILES + dy // 2
    row = lax.broadcasted_iota(jnp.int32, (SIDE, LANES), 0)
    lefts, rights = [], []
    for r in range(count):
        mine = row == place[r : r + 1, :]
        parts = [jnp.where(mine, x[r : r + 1, :], 0.0) for x in (high, low)]
        lefts.append(jnp.concatenate(parts, axis=0).astype(BF16))
        right = jnp.where(row == dx[r : r + 1, :], 1.0, 0.0).astype(BF16)
        rights.append(jnp.concatenate([right, right], axis=0))
    both = lax.dot_general(
        jnp.concatenate(lefts, axis=1),
        jnp.concatenate(rights, axis=1),
        (((1,), (1,)), ((), ())),
        preferred_element_type=F32,
    )
    total = both[0:SIDE] + both[SIDE:]
    lane = lax.broadcasted_iota(jnp.int32, (TILES, LANES), 1)
    return jnp.where(lane < SIDE, total[0:TILES], total[TILES:])


def log2_or_far(total):
    some = total > 0.0
    return jnp.where(some, jnp.log(jnp.where(some, total, 1.0)) / math.log(2.0), FAR)


def pair_products(f_ref, q_ref, de, first, count, lhs):
    for k in range(HALF):
        f, q = f_ref[k], q_ref[:, k * 2 * LANES : (k + 1) * 2 * LANES]
        fr, fi, qr, qi = f[:, :LANES], f[:, LANES:], q[:, :LANES], q[:, LANES:]
        fd, qd = fr - fi, qr - qi
        parts = []
        for c in range(first, first + count):
            d, e = de[k, c : c + 1, :], de[k, ROWS + c : ROWS + c + 1, :]
            dr, ds, dm = (d[:, i * LANES : (i + 1) * LANES] for i in range(3))
            er, es, em = (e[:, i * LANES : (i + 1) * LANES] for i in range(3))
            shared = dr * fd + er * qd
            re = shared + (fi * ds + qi * es)
            im = shared + (fr * dm + qr * em)
            parts.append(jnp.concatenate([re, im], axis=1))
        for i in range(0, count, 2):
            high, low = split_in_two(jnp.concatenate(parts[i : i + 2], axis=0))
            rows = pl.ds(i * ROWS, 2 * ROWS)
            lhs[k, rows, 0 : 2 * LANES] = high
            lhs[k, rows, 2 * LANES :] = low


def inverse_lanes(lhs, w_ref, dst):
    rows = lhs.shape[1]
    x = lhs[...].reshape(HALF * rows, 4 * LANES)
    out = times_lane_matrix(x[:, : 2 * LANES], x[:, 2 * LANES :], w_ref)
    dst[...] = out.reshape(HALF, rows, 2 * LANES)


def scores(g_ref, score_ref, first, count):
    for i in range(count):
        rows = pl.ds(i * ROWS, ROWS)
        spec = [
            inverse_turn(k, g_ref[k, rows, 0:LANES], g_ref[k, rows, LANES : 2 * LANES])
            for k in range(HALF)
        ]
        for j, value in enumerate(inverse_real_dft(spec)):
            score_ref[first + i, j] = value


def tree(join, values):
    while len(values) > 1:
        values = [join(*values[i : i + 2]) for i in range(0, len(values) - 1, 2)] + (
            [values[-1]] if len(values) % 2 else []
        )
    return values[0]


def log_sums(score_ref, lw_ref, ms_ref, first, end):
    def one_visit(v, _):
        for p in range(ROWS):
            i = v * ROWS + p
            value = [score_ref[i, j] + lw_ref[j : j + 1, :] for j in range(TILES)]
            top = tree(jnp.maximum, value)
            total = tree(jnp.add, [jnp.exp2(v - top) for v in value])
            ms_ref[i, 0:ROWS, :] = top
            ms_ref[i, ROWS : 2 * ROWS, :] = total
        return 0

    lax.fori_loop(first, end, one_visit, 0)


def results(ms_ref):
    lane = lax.broadcasted_iota(jnp.int32, (ROWS, LANES), 1)
    tops = jnp.zeros((ROWS, LANES), F32)
    sums = jnp.ones((ROWS, LANES), F32)
    for i in range(ms_ref.shape[0]):
        top, total = ms_ref[i, 0:ROWS, :], ms_ref[i, ROWS : 2 * ROWS, :]
        highest = jnp.max(top, axis=1, keepdims=True)
        summed = jnp.sum(total * jnp.exp2(top - highest), axis=1, keepdims=True)
        tops = jnp.where(lane == i, highest, tops)
        sums = jnp.where(lane == i, summed, sums)
    return (tops * math.log(2.0) + jnp.log(sums)).T


def kernel(
    n_conf,
    n_orient,
    cls_hbm,
    part_hbm,
    dens_hbm,
    con_hbm,
    shift_hbm,
    prior_hbm,
    w_hbm,
    out_ref,
    cls_ref,
    part_ref,
    dens_ref,
    con_ref,
    shift_ref,
    prior_ref,
    w_ref,
    blocks,
    msg,
    gath,
    stage,
    stage_f,
    spec_f,
    spec_q,
    spec_de,
    lhs_a,
    g_a,
    score_ref,
    class_spec,
    early_ref,
    lw_ref,
    ms_ref,
    in_sem,
    block_send_sem,
    block_recv_sem,
    grid_send_sem,
    grid_recv_sem,
    lw_send_sem,
    lw_recv_sem,
    pair_sem,
):
    b = lax.axis_index("conf")
    o = lax.axis_index("orient")
    n_layers = n_orient // LAYER
    n_hubs = max(n_layers // 4, 1)
    z = o // LAYER
    place = lax.rem(o, LAYER)
    core = lax.rem(o, 2)
    first_core = core == 0
    is_hub = z < n_hubs

    def conf_at(offset):
        return lax.rem(b + offset + n_conf, n_conf)

    barrier = pltpu.get_barrier_semaphore()

    def greet(conf, orient):
        pl.semaphore_signal(
            barrier, inc=1, device_id=(conf, orient), device_id_type=MESH
        )

    def tell_sibling():
        pl.semaphore_signal(
            pair_sem, inc=1, device_id=(b, o + 1 - 2 * core), device_id_type=MESH
        )

    x = lax.rem(b, n_conf // 2)
    last_x = x == n_conf // 2 - 1

    @pl.when(x != 1)
    def _():
        greet(conf_at(-2), o - core + 1)

    greet(conf_at(-1), o - core + 1)

    loads = []
    for i, (src, dst) in enumerate(
        (
            (shift_hbm, shift_ref),
            (prior_hbm, prior_ref),
            (cls_hbm, cls_ref),
            (part_hbm, part_ref),
            (con_hbm, con_ref),
            (dens_hbm, dens_ref),
            (w_hbm, w_ref),
        )
    ):
        loads.append(pltpu.make_async_copy(src, dst, in_sem.at[i]))
        loads[-1].start()

    greet(b, o + 1 - 2 * core)

    @pl.when(is_hub)
    def _():
        for t in range(2, LAYER, 2):
            greet(b, z * LAYER + lax.rem(place - core + t, LAYER))

        def above(t, _):
            greet(b, 2 * t)
            return 0

        lax.fori_loop((z + 1) * (LAYER // 2), n_orient // 2, above, 0)

    count = shift_ref.shape[0]
    loads[0].wait()
    loads[1].wait()
    msg[...] = jnp.zeros_like(msg)
    msg[0:1, 0:count] = shift_ref[...].astype(F32).reshape(1, count)
    msg[1:2, 0:count] = jnp.exp(prior_ref[...]).reshape(1, count)
    gath[o] = msg[...]

    half = TILES // 2

    def prepare_block():
        for load in loads[2:5]:
            load.wait()
        row = lax.broadcasted_iota(jnp.int32, (ROWS, LANES), 0)
        cls = jnp.zeros((ROWS, LANES), jnp.int32)
        for i in range(ROWS):
            cls = jnp.where(row == i, cls_ref[i], cls)

        picked = [cls == k for k in range(con_ref.shape[0])]

        def envelope(j):
            out = jnp.zeros((ROWS, LANES), F32)
            for k, mask in enumerate(picked):
                out = jnp.where(mask, con_ref[k : k + 1, j * LANES : (j + 1) * LANES], out)
            return out

        for j in range(half):
            pair = [
                part_ref[:, t * LANES : (t + 1) * LANES].astype(F32) * envelope(t)
                for t in (j, j + half)
            ]
            blocks[0, :, j * LANES : (j + 1) * LANES] = jnp.concatenate(pair, axis=0).astype(BF16)
        blocks[0, :, half * LANES :] = jnp.concatenate([cls, cls], axis=0).astype(F32).astype(BF16)

    middle = half // 2 * LANES
    pieces = (pl.ds(0, middle), pl.ds(middle, blocks.shape[2] - middle))

    def block_copies(src, dst, to):
        return [
            pltpu.make_async_remote_copy(
                src_ref=blocks.at[src, :, piece],
                dst_ref=blocks.at[dst, :, piece],
                send_sem=block_send_sem.at[2 * src + to - 1, i],
                recv_sem=block_recv_sem.at[dst, i],
                device_id=(conf_at(to), o),
                device_id_type=MESH,
            )
            for i, piece in enumerate(pieces)
        ]

    first_copies, second_copies, passed_copies = (
        block_copies(0, 1, 1),
        block_copies(0, 2, 2),
        block_copies(1, 2, 1),
    )

    def send_blocks():
        @pl.when(core == 1)
        def _():
            pl.semaphore_wait(barrier, jnp.where(last_x, 3, 5))
            tell_sibling()

        @pl.when(first_core)
        def _():
            pl.semaphore_wait(pair_sem, 1)

        for copy in first_copies:
            copy.start()

        @pl.when(jnp.logical_not(last_x))
        def _():
            for copy in second_copies:
                copy.start()

    send_early = x >= n_conf // 2 - 2
    at_once = b >= n_conf - 2

    @pl.when(at_once)
    def _():
        prepare_block()
        send_blocks()

    hubs_below = LAYER * jnp.minimum(z, n_hubs)

    @pl.when(first_core)
    def _():
        pl.semaphore_wait(barrier, 1 + hubs_below + jnp.where(is_hub, LAYER - 2, 0))
        tell_sibling()

    @pl.when(core == 1)
    def _():
        pl.semaphore_wait(pair_sem, 1)

    def send_grid(to):
        pltpu.make_async_remote_copy(
            src_ref=msg,
            dst_ref=gath.at[o],
            send_sem=grid_send_sem,
            recv_sem=grid_recv_sem.at[z],
            device_id=(b, to),
            device_id_type=MESH,
        ).start()

    def send_below(t, _):
        send_grid(t)
        return 0

    def send_beside(t, _):
        send_grid(z * LAYER + lax.rem(place + t, LAYER))
        return 0

    lax.fori_loop(0, hubs_below, send_below, 0)
    lax.fori_loop(1, jnp.where(is_hub, LAYER, 1), send_beside, 0)

    pl.when(jnp.logical_not(at_once))(prepare_block)
    pl.when(send_early & jnp.logical_not(at_once))(send_blocks)

    def grid_wait(layer, number):
        slots = gath.at[pl.ds(layer * LAYER, number)]
        return pltpu.make_async_remote_copy(
            src_ref=slots,
            dst_ref=slots,
            send_sem=grid_send_sem,
            recv_sem=grid_recv_sem.at[layer],
            device_id=(conf_at(1), o),
            device_id_type=MESH,
        )

    def answer(layer):
        @pl.when(z < layer)
        def _():
            grid_wait(layer, LAYER).wait_recv()
            for t in range(LAYER):
                send_grid(layer * LAYER + t)

    loads[5].wait()
    loads[6].wait()
    dens = [dens_ref[:, j * LANES : (j + 1) * LANES].astype(F32) for j in range(TILES)]
    forward_rows(dens, stage, 0)
    excess = [(t * t - 1.0).astype(BF16).astype(F32) for t in dens]
    forward_rows(excess, stage, ROWS)
    de = forward_lanes(stage, w_ref)
    dr, di = de[:, :, :LANES], de[:, :, LANES:]
    spec_de[...] = jnp.concatenate([dr, dr + di, di - dr], axis=2)

    n_cls = con_ref.shape[0]
    for row in range(0, n_cls, ROWS):
        squares = []
        for j in range(TILES):
            tile = con_ref[row : row + ROWS, j * LANES : (j + 1) * LANES]
            squares.append((tile * tile).astype(BF16).astype(F32))
        forward_rows(squares, stage, row, -LOG2E * 2.0**-17, True)
    of_classes = forward_lanes(stage, w_ref)
    for k in range(HALF):
        high, low = split_in_two(of_classes[k])
        cols = slice(k * 2 * LANES, (k + 1) * 2 * LANES)
        class_spec[0:n_cls, cols] = high
        class_spec[n_cls:, cols] = low

    def visit(v):
        classes = blocks[v, :, half * LANES :].astype(F32)[0:ROWS, 0 : 2 * n_cls]
        column = lax.broadcasted_iota(jnp.int32, (ROWS, 2 * n_cls), 1) % n_cls
        picks = jnp.where(classes == column.astype(F32), 1.0, 0.0).astype(BF16)
        spec_q[...] = jnp.dot(picks, class_spec[...], preferred_element_type=F32)
        pairs = [blocks[v, :, j * LANES : (j + 1) * LANES].astype(F32) for j in range(half)]
        rows = [p[0:ROWS] for p in pairs] + [p[ROWS:] for p in pairs]
        forward_rows(rows, stage_f, 0, LOG2E * 2.0**-16, True)
        spec_f[...] = forward_lanes(stage_f, w_ref)
        pair_products(spec_f, spec_q, spec_de, 0, ROWS, lhs_a)
        inverse_lanes(lhs_a, w_ref, g_a)
        scores(g_a, score_ref, v * ROWS, ROWS)

    def lw_copy(layer):
        return pltpu.make_async_remote_copy(
            src_ref=lw_ref,
            dst_ref=lw_ref,
            send_sem=lw_send_sem.at[layer],
            recv_sem=lw_recv_sem,
            device_id=(b, layer * LAYER + place),
            device_id_type=MESH,
        )

    def hub_of(layer):
        return n_hubs - 1 if layer <= n_layers // 2 else 0

    def hear(layers):
        for layer in layers:

            @pl.when(z == layer)
            def _():
                grid_wait(layer, LAYER - 1).wait_recv()

            @pl.when((z > layer) | ((z != layer) & (layer >= n_hubs)))
            def _():
                grid_wait(layer, LAYER).wait_recv()

    early = n_layers // 2

    def make_weights():
        last = (early + n_layers) // 2
        total = early_ref[...]
        for first, end in ((last, n_layers), (early, last)):
            hear(range(first, end))
            total = total + grid_weights(gath, first * LAYER, (end - first) * LAYER)
        lw_ref[...] = log2_or_far(total)
        for layer in range(n_hubs, n_layers):

            @pl.when(z == hub_of(layer))
            def _():
                lw_copy(layer).start()

    visit(0)
    pl.when(jnp.logical_not(send_early))(send_blocks)

    for layer in range(1, n_hubs):
        answer(layer)

    @pl.when(is_hub)
    def _():
        hear(range(early))
        early_ref[...] = grid_weights(gath, 0, early * LAYER)

    starts_first = (b == 0) & (place < 2)
    weights_at = jnp.where((x == 1) | (z > 0), 2, 3) - jnp.where(starts_first, 1, 0)
    sums_early = is_hub & (x == 1)

    def hear_block(v):
        for i, piece in enumerate(pieces):
            pltpu.make_async_remote_copy(
                src_ref=blocks.at[0, :, piece],
                dst_ref=blocks.at[v, :, piece],
                send_sem=block_send_sem.at[0, i],
                recv_sem=block_recv_sem.at[v, i],
                device_id=(conf_at(1), o),
                device_id_type=MESH,
            ).wait_recv()
            if v == 1:
                pl.when(x == 0)(passed_copies[i].start)

    def step(v, _):
        pl.when(v == 1)(lambda: hear_block(1))
        pl.when(is_hub & (weights_at == v))(make_weights)

        @pl.when(sums_early & (v == 2))
        def _():
            log_sums(score_ref, lw_ref, ms_ref, 0, 2)

        pl.when(v == 2)(lambda: hear_block(2))
        pl.when(v < 3)(lambda: visit(v))
        return 0

    lax.fori_loop(1, 4, step, 0)

    @pl.when(jnp.logical_not(is_hub))
    def _():
        pltpu.make_async_remote_copy(
            src_ref=lw_ref,
            dst_ref=lw_ref,
            send_sem=lw_send_sem.at[0],
            recv_sem=lw_recv_sem,
            device_id=(b, place),
            device_id_type=MESH,
        ).wait_recv()

    log_sums(score_ref, lw_ref, ms_ref, jnp.where(sums_early, 2, 0), 3)
    final = results(ms_ref)
    for v in range(3):
        out_ref[v] = final[v * ROWS : (v + 1) * ROWS, :]

    for layer in range(n_hubs, n_layers):

        @pl.when(z == hub_of(layer))
        def _():
            lw_copy(layer).wait_send()

    @pl.when(is_hub)
    def _():
        grid_wait(0, LAYER * n_hubs - 1).wait_send()

    @pl.when(jnp.logical_not(is_hub))
    def _():
        grid_wait(0, LAYER * n_hubs).wait_send()

    for copies, sent in (
        (first_copies, x >= 0),
        (second_copies, jnp.logical_not(last_x)),
        (passed_copies, x == 0),
    ):
        for copy in copies:
            pl.when(sent)(copy.wait_send)


def solution(mesh):
    n_conf, n_orient = mesh.shape["conf"], mesh.shape["orient"]
    w = lane_matrix()

    def per_device(*given):
        particles, defocus_class, densities, contrast, grid_shift, log_prior = given
        operands = [
            pltpu.with_memory_space_constraint(x, pltpu.HBM)
            for x in (
                defocus_class,
                particles,
                densities,
                contrast,
                grid_shift,
                log_prior,
                jnp.asarray(w),
            )
        ]
        return pl.pallas_call(
            functools.partial(kernel, n_conf, n_orient),
            out_shape=pltpu.VMEM((3, ROWS, ROWS), F32),
            in_specs=[pl.BlockSpec(memory_space=pltpu.HBM)] * 7,
            out_specs=pl.BlockSpec(memory_space=pltpu.VMEM),
            scratch_shapes=[
                pltpu.SMEM(defocus_class.shape, jnp.int32),
                pltpu.VMEM(particles.shape, BF16),
                pltpu.VMEM(densities.shape, BF16),
                pltpu.VMEM(contrast.shape, F32),
                pltpu.VMEM(grid_shift.shape, jnp.int32),
                pltpu.VMEM(log_prior.shape, F32),
                pltpu.VMEM(w.shape, BF16),
                pltpu.VMEM((3, 2 * ROWS, (TILES // 2 + 1) * LANES), BF16),
                pltpu.VMEM((2, LANES), F32),
                pltpu.VMEM((n_orient, 2, LANES), F32),
                pltpu.VMEM((HALF, 2 * ROWS, 2 * LANES), F32),
                pltpu.VMEM((HALF, ROWS, 2 * LANES), F32),
                pltpu.VMEM((HALF, ROWS, 2 * LANES), F32),
                pltpu.VMEM((ROWS, HALF * 2 * LANES), F32),
                pltpu.VMEM((HALF, 2 * ROWS, 3 * LANES), F32),
                pltpu.VMEM((HALF, ROWS * ROWS, 4 * LANES), BF16),
                pltpu.VMEM((HALF, ROWS * ROWS, 2 * LANES), F32),
                pltpu.VMEM((3 * ROWS, TILES, ROWS, LANES), F32),
                pltpu.VMEM((2 * contrast.shape[0], HALF * 2 * LANES), BF16),
                pltpu.VMEM((TILES, LANES), F32),
                pltpu.VMEM((TILES, LANES), F32),
                pltpu.VMEM((3 * ROWS, 2 * ROWS, LANES), F32),
                pltpu.SemaphoreType.DMA((7,)),
                pltpu.SemaphoreType.DMA((4, 2)),
                pltpu.SemaphoreType.DMA((3, 2)),
                pltpu.SemaphoreType.DMA,
                pltpu.SemaphoreType.DMA((n_orient // LAYER,)),
                pltpu.SemaphoreType.DMA((n_orient // LAYER,)),
                pltpu.SemaphoreType.DMA,
                pltpu.SemaphoreType.REGULAR,
            ],
            compiler_params=pltpu.CompilerParams(
                collective_id=0, has_side_effects=True, vmem_limit_bytes=56 * 2**20
            ),
        )(*operands)

    placed = (
        P(("conf", "orient"), None),
        P(("conf", "orient")),
        P("conf", None),
        P(),
        P("orient"),
        P("orient"),
    )
    return jax.shard_map(
        per_device,
        mesh=mesh,
        in_specs=placed,
        out_specs=P(None, None, ("conf", "orient")),
        check_vma=False,
    )
```

```python
import functools
import math

import jax
import jax.numpy as jnp
import numpy as np
from jax import lax
from jax.experimental import pallas as pl
from jax.experimental.pallas import tpu as pltpu
from jax.sharding import PartitionSpec as P

SIDE = 64
ROWS = 8
LANES = 128
TILES = 32
HALF = TILES // 2 + 1
MESH = pl.DeviceIdType.MESH
F32 = jnp.float32
BF16 = jnp.bfloat16
FAR = -1e30
LOG2E = 1.0 / math.log(2.0)
LAYER = 4


def lane_matrix():
    yl, x = np.divmod(np.arange(LANES), SIDE)
    phase = 2.0 * np.pi * (np.outer(x, x) % SIDE) / SIDE + np.pi * (np.outer(yl, yl) % 2)
    c, s = np.cos(phase), np.sin(phase)
    full = np.block([[c, s], [-s, c]]).astype(np.float32)
    high = full.astype(jnp.bfloat16)
    low = (full - high.astype(np.float32)).astype(jnp.bfloat16)
    return np.concatenate([high, low], axis=0)


def turned(z, num, den):
    re, im = z
    eighth = (8 * num / den) % 8
    if eighth == 0:
        return z
    if eighth == 2:
        return (-im, re)
    angle = 2.0 * math.pi * num / den
    c, s = math.cos(angle), math.sin(angle)
    if eighth == 1:
        return ((re - im) * c, (re + im) * c)
    if eighth == 3:
        return ((re + im) * c, (im - re) * c)
    return (re * c - im * s, re * s + im * c)


def complex_dft(z):
    n = len(z)
    if n == 1:
        return z
    even, odd = complex_dft(z[0::2]), complex_dft(z[1::2])
    out = [None] * n
    for k in range(n // 2):
        (er, ei), (re, im) = even[k], odd[k]
        if 4 * k == n:
            out[k], out[k + n // 2] = (er - im, ei + re), (er + im, ei - re)
        else:
            tr, ti = turned((re, im), k, n)
            out[k], out[k + n // 2] = (er + tr, ei + ti), (er - tr, ei - ti)
    return out


def real_dft(x):
    n = len(x)
    if n == 2:
        return [(x[0] + x[1], None, False), (x[0] - x[1], None, False)]
    h, q = n // 2, n // 4
    a = [x[j] + x[j + h] for j in range(h)]
    b = [x[j] - x[j + h] for j in range(h)]
    out = [None] * (h + 1)
    out[0::2] = real_dft(a)
    z = complex_dft([turned((b[j], b[j + q]), j, n) for j in range(q)])
    for m in range(q):
        k = 4 * m + 1
        if k <= h:
            out[k] = (*z[m], False)
        else:
            out[n - k] = (*z[m], True)
    return out


def inverse_real_dft(spec):
    h = len(spec) - 1
    n = 2 * h
    if n == 2:
        return [spec[0][0] + spec[1][0], spec[0][0] - spec[1][0]]
    q = n // 4
    even = inverse_real_dft(spec[0::2])
    z = complex_dft([spec[k] if k <= h else spec[n - k] for k in range(1, n, 4)])
    out = [None] * n
    for j in range(q):
        tr, ti = turned(z[j], j, n)
        out[j], out[j + h] = even[j] + tr, even[j] - tr
        out[j + q], out[j + q + h] = even[j + q] - ti, even[j + q] + ti
    return out


def needs_conjugate(k):
    while k % 2 == 0:
        k //= 2
    return k % 4 == 3


def by_half(first, second):
    lane = lax.broadcasted_iota(jnp.int32, (ROWS, LANES), 1)
    return jnp.where(lane >= SIDE, F32(second), F32(first))


def forward_rows(tiles, dst, row, scale=1.0, for_products=False):
    spec = real_dft(tiles)
    rows = pl.ds(row, ROWS)
    zero = jnp.zeros((ROWS, LANES), F32)
    lane = lax.broadcasted_iota(jnp.int32, (ROWS, LANES), 1)
    for k, (re, im, conj) in enumerate(spec):
        if im is None:
            re = re if scale == 1.0 else re * scale
        if k == 0:
            nr, ni = re, zero
        elif k == HALF - 1:
            nr, ni = jnp.where(lane < SIDE, re, 0.0), jnp.where(lane < SIDE, 0.0, re)
        else:
            angle = 2.0 * math.pi * k / SIDE
            if for_products:
                h = math.cos(angle / 2.0) * 2.0 * scale
                c, v = F32(h * math.cos(angle / 2.0)), h * math.sin(angle / 2.0)
                s = by_half(-v, v)
            else:
                c, s = by_half(1.0, math.cos(angle)), by_half(0.0, math.sin(angle))
            if conj:
                nr, ni = re * c + im * s, re * s - im * c
            else:
                nr, ni = re * c - im * s, re * s + im * c
        dst[k, rows, 0:LANES] = nr
        dst[k, rows, LANES : 2 * LANES] = ni


def inverse_turn(k, re, im):
    if k == 0:
        return re, None
    if k == HALF - 1:
        lane = lax.broadcasted_iota(jnp.int32, (ROWS, LANES), 1)
        return jnp.where(lane < SIDE, re, -im), None
    t = math.tan(math.pi * k / SIDE)
    if needs_conjugate(k):
        return re - im * by_half(-t, t), re * by_half(t, -t) - im
    return re - im * by_half(-t, t), im + re * by_half(-t, t)


def split_in_two(x):
    high = x.astype(BF16)
    return high, (x - high.astype(F32)).astype(BF16)


def times_lane_matrix(high, low, w_ref):
    w_high, w_low = w_ref[0 : 2 * LANES, :], w_ref[2 * LANES :, :]
    return jnp.dot(
        jnp.concatenate([high, low, high], axis=1),
        jnp.concatenate([w_high, w_high, w_low], axis=0),
        preferred_element_type=F32,
    )


def forward_lanes(src, w_ref):
    tiles, rows, lanes = src.shape
    high, low = split_in_two(src[...].reshape(tiles * rows, lanes))
    return times_lane_matrix(high, low, w_ref).reshape(tiles, rows, lanes)


def grid_weights(gath, first, count):
    shift = gath[first : first + count, 0, :].astype(jnp.int32)
    weight = gath[first : first + count, 1, :]
    high = weight.astype(BF16).astype(F32)
    low = weight - high
    dy, dx = shift // SIDE, shift % SIDE
    place = dy % 2 * TILES + dy // 2
    row = lax.broadcasted_iota(jnp.int32, (SIDE, LANES), 0)
    lefts, rights = [], []
    for r in range(count):
        mine = row == place[r : r + 1, :]
        parts = [jnp.where(mine, x[r : r + 1, :], 0.0) for x in (high, low)]
        lefts.append(jnp.concatenate(parts, axis=0).astype(BF16))
        right = jnp.where(row == dx[r : r + 1, :], 1.0, 0.0).astype(BF16)
        rights.append(jnp.concatenate([right, right], axis=0))
    both = lax.dot_general(
        jnp.concatenate(lefts, axis=1),
        jnp.concatenate(rights, axis=1),
        (((1,), (1,)), ((), ())),
        preferred_element_type=F32,
    )
    total = both[0:SIDE] + both[SIDE:]
    lane = lax.broadcasted_iota(jnp.int32, (TILES, LANES), 1)
    return jnp.where(lane < SIDE, total[0:TILES], total[TILES:])


def log2_or_far(total):
    some = total > 0.0
    return jnp.where(some, jnp.log(jnp.where(some, total, 1.0)) / math.log(2.0), FAR)


def pair_products(f_ref, q_ref, de, first, count, lhs):
    for k in range(HALF):
        f, q = f_ref[k], q_ref[:, k * 2 * LANES : (k + 1) * 2 * LANES]
        fr, fi, qr, qi = f[:, :LANES], f[:, LANES:], q[:, :LANES], q[:, LANES:]
        fd, qd = fr - fi, qr - qi
        parts = []
        for c in range(first, first + count):
            d, e = de[k, c : c + 1, :], de[k, ROWS + c : ROWS + c + 1, :]
            dr, ds, dm = (d[:, i * LANES : (i + 1) * LANES] for i in range(3))
            er, es, em = (e[:, i * LANES : (i + 1) * LANES] for i in range(3))
            shared = dr * fd + er * qd
            re = shared + (fi * ds + qi * es)
            im = shared + (fr * dm + qr * em)
            parts.append(jnp.concatenate([re, im], axis=1))
        for i in range(0, count, 2):
            high, low = split_in_two(jnp.concatenate(parts[i : i + 2], axis=0))
            rows = pl.ds(i * ROWS, 2 * ROWS)
            lhs[k, rows, 0 : 2 * LANES] = high
            lhs[k, rows, 2 * LANES :] = low


def inverse_lanes(lhs, w_ref, dst):
    rows = lhs.shape[1]
    x = lhs[...].reshape(HALF * rows, 4 * LANES)
    out = times_lane_matrix(x[:, : 2 * LANES], x[:, 2 * LANES :], w_ref)
    dst[...] = out.reshape(HALF, rows, 2 * LANES)


def scores(g_ref, score_ref, first, count):
    for i in range(count):
        rows = pl.ds(i * ROWS, ROWS)
        spec = [
            inverse_turn(k, g_ref[k, rows, 0:LANES], g_ref[k, rows, LANES : 2 * LANES])
            for k in range(HALF)
        ]
        for j, value in enumerate(inverse_real_dft(spec)):
            score_ref[first + i, j] = value


def tree(join, values):
    while len(values) > 1:
        values = [join(*values[i : i + 2]) for i in range(0, len(values) - 1, 2)] + (
            [values[-1]] if len(values) % 2 else []
        )
    return values[0]


def log_sums(score_ref, lw_ref, ms_ref, first, end):
    def one_visit(v, _):
        for p in range(ROWS):
            i = v * ROWS + p
            value = [score_ref[i, j] + lw_ref[j : j + 1, :] for j in range(TILES)]
            top = tree(jnp.maximum, value)
            total = tree(jnp.add, [jnp.exp2(v - top) for v in value])
            ms_ref[i, 0:ROWS, :] = top
            ms_ref[i, ROWS : 2 * ROWS, :] = total
        return 0

    lax.fori_loop(first, end, one_visit, 0)


def results(ms_ref):
    lane = lax.broadcasted_iota(jnp.int32, (ROWS, LANES), 1)
    tops = jnp.zeros((ROWS, LANES), F32)
    sums = jnp.ones((ROWS, LANES), F32)
    for i in range(ms_ref.shape[0]):
        top, total = ms_ref[i, 0:ROWS, :], ms_ref[i, ROWS : 2 * ROWS, :]
        highest = jnp.max(top, axis=1, keepdims=True)
        summed = jnp.sum(total * jnp.exp2(top - highest), axis=1, keepdims=True)
        tops = jnp.where(lane == i, highest, tops)
        sums = jnp.where(lane == i, summed, sums)
    return (tops * math.log(2.0) + jnp.log(sums)).T


def kernel(
    n_conf,
    n_orient,
    cls_hbm,
    part_hbm,
    dens_hbm,
    con_hbm,
    shift_hbm,
    prior_hbm,
    w_hbm,
    out_ref,
    cls_ref,
    part_ref,
    dens_ref,
    con_ref,
    shift_ref,
    prior_ref,
    w_ref,
    blocks,
    msg,
    gath,
    stage,
    stage_f,
    spec_f,
    spec_q,
    spec_de,
    lhs_a,
    g_a,
    score_ref,
    class_spec,
    early_ref,
    lw_ref,
    ms_ref,
    in_sem,
    block_send_sem,
    block_recv_sem,
    grid_send_sem,
    grid_recv_sem,
    lw_send_sem,
    lw_recv_sem,
    pair_sem,
):
    b = lax.axis_index("conf")
    o = lax.axis_index("orient")
    n_layers = n_orient // LAYER
    n_hubs = max(n_layers // 4, 1)
    z = o // LAYER
    place = lax.rem(o, LAYER)
    core = lax.rem(o, 2)
    first_core = core == 0
    is_hub = z < n_hubs

    def conf_at(offset):
        return lax.rem(b + offset + n_conf, n_conf)

    barrier = pltpu.get_barrier_semaphore()

    def greet(conf, orient):
        pl.semaphore_signal(
            barrier, inc=1, device_id=(conf, orient), device_id_type=MESH
        )

    def tell_sibling():
        pl.semaphore_signal(
            pair_sem, inc=1, device_id=(b, o + 1 - 2 * core), device_id_type=MESH
        )

    x = lax.rem(b, n_conf // 2)
    last_x = x == n_conf // 2 - 1

    @pl.when(x != 1)
    def _():
        greet(conf_at(-2), o - core + 1)

    greet(conf_at(-1), o - core + 1)

    loads = []
    for i, (src, dst) in enumerate(
        (
            (shift_hbm, shift_ref),
            (prior_hbm, prior_ref),
            (cls_hbm, cls_ref),
            (part_hbm, part_ref),
            (con_hbm, con_ref),
            (dens_hbm, dens_ref),
            (w_hbm, w_ref),
        )
    ):
        loads.append(pltpu.make_async_copy(src, dst, in_sem.at[i]))
        loads[-1].start()

    greet(b, o + 1 - 2 * core)

    @pl.when(is_hub)
    def _():
        for t in range(2, LAYER, 2):
            greet(b, z * LAYER + lax.rem(place - core + t, LAYER))

        def above(t, _):
            greet(b, 2 * t)
            return 0

        lax.fori_loop((z + 1) * (LAYER // 2), n_orient // 2, above, 0)

    count = shift_ref.shape[0]
    loads[0].wait()
    loads[1].wait()
    msg[...] = jnp.zeros_like(msg)
    msg[0:1, 0:count] = shift_ref[...].astype(F32).reshape(1, count)
    msg[1:2, 0:count] = jnp.exp(prior_ref[...]).reshape(1, count)
    gath[o] = msg[...]

    half = TILES // 2

    def prepare_block():
        for load in loads[2:5]:
            load.wait()
        row = lax.broadcasted_iota(jnp.int32, (ROWS, LANES), 0)
        cls = jnp.zeros((ROWS, LANES), jnp.int32)
        for i in range(ROWS):
            cls = jnp.where(row == i, cls_ref[i], cls)

        picked = [cls == k for k in range(con_ref.shape[0])]

        def envelope(j):
            out = jnp.zeros((ROWS, LANES), F32)
            for k, mask in enumerate(picked):
                out = jnp.where(mask, con_ref[k : k + 1, j * LANES : (j + 1) * LANES], out)
            return out

        for j in range(half):
            pair = [
                part_ref[:, t * LANES : (t + 1) * LANES].astype(F32) * envelope(t)
                for t in (j, j + half)
            ]
            blocks[0, :, j * LANES : (j + 1) * LANES] = jnp.concatenate(pair, axis=0).astype(BF16)
        blocks[0, :, half * LANES :] = jnp.concatenate([cls, cls], axis=0).astype(F32).astype(BF16)

    middle = half // 2 * LANES
    pieces = (pl.ds(0, middle), pl.ds(middle, blocks.shape[2] - middle))

    def block_copies(src, dst, to):
        return [
            pltpu.make_async_remote_copy(
                src_ref=blocks.at[src, :, piece],
                dst_ref=blocks.at[dst, :, piece],
                send_sem=block_send_sem.at[2 * src + to - 1, i],
                recv_sem=block_recv_sem.at[dst, i],
                device_id=(conf_at(to), o),
                device_id_type=MESH,
            )
            for i, piece in enumerate(pieces)
        ]

    first_copies, second_copies, passed_copies = (
        block_copies(0, 1, 1),
        block_copies(0, 2, 2),
        block_copies(1, 2, 1),
    )

    def send_blocks():
        @pl.when(core == 1)
        def _():
            pl.semaphore_wait(barrier, jnp.where(last_x, 3, 5))
            tell_sibling()

        @pl.when(first_core)
        def _():
            pl.semaphore_wait(pair_sem, 1)

        for copy in first_copies:
            copy.start()

        @pl.when(jnp.logical_not(last_x))
        def _():
            for copy in second_copies:
                copy.start()

    send_early = x >= n_conf // 2 - 2
    at_once = b >= n_conf - 2

    @pl.when(at_once)
    def _():
        prepare_block()
        send_blocks()

    hubs_below = LAYER * jnp.minimum(z, n_hubs)

    @pl.when(first_core)
    def _():
        pl.semaphore_wait(barrier, 1 + hubs_below + jnp.where(is_hub, LAYER - 2, 0))
        tell_sibling()

    @pl.when(core == 1)
    def _():
        pl.semaphore_wait(pair_sem, 1)

    def send_grid(to):
        pltpu.make_async_remote_copy(
            src_ref=msg,
            dst_ref=gath.at[o],
            send_sem=grid_send_sem,
            recv_sem=grid_recv_sem.at[z],
            device_id=(b, to),
            device_id_type=MESH,
        ).start()

    def send_below(t, _):
        send_grid(t)
        return 0

    def send_beside(t, _):
        send_grid(z * LAYER + lax.rem(place + t, LAYER))
        return 0

    lax.fori_loop(0, hubs_below, send_below, 0)
    lax.fori_loop(1, jnp.where(is_hub, LAYER, 1), send_beside, 0)

    pl.when(jnp.logical_not(at_once))(prepare_block)
    pl.when(send_early & jnp.logical_not(at_once))(send_blocks)

    def grid_wait(layer, number):
        slots = gath.at[pl.ds(layer * LAYER, number)]
        return pltpu.make_async_remote_copy(
            src_ref=slots,
            dst_ref=slots,
            send_sem=grid_send_sem,
            recv_sem=grid_recv_sem.at[layer],
            device_id=(conf_at(1), o),
            device_id_type=MESH,
        )

    def answer(layer):
        @pl.when(z < layer)
        def _():
            grid_wait(layer, LAYER).wait_recv()
            for t in range(LAYER):
                send_grid(layer * LAYER + t)

    loads[5].wait()
    loads[6].wait()
    dens = [dens_ref[:, j * LANES : (j + 1) * LANES].astype(F32) for j in range(TILES)]
    forward_rows(dens, stage, 0)
    excess = [(t * t - 1.0).astype(BF16).astype(F32) for t in dens]
    forward_rows(excess, stage, ROWS)
    de = forward_lanes(stage, w_ref)
    dr, di = de[:, :, :LANES], de[:, :, LANES:]
    spec_de[...] = jnp.concatenate([dr, dr + di, di - dr], axis=2)

    n_cls = con_ref.shape[0]
    for row in range(0, n_cls, ROWS):
        squares = []
        for j in range(TILES):
            tile = con_ref[row : row + ROWS, j * LANES : (j + 1) * LANES]
            squares.append((tile * tile).astype(BF16).astype(F32))
        forward_rows(squares, stage, row, -LOG2E * 2.0**-17, True)
    of_classes = forward_lanes(stage, w_ref)
    for k in range(HALF):
        high, low = split_in_two(of_classes[k])
        cols = slice(k * 2 * LANES, (k + 1) * 2 * LANES)
        class_spec[0:n_cls, cols] = high
        class_spec[n_cls:, cols] = low

    def visit(v):
        classes = blocks[v, :, half * LANES :].astype(F32)[0:ROWS, 0 : 2 * n_cls]
        column = lax.broadcasted_iota(jnp.int32, (ROWS, 2 * n_cls), 1) % n_cls
        picks = jnp.where(classes == column.astype(F32), 1.0, 0.0).astype(BF16)
        spec_q[...] = jnp.dot(picks, class_spec[...], preferred_element_type=F32)
        pairs = [blocks[v, :, j * LANES : (j + 1) * LANES].astype(F32) for j in range(half)]
        rows = [p[0:ROWS] for p in pairs] + [p[ROWS:] for p in pairs]
        forward_rows(rows, stage_f, 0, LOG2E * 2.0**-16, True)
        spec_f[...] = forward_lanes(stage_f, w_ref)
        pair_products(spec_f, spec_q, spec_de, 0, ROWS, lhs_a)
        inverse_lanes(lhs_a, w_ref, g_a)
        scores(g_a, score_ref, v * ROWS, ROWS)

    def lw_copy(layer):
        return pltpu.make_async_remote_copy(
            src_ref=lw_ref,
            dst_ref=lw_ref,
            send_sem=lw_send_sem.at[layer],
            recv_sem=lw_recv_sem,
            device_id=(b, layer * LAYER + place),
            device_id_type=MESH,
        )

    def hub_of(layer):
        return n_hubs - 1 if layer <= n_layers // 2 else 0

    def hear(layers):
        for layer in layers:

            @pl.when(z == layer)
            def _():
                grid_wait(layer, LAYER - 1).wait_recv()

            @pl.when((z > layer) | ((z != layer) & (layer >= n_hubs)))
            def _():
                grid_wait(layer, LAYER).wait_recv()

    early = n_layers // 2

    def make_weights():
        last = early + 1
        total = early_ref[...]
        for first, end in ((last, n_layers), (early, last)):
            hear(range(first, end))
            total = total + grid_weights(gath, first * LAYER, (end - first) * LAYER)
        lw_ref[...] = log2_or_far(total)
        for layer in range(n_hubs, n_layers):

            @pl.when(z == hub_of(layer))
            def _():
                lw_copy(layer).start()

    visit(0)
    pl.when(jnp.logical_not(send_early))(send_blocks)

    for layer in range(1, n_hubs):
        answer(layer)

    @pl.when(is_hub)
    def _():
        hear(range(early))
        early_ref[...] = grid_weights(gath, 0, early * LAYER)

    starts_first = (b == 0) & (place < 2)
    weights_at = jnp.where((x == 1) | (z > 0), 2, 3) - jnp.where(starts_first, 1, 0)
    sums_early = is_hub & (x == 1)

    def hear_block(v):
        for i, piece in enumerate(pieces):
            pltpu.make_async_remote_copy(
                src_ref=blocks.at[0, :, piece],
                dst_ref=blocks.at[v, :, piece],
                send_sem=block_send_sem.at[0, i],
                recv_sem=block_recv_sem.at[v, i],
                device_id=(conf_at(1), o),
                device_id_type=MESH,
            ).wait_recv()
            if v == 1:
                pl.when(x == 0)(passed_copies[i].start)

    def step(v, _):
        pl.when(v == 1)(lambda: hear_block(1))
        pl.when(is_hub & (weights_at == v))(make_weights)

        @pl.when(sums_early & (v == 2))
        def _():
            log_sums(score_ref, lw_ref, ms_ref, 0, 2)

        pl.when(v == 2)(lambda: hear_block(2))
        pl.when(v < 3)(lambda: visit(v))
        return 0

    lax.fori_loop(1, 4, step, 0)

    @pl.when(jnp.logical_not(is_hub))
    def _():
        pltpu.make_async_remote_copy(
            src_ref=lw_ref,
            dst_ref=lw_ref,
            send_sem=lw_send_sem.at[0],
            recv_sem=lw_recv_sem,
            device_id=(b, place),
            device_id_type=MESH,
        ).wait_recv()

    log_sums(score_ref, lw_ref, ms_ref, jnp.where(sums_early, 2, 0), 3)
    final = results(ms_ref)
    for v in range(3):
        out_ref[v] = final[v * ROWS : (v + 1) * ROWS, :]

    for layer in range(n_hubs, n_layers):

        @pl.when(z == hub_of(layer))
        def _():
            lw_copy(layer).wait_send()

    @pl.when(is_hub)
    def _():
        grid_wait(0, LAYER * n_hubs - 1).wait_send()

    @pl.when(jnp.logical_not(is_hub))
    def _():
        grid_wait(0, LAYER * n_hubs).wait_send()

    for copies, sent in (
        (first_copies, x >= 0),
        (second_copies, jnp.logical_not(last_x)),
        (passed_copies, x == 0),
    ):
        for copy in copies:
            pl.when(sent)(copy.wait_send)


def solution(mesh):
    n_conf, n_orient = mesh.shape["conf"], mesh.shape["orient"]
    w = lane_matrix()

    def per_device(*given):
        particles, defocus_class, densities, contrast, grid_shift, log_prior = given
        operands = [
            pltpu.with_memory_space_constraint(x, pltpu.HBM)
            for x in (
                defocus_class,
                particles,
                densities,
                contrast,
                grid_shift,
                log_prior,
                jnp.asarray(w),
            )
        ]
        return pl.pallas_call(
            functools.partial(kernel, n_conf, n_orient),
            out_shape=pltpu.VMEM((3, ROWS, ROWS), F32),
            in_specs=[pl.BlockSpec(memory_space=pltpu.HBM)] * 7,
            out_specs=pl.BlockSpec(memory_space=pltpu.VMEM),
            scratch_shapes=[
                pltpu.SMEM(defocus_class.shape, jnp.int32),
                pltpu.VMEM(particles.shape, BF16),
                pltpu.VMEM(densities.shape, BF16),
                pltpu.VMEM(contrast.shape, F32),
                pltpu.VMEM(grid_shift.shape, jnp.int32),
                pltpu.VMEM(log_prior.shape, F32),
                pltpu.VMEM(w.shape, BF16),
                pltpu.VMEM((3, 2 * ROWS, (TILES // 2 + 1) * LANES), BF16),
                pltpu.VMEM((2, LANES), F32),
                pltpu.VMEM((n_orient, 2, LANES), F32),
                pltpu.VMEM((HALF, 2 * ROWS, 2 * LANES), F32),
                pltpu.VMEM((HALF, ROWS, 2 * LANES), F32),
                pltpu.VMEM((HALF, ROWS, 2 * LANES), F32),
                pltpu.VMEM((ROWS, HALF * 2 * LANES), F32),
                pltpu.VMEM((HALF, 2 * ROWS, 3 * LANES), F32),
                pltpu.VMEM((HALF, ROWS * ROWS, 4 * LANES), BF16),
                pltpu.VMEM((HALF, ROWS * ROWS, 2 * LANES), F32),
                pltpu.VMEM((3 * ROWS, TILES, ROWS, LANES), F32),
                pltpu.VMEM((2 * contrast.shape[0], HALF * 2 * LANES), BF16),
                pltpu.VMEM((TILES, LANES), F32),
                pltpu.VMEM((TILES, LANES), F32),
                pltpu.VMEM((3 * ROWS, 2 * ROWS, LANES), F32),
                pltpu.SemaphoreType.DMA((7,)),
                pltpu.SemaphoreType.DMA((4, 2)),
                pltpu.SemaphoreType.DMA((3, 2)),
                pltpu.SemaphoreType.DMA,
                pltpu.SemaphoreType.DMA((n_orient // LAYER,)),
                pltpu.SemaphoreType.DMA((n_orient // LAYER,)),
                pltpu.SemaphoreType.DMA,
                pltpu.SemaphoreType.REGULAR,
            ],
            compiler_params=pltpu.CompilerParams(
                collective_id=0, has_side_effects=True, vmem_limit_bytes=56 * 2**20
            ),
        )(*operands)

    placed = (
        P(("conf", "orient"), None),
        P(("conf", "orient")),
        P("conf", None),
        P(),
        P("orient"),
        P("orient"),
    )
    return jax.shard_map(
        per_device,
        mesh=mesh,
        in_specs=placed,
        out_specs=P(None, None, ("conf", "orient")),
        check_vma=False,
    )
```
